32 devices in a mesh: frame: 2 (over x), row: 8 (over z, y), head: 2 (over core).
Axes of the slice: x: 2, y: 2, z: 4, core: 2. Of those that a mesh axis runs over, the one named last changes fastest.
Arguments:
- q_pre: bfloat16 [2, 16, 64, 2560], P('frame', 'row', None, 'head'), may hold values from -60 to 60
- k_pre: bfloat16 [2, 16, 64, 2560], P('frame', 'row', None, 'head'), may hold values from -60 to 60
- values: bfloat16 [2, 16, 64, 2560], P('frame', 'row', None, 'head'), may hold values from -6 to 6
- target: bfloat16 [2, 16, 64, 2560], P('frame', 'row', None, 'head'), may hold values from -6 to 6
- gain_q: float32 [2560], P('head'), may hold values from 0.5 to 2
- gain_k: float32 [2560], P('head'), may hold values from 0.5 to 2
- kept: int32 [2, 16, 4], replicated, may hold values 0 or 1
Outputs:
- grad_q: bfloat16 [2, 16, 64, 2560], P('frame', 'row', None, 'head')
- grad_k: bfloat16 [2, 16, 64, 2560], P('frame', 'row', None, 'head')
- grad_v: bfloat16 [2, 16, 64, 2560], P('frame', 'row', None, 'head')
The draws below stay inside these ranges and needn't reach their ends.
All inputs are finite; a program needn't handle non-finite values.
Results may differ from the reference program's by a relative error of at most 0.0107.
The reference program's roundings to bfloat16 on the way (of `prob_b`, `d_out` and `score_grad`) count: a program that leaves them out, or rounds other values in their place, can miss the bound.
Values may be sent and summed in bfloat16 or wider, within the bound.
No kernel may reach another device: no remote copies, remote signals or barrier semaphores. Data moves between devices by JAX's collectives and lax.ppermute only.
A program may use at most 128 MiB of HBM per device.

```python
import math
import jax
import jax.numpy as jnp
from jax import lax

CW = 64
TC = 16
HEADS = 20
HD = 128
NF = 2
NR = 16
NCT = 4
FEAT = 2560


def scaled_pair(key):
    count = NF * NR * CW
    features = HEADS * HD
    head_of = jnp.arange(features) // HD
    jitter = jax.random.uniform(jax.random.fold_in(key, 11), (HEADS,))
    head_scale = 0.3 * 10.0 ** ((jnp.arange(HEADS) + jitter) / HEADS)
    column_scale = jnp.sum((head_of[:, None] == jnp.arange(HEADS)[None, :]) * head_scale[None, :], axis=1)
    rows_k = jnp.exp(jax.random.uniform(jax.random.fold_in(key, 12), (count, 1), minval=jnp.log(0.5), maxval=jnp.log(5.0)))
    rows_q = jnp.exp(jax.random.uniform(jax.random.fold_in(key, 13), (count, 1), minval=jnp.log(0.5), maxval=jnp.log(5.0)))
    base_k = jax.random.truncated_normal(jax.random.fold_in(key, 14), -4.0, 4.0, (count, features))
    base_q = jax.random.truncated_normal(jax.random.fold_in(key, 15), -4.0, 4.0, (count, features))
    keys_all = base_k * column_scale[None, :] * rows_k
    queries_all = base_q * column_scale[None, :] * rows_q
    shape = (NF, NR, CW, features)
    return (queries_all.reshape(shape), keys_all.reshape(shape))


def draw_q_pre(key, part):
    return scaled_pair(key)[0].astype(jnp.bfloat16)


def draw_k_pre(key, part):
    return scaled_pair(key)[1].astype(jnp.bfloat16)


def touch_ends(values, key, low, top_value):
    longest = values.shape.index(max(values.shape))
    spots = []
    for shift in (0, 1):
        where = [jax.random.randint(jax.random.fold_in(key, axis), (), 0, length) for axis, length in enumerate(values.shape)]
        where[longest] = (where[longest] + shift) % values.shape[longest]
        spots.append(tuple(where))
    return values.at[spots[0]].set(low).at[spots[1]].set(top_value)


def block_scale(rng, dims, split, least, top_value):
    loudness, own = 1.0, jax.random.fold_in(rng, 6)
    for position, blocks in split:
        heights = jnp.exp(jax.random.uniform(jax.random.fold_in(own, position), (blocks,), jnp.float32, least / len(split), top_value / len(split)))
        loudness = loudness * jnp.repeat(heights, dims[position] // blocks).reshape([-1 if axis == position else 1 for axis in range(len(dims))])
    return loudness


def bell_draw(key, shape, width, bound, pieces=(), kind=jnp.bfloat16):
    result = width * jax.random.normal(key, shape, jnp.float32)
    if pieces:
        result = result * block_scale(key, shape, pieces, -0.22, 0.18)
    return jnp.clip(result, -bound, bound).astype(kind)


def setup_inputs(seed: int = 0) -> dict:
    streams_of = jax.random.split(jax.random.key(seed), 8)
    q_pre = draw_q_pre(jax.random.fold_in(streams_of[7], 71), 0)
    k_pre = draw_k_pre(jax.random.fold_in(streams_of[7], 71), 0)
    values = bell_draw(streams_of[2], (NF, NR, CW, FEAT), 1.0, 6.0, ((0, 2), (1, 8), (3, 2)))
    target = bell_draw(streams_of[3], (NF, NR, CW, FEAT), 1.0, 6.0, ((0, 2), (1, 8), (3, 2)))
    gain_q = jnp.clip(jnp.exp(math.log(2.0) - 1.3862944 * jax.random.uniform(streams_of[4], (FEAT,), jnp.float32) ** block_scale(streams_of[4], (FEAT,), ((0, 2),), -0.2, 0.2)), 0.5, 2.0)
    gain_k = jnp.clip(jnp.exp(math.log(2.0) - 1.3862944 * jax.random.uniform(streams_of[5], (FEAT,), jnp.float32) ** block_scale(streams_of[5], (FEAT,), ((0, 2),), -0.2, 0.2)), 0.5, 2.0)
    kept = touch_ends((jax.random.randint(streams_of[6], (NF, NR, NCT), 0, 4) < 3).astype(jnp.int32), jax.random.fold_in(streams_of[6], 1), 0, 1)
    return dict(q_pre=q_pre, k_pre=k_pre, values=values, target=target, gain_q=gain_q, gain_k=gain_k, kept=kept)


norm_eps = 1e-06

def window_mask(kept_win, col_tile, tiles):
    near_cols = jnp.abs(col_tile[:, None] - col_tile[None, :]) <= 1
    same_tile = col_tile[:, None] == col_tile[None, :]
    one_hot = col_tile[:, None] == jnp.arange(tiles)[None, :]
    key_kept = jnp.any(one_hot[None, None] & (kept_win[:, :, None, :] > 0), axis=-1)
    centre = (jnp.arange(3)[:, None] == 1) & (jnp.arange(3)[None, :] == 1)
    allowed = near_cols[:, None, None, :] & (key_kept[None] | centre[None, :, :, None] & same_tile[:, None, None, :])
    return allowed.reshape(col_tile.shape[0], -1)

def key_mask(kept_own, valid_win, col_tile, tiles):
    near_cols = jnp.abs(col_tile[:, None] - col_tile[None, :]) <= 1
    same_tile = col_tile[:, None] == col_tile[None, :]
    one_hot = col_tile[:, None] == jnp.arange(tiles)[None, :]
    own_kept = jnp.any(one_hot & (kept_own[None, :] > 0), axis=-1)
    centre = (jnp.arange(3)[:, None] == 1) & (jnp.arange(3)[None, :] == 1)
    allowed = near_cols[None, None] & (own_kept[None, None, None, :] | centre[:, :, None, None] & same_tile[None, None]) & valid_win[:, :, None, None]
    return allowed.reshape(-1, col_tile.shape[0])

def reference(q_pre, k_pre, values, target, gain_q, gain_k, kept):
    features = HEADS * HD
    score_scale = HD ** (-0.5)
    q_float = q_pre.astype(jnp.float32)
    k_float = k_pre.astype(jnp.float32)
    scale_q = lax.rsqrt(lax.optimization_barrier(jnp.sum(q_float * q_float, -1, keepdims=True)) / features + norm_eps)
    scale_k = lax.rsqrt(lax.optimization_barrier(jnp.sum(k_float * k_float, -1, keepdims=True)) / features + norm_eps)
    q_norm = (q_float * scale_q * gain_q).astype(jnp.bfloat16)
    k_norm = (k_float * scale_k * gain_k).astype(jnp.bfloat16)
    col_tile = jnp.arange(CW) // TC
    pad_two = ((1, 1), (1, 1), (0, 0), (0, 0))
    kv_pad = jnp.stack([jnp.pad(k_norm, pad_two), jnp.pad(values, pad_two)])
    kept_pad = jnp.pad(kept, ((1, 1), (1, 1), (0, 0)))
    line_ids = jnp.arange(NF * NR, dtype=jnp.int32)
    q_lines = q_norm.reshape(NF * NR, CW, features)
    t_lines = target.reshape(NF * NR, CW, features)

    def query_pass(line):
        f_at = (line // NR).astype(jnp.int32)
        r_at = (line % NR).astype(jnp.int32)
        zero = jnp.int32(0)
        query = lax.dynamic_index_in_dim(q_lines, line, 0, False).reshape(CW, HEADS, HD).astype(jnp.float32)
        t_line = lax.dynamic_index_in_dim(t_lines, line, 0, False).reshape(CW, HEADS, HD).astype(jnp.float32)
        kv_win = lax.dynamic_slice(kv_pad, (zero, f_at, r_at, zero, zero), (2, 3, 3, CW, features))
        kept_win = lax.dynamic_slice(kept_pad, (f_at, r_at, zero), (3, 3, NCT))
        allowed = window_mask(kept_win, col_tile, NCT)
        key_block = kv_win[0].reshape(9 * CW, HEADS, HD).astype(jnp.float32)
        value_block = kv_win[1].reshape(9 * CW, HEADS, HD).astype(jnp.float32)
        scores = jnp.einsum('qhd,khd->hqk', query, key_block) * score_scale
        scores = jnp.where(allowed[None], scores, -jnp.inf)
        row_max = lax.optimization_barrier(jnp.max(scores, -1, keepdims=True))
        expo = jnp.where(allowed[None], jnp.exp(scores - row_max), 0.0)
        denominator = lax.optimization_barrier(jnp.sum(expo, -1, keepdims=True))
        probability = expo / denominator
        prob_b = probability.astype(jnp.bfloat16)
        attended = jnp.einsum('hqk,khd->qhd', prob_b.astype(jnp.float32), value_block)
        d_out = (attended - t_line).astype(jnp.bfloat16)
        delta_sum = lax.optimization_barrier(jnp.sum(d_out.astype(jnp.float32) * attended, -1)).T
        prob_grad = jnp.einsum('qhd,khd->hqk', d_out.astype(jnp.float32), value_block)
        score_grad = (probability * (prob_grad - delta_sum[:, :, None]) * score_scale).astype(jnp.bfloat16)
        dq_line = jnp.einsum('hqk,khd->qhd', score_grad.astype(jnp.float32), key_block)
        log_total = row_max[..., 0] + jnp.log(denominator[..., 0])
        return (dq_line.reshape(CW, features), d_out.reshape(CW, features), log_total, delta_sum)
    dq_lines, dout_lines, total_lines, delta_lines = lax.map(query_pass, line_ids)
    d_out_grid = dout_lines.reshape(NF, NR, CW, features)
    stat_grid = jnp.stack([total_lines.reshape(NF, NR, HEADS, CW), delta_lines.reshape(NF, NR, HEADS, CW)])
    qd_pad = jnp.stack([jnp.pad(q_norm, pad_two), jnp.pad(d_out_grid, pad_two)])
    stat_pad = jnp.pad(stat_grid, ((0, 0), (1, 1), (1, 1), (0, 0), (0, 0)))
    valid_pad = jnp.pad(jnp.ones((NF, NR), dtype=bool), ((1, 1), (1, 1)))
    k_lines = k_norm.reshape(NF * NR, CW, features)
    v_lines = values.reshape(NF * NR, CW, features)

    def key_pass(line):
        f_at = (line // NR).astype(jnp.int32)
        r_at = (line % NR).astype(jnp.int32)
        zero = jnp.int32(0)
        key_own = lax.dynamic_index_in_dim(k_lines, line, 0, False).reshape(CW, HEADS, HD).astype(jnp.float32)
        value_own = lax.dynamic_index_in_dim(v_lines, line, 0, False).reshape(CW, HEADS, HD).astype(jnp.float32)
        qd_win = lax.dynamic_slice(qd_pad, (zero, f_at, r_at, zero, zero), (2, 3, 3, CW, features))
        stat_win = lax.dynamic_slice(stat_pad, (zero, f_at, r_at, zero, zero), (2, 3, 3, HEADS, CW))
        valid_win = lax.dynamic_slice(valid_pad, (f_at, r_at), (3, 3))
        kept_own = lax.dynamic_slice(kept, (f_at, r_at, zero), (1, 1, NCT)).reshape(NCT)
        allowed = key_mask(kept_own, valid_win, col_tile, NCT)
        query_win = qd_win[0].reshape(9 * CW, HEADS, HD).astype(jnp.float32)
        dout_win = qd_win[1].reshape(9 * CW, HEADS, HD).astype(jnp.float32)
        total_win = jnp.transpose(stat_win[0], (2, 0, 1, 3)).reshape(HEADS, 9 * CW)
        delta_win = jnp.transpose(stat_win[1], (2, 0, 1, 3)).reshape(HEADS, 9 * CW)
        scores = jnp.einsum('qhd,khd->hqk', query_win, key_own) * score_scale
        probability = jnp.where(allowed[None], jnp.exp(scores - total_win[:, :, None]), 0.0)
        prob_b = probability.astype(jnp.bfloat16)
        prob_grad = jnp.einsum('qhd,khd->hqk', dout_win, value_own)
        score_grad = (probability * (prob_grad - delta_win[:, :, None]) * score_scale).astype(jnp.bfloat16)
        dk_line = jnp.einsum('hqk,qhd->khd', score_grad.astype(jnp.float32), query_win)
        dv_line = jnp.einsum('hqk,qhd->khd', prob_b.astype(jnp.float32), dout_win)
        return (dk_line.reshape(CW, features), dv_line.reshape(CW, features))
    dk_lines, dv_lines = lax.map(key_pass, line_ids)
    dq_norm = dq_lines.reshape(NF, NR, CW, features)
    dk_norm = dk_lines.reshape(NF, NR, CW, features)
    grad_v = dv_lines.reshape(NF, NR, CW, features).astype(jnp.bfloat16)
    gated_q = gain_q * dq_norm
    gated_k = gain_k * dk_norm
    sum_q = lax.optimization_barrier(jnp.sum(q_float * gated_q, -1, keepdims=True))
    sum_k = lax.optimization_barrier(jnp.sum(k_float * gated_k, -1, keepdims=True))
    grad_q = (scale_q * gated_q - q_float * scale_q ** 3 * sum_q / features).astype(jnp.bfloat16)
    grad_k = (scale_k * gated_k - k_float * scale_k ** 3 * sum_k / features).astype(jnp.bfloat16)
    return (grad_q, grad_k, grad_v)
```

```python
import functools

import jax
import jax.numpy as jnp
from jax import lax
from jax.experimental import pallas as pl
from jax.experimental.pallas import tpu as pltpu
from jax.sharding import PartitionSpec as P

TC = 16
HEADS = 20
HD = 128


norm_eps = 1e-06


def padded(x, sides, width):
    for axis, dim in sides:
        size, length = (lax.axis_size(axis), x.shape[dim])
        up = [(i, (i + 1) % size) for i in range(size - 1)]
        down = [(j, i) for i, j in up]
        last = lax.slice_in_dim(x, length - width, length, axis=dim)
        first = lax.slice_in_dim(x, 0, width, axis=dim)
        before = lax.ppermute(last, axis, up)
        after = lax.ppermute(first, axis, down)
        x = jnp.concatenate([before, x, after], axis=dim)
    return x


def from_behind(value, axis, steps):
    count = lax.axis_size(axis)
    first, last = (max(0, -steps), min(count, count - steps))
    return lax.ppermute(value, axis, [(source, source + steps) for source in range(first, last)])


def query_mask(kept_win, col_tile, tiles):
    near_cols = jnp.abs(col_tile[:, None] - col_tile[None, :]) <= 1
    same_tile = col_tile[:, None] == col_tile[None, :]
    one_hot = col_tile[:, None] == jnp.arange(tiles)[None, :]
    key_kept = jnp.any(one_hot[None, None] & (kept_win[:, :, None, :] > 0), axis=-1)
    centre = (jnp.arange(3)[:, None] == 1) & (jnp.arange(3)[None, :] == 1)
    allowed = near_cols[:, None, None, :] & (
        key_kept[None] | centre[None, :, :, None] & same_tile[:, None, None, :]
    )
    return allowed.reshape(col_tile.shape[0], -1)


def attend_line(query, kv_win, t_line, allowed):
    width, heads_dev, _ = query.shape
    score_scale = HD ** (-0.5)
    key_block = kv_win[0].reshape(9 * width, heads_dev, HD)
    value_block = kv_win[1].reshape(9 * width, heads_dev, HD)
    mask = allowed[None]
    scores = (
        jnp.einsum("qhd,khd->hqk", query, key_block, preferred_element_type=jnp.float32)
        * score_scale
    )
    scores = jnp.where(mask, scores, -jnp.inf)
    row_max = jnp.max(scores, -1, keepdims=True)
    expo = jnp.where(mask, jnp.exp(scores - row_max), 0.0)
    denominator = jnp.sum(expo, -1, keepdims=True)
    probability = expo / denominator
    prob_b = probability.astype(jnp.bfloat16)
    attended = jnp.einsum("hqk,khd->qhd", prob_b, value_block, preferred_element_type=jnp.float32)
    d_out = (attended - t_line.astype(jnp.float32)).astype(jnp.bfloat16)
    delta_sum = jnp.sum(d_out.astype(jnp.float32) * attended, -1).T
    prob_grad = jnp.einsum("qhd,khd->hqk", d_out, value_block, preferred_element_type=jnp.float32)
    score_grad = (probability * (prob_grad - delta_sum[:, :, None]) * score_scale).astype(
        jnp.bfloat16
    )
    dq_line = jnp.einsum("hqk,khd->qhd", score_grad, key_block, preferred_element_type=jnp.float32)
    log_total = row_max[..., 0] + jnp.log(denominator[..., 0])
    return (dq_line.reshape(width, heads_dev * HD), d_out, log_total, delta_sum, prob_b, score_grad)


def per_device(q_pre, k_pre, values, target, gain_q, gain_k, kept):
    frames, rows, width, feat_dev = q_pre.shape
    heads_dev = feat_dev // HD
    tiles = width // TC
    features = HEADS * HD
    line_count = frames * rows
    col_tile = jnp.arange(width) // TC
    q_float = q_pre.astype(jnp.float32)
    k_float = k_pre.astype(jnp.float32)
    square_q, square_k = lax.psum(
        (jnp.sum(q_float * q_float, -1), jnp.sum(k_float * k_float, -1)), "head"
    )
    scale_q = lax.rsqrt(square_q[..., None] / features + norm_eps)
    scale_k = lax.rsqrt(square_k[..., None] / features + norm_eps)
    q_norm = (q_float * scale_q * gain_q).astype(jnp.bfloat16)
    k_norm = (k_float * scale_k * gain_k).astype(jnp.bfloat16)
    kv_ext = padded(jnp.stack([k_norm, values]), (("frame", 1), ("row", 2)), 1)
    frame_at = lax.axis_index("frame")
    row_at = lax.axis_index("row")
    zero = jnp.int32(0)
    kept_pad = jnp.pad(kept, ((1, 1), (1, 1), (0, 0)))
    kept_ext = lax.dynamic_slice(
        kept_pad, (frame_at * frames, row_at * rows, zero), (frames + 2, rows + 2, tiles)
    )
    line_ids = jnp.arange(line_count, dtype=jnp.int32)
    q_lines = q_norm.reshape(line_count, width, heads_dev, HD)
    t_lines = target.reshape(line_count, width, heads_dev, HD)

    def query_window(line):
        f_at = line // rows
        r_at = line % rows
        kv_win = lax.dynamic_slice(
            kv_ext, (zero, f_at, r_at, zero, zero), (2, 3, 3, width, feat_dev)
        )
        kept_win = lax.dynamic_slice(kept_ext, (f_at, r_at, zero), (3, 3, tiles))
        return (f_at, r_at, kv_win, query_mask(kept_win, col_tile, tiles))

    def returned_step(totals, inputs):
        line, query, t_line = inputs
        f_at, r_at, kv_win, allowed = query_window(line)
        dq_line, d_out, log_total, delta_sum, prob_b, score_grad = attend_line(
            query, kv_win, t_line, allowed
        )
        key_grad = jnp.einsum("hqk,qhd->khd", score_grad, query, preferred_element_type=jnp.float32)
        value_grad = jnp.einsum("hqk,qhd->khd", prob_b, d_out, preferred_element_type=jnp.float32)
        both = jnp.stack(
            [key_grad.reshape(3, 3, width, feat_dev), value_grad.reshape(3, 3, width, feat_dev)]
        )
        start = (zero, f_at, r_at, zero, zero)
        current = lax.dynamic_slice(totals, start, (2, 3, 3, width, feat_dev))
        totals = lax.dynamic_update_slice(totals, current + both, start)
        return (totals, dq_line)

    empty = jnp.zeros((2, frames + 2, rows + 2, width, feat_dev), jnp.float32)
    totals, dq_lines = lax.scan(returned_step, empty, (line_ids, q_lines, t_lines))
    inner = totals[:, :, 1 : rows + 1]
    row_edges = (totals[:, :, 0:1], totals[:, :, rows + 1 : rows + 2])
    row_moved = [
        from_behind(row_edges[side], "row", by_value) for side, by_value in ((0, -1), (1, 1))
    ]
    inner = inner.at[:, :, rows - 1 : rows].add(row_moved[0])
    inner = inner.at[:, :, 0:1].add(row_moved[1])
    middle = inner[:, 1 : frames + 1]
    frame_edges = (inner[:, 0:1], inner[:, frames + 1 : frames + 2])
    frame_moved = [
        from_behind(frame_edges[side], "frame", by_value) for side, by_value in ((0, -1), (1, 1))
    ]
    middle = middle.at[:, frames - 1 : frames].add(frame_moved[0])
    middle = middle.at[:, 0:1].add(frame_moved[1])
    dk_norm = middle[0]
    value_total = middle[1]
    dq_norm = dq_lines.reshape(frames, rows, width, feat_dev)
    gated_q = gain_q * dq_norm
    gated_k = gain_k * dk_norm
    sum_q, sum_k = lax.psum(
        (jnp.sum(q_float * gated_q, -1), jnp.sum(k_float * gated_k, -1)), "head"
    )
    grad_q = (scale_q * gated_q - q_float * scale_q**3 * sum_q[..., None] / features).astype(
        jnp.bfloat16
    )
    grad_k = (scale_k * gated_k - k_float * scale_k**3 * sum_k[..., None] / features).astype(
        jnp.bfloat16
    )
    return (grad_q, grad_k, value_total.astype(jnp.bfloat16))


SWAP = [(0, 1), (1, 0)]
F32 = jnp.float32
BF16 = jnp.bfloat16
VMEM_LIMIT = 48 * 1024 * 1024


def call(body, out_shape, **kw):
    flops = kw.pop("flops", 10**6)
    moved = kw.pop("moved", 10**6)
    return pl.pallas_call(
        body,
        out_shape=out_shape,
        compiler_params=pltpu.CompilerParams(vmem_limit_bytes=VMEM_LIMIT),
        cost_estimate=pl.CostEstimate(flops=flops, bytes_accessed=moved, transcendentals=0),
        **kw,
    )


def halves(half):
    frame_at = lax.axis_index("frame")
    mine = pl.multiple_of(frame_at * half, HD)
    theirs = pl.multiple_of((1 - frame_at) * half, HD)
    return (pl.ds(mine, half), pl.ds(theirs, half))


def squares_kernel(q_ref, k_ref, v_ref, t_ref, sums_ref, vt_ref):
    tokens, feat_dev = q_ref.shape
    _, theirs = halves(feat_dev // 2)
    vt_ref[:tokens] = v_ref[:, theirs]
    vt_ref[tokens:] = t_ref[:, theirs]
    q_float = q_ref[...].astype(F32)
    k_float = k_ref[...].astype(F32)
    sums_ref[:tokens] = jnp.sum(q_float * q_float, -1, keepdims=True)
    sums_ref[tokens:] = jnp.sum(k_float * k_float, -1, keepdims=True)


def norm_kernel(
    width,
    q_ref,
    k_ref,
    v_ref,
    sums_ref,
    peer_ref,
    gain_q_ref,
    gain_k_ref,
    scale_ref,
    own_ref,
    swap_ref,
    up_ref,
    down_ref,
    swap_up_ref,
    swap_down_ref,
):
    tokens, feat_dev = q_ref.shape
    features = HEADS * HD
    mine, theirs = halves(feat_dev // 2)
    scale = lax.rsqrt((sums_ref[...] + peer_ref[...]) / features + norm_eps)
    scale_ref[...] = scale
    scale_q, scale_k = (scale[:tokens], scale[tokens:])
    for part, qk_ref, last_ref, first_ref in (
        (mine, own_ref, up_ref, down_ref),
        (theirs, swap_ref, swap_up_ref, swap_down_ref),
    ):
        q_norm = (q_ref[:, part].astype(F32) * scale_q * gain_q_ref[:, part]).astype(BF16)
        k_norm = (k_ref[:, part].astype(F32) * scale_k * gain_k_ref[:, part]).astype(BF16)
        qk_ref[:tokens] = q_norm
        qk_ref[tokens:] = k_norm
        last_ref[:width] = k_norm[tokens - width :]
        last_ref[width:] = v_ref[tokens - width :, part]
        first_ref[:width] = k_norm[:width]
        first_ref[width:] = v_ref[:width, part]


def attend_kernel(
    width,
    frame_ref,
    own_qk_ref,
    v_ref,
    t_ref,
    swap_qk_ref,
    swap_vt_ref,
    before_ref,
    after_ref,
    swap_before_ref,
    swap_after_ref,
    bias_ref,
    own_grad_ref,
    swap_grad_ref,
    before_grad_ref,
    after_grad_ref,
    swap_before_grad_ref,
    swap_after_grad_ref,
):
    tokens = v_ref.shape[0]
    score_scale = HD ** (-0.5)
    query = jnp.concatenate([own_qk_ref[:tokens], swap_qk_ref[:tokens]], 0)
    target = jnp.concatenate([t_ref[...], swap_vt_ref[tokens:]], 0)
    key = jnp.concatenate(
        [
            before_ref[:width],
            own_qk_ref[tokens:],
            after_ref[:width],
            swap_before_ref[:width],
            swap_qk_ref[tokens:],
            swap_after_ref[:width],
        ],
        0,
    )
    value = jnp.concatenate(
        [
            before_ref[width:],
            v_ref[...],
            after_ref[width:],
            swap_before_ref[width:],
            swap_vt_ref[:tokens],
            swap_after_ref[width:],
        ],
        0,
    )

    def product(a, b, a_dim, b_dim):
        return lax.dot_general(a, b, (((a_dim,), (b_dim,)), ((), ())), preferred_element_type=F32)

    scores = product(query, key, 1, 1) * score_scale + bias_ref[...]
    row_max = jnp.max(scores, -1, keepdims=True)
    expo = jnp.exp(scores - row_max)
    probability = expo * (1.0 / jnp.sum(expo, -1, keepdims=True))
    prob_b = probability.astype(BF16)
    attended = product(prob_b, value, 1, 0)
    d_out = (attended - target.astype(F32)).astype(BF16)
    delta_sum = jnp.sum(d_out.astype(F32) * attended, -1, keepdims=True)
    prob_grad = product(d_out, value, 1, 1)
    score_grad = (probability * (prob_grad - delta_sum) * score_scale).astype(BF16)
    dq = product(score_grad, key, 1, 0)
    dk = product(score_grad, query, 0, 0)
    dv = product(prob_b, d_out, 0, 0)
    side = tokens + 2 * width
    own_grad_ref[:tokens] = dq[:tokens]
    swap_grad_ref[:tokens] = dq[tokens:].astype(BF16)
    for at, grad in ((1, dk), (2, dv)):
        own_grad_ref[at * tokens : (at + 1) * tokens] = grad[width : width + tokens]
        swap_grad_ref[at * tokens : (at + 1) * tokens] = grad[
            side + width : side + width + tokens
        ].astype(BF16)
        to = slice((at - 1) * width, at * width)
        before_grad_ref[to] = grad[:width].astype(BF16)
        after_grad_ref[to] = grad[width + tokens : side].astype(BF16)
        swap_before_grad_ref[to] = grad[side : side + width].astype(BF16)
        swap_after_grad_ref[to] = grad[side + width + tokens :].astype(BF16)


def gather_kernel(
    width,
    q_ref,
    k_ref,
    gain_q_ref,
    gain_k_ref,
    own_ref,
    swap_ref,
    before_ref,
    after_ref,
    swap_before_ref,
    swap_after_ref,
    gated_q_ref,
    gated_k_ref,
    grad_v_ref,
    sums_ref,
):
    tokens, feat_dev = q_ref.shape
    mine, theirs = halves(feat_dev // 2)
    sum_q = jnp.zeros((tokens, 1), F32)
    sum_k = jnp.zeros((tokens, 1), F32)
    for part, grad_ref, last_ref, first_ref in (
        (mine, own_ref, before_ref, after_ref),
        (theirs, swap_ref, swap_before_ref, swap_after_ref),
    ):
        half = feat_dev // 2
        middle = jnp.zeros((tokens - 2 * width, half), F32)

        def total(at):
            sides = slice((at - 1) * width, at * width)
            edge = [last_ref[sides].astype(F32), middle, first_ref[sides].astype(F32)]
            if tokens == 2 * width:
                edge = [edge[0], edge[2]]
            grad = grad_ref[at * tokens : (at + 1) * tokens].astype(F32)
            return grad + jnp.concatenate(edge, 0)

        gated_q = gain_q_ref[:, part] * grad_ref[:tokens].astype(F32)
        gated_k = gain_k_ref[:, part] * total(1)
        grad_v_ref[:, part] = total(2).astype(BF16)
        gated_q_ref[:, part] = gated_q
        gated_k_ref[:, part] = gated_k
        sum_q += jnp.sum(q_ref[:, part].astype(F32) * gated_q, -1, keepdims=True)
        sum_k += jnp.sum(k_ref[:, part].astype(F32) * gated_k, -1, keepdims=True)
    sums_ref[:tokens] = sum_q
    sums_ref[tokens:] = sum_k


def finish_kernel(
    q_ref, k_ref, gated_q_ref, gated_k_ref, scale_ref, sums_ref, peer_ref, grad_q_ref, grad_k_ref
):
    tokens = q_ref.shape[0]
    features = HEADS * HD
    scale = scale_ref[...]
    slope = scale * scale * scale * (sums_ref[...] + peer_ref[...]) / features
    for rows, pre_ref, gated_ref, out_ref in (
        (slice(0, tokens), q_ref, gated_q_ref, grad_q_ref),
        (slice(tokens, 2 * tokens), k_ref, gated_k_ref, grad_k_ref),
    ):
        out_ref[...] = (
            scale[rows] * gated_ref[...] - pre_ref[...].astype(F32) * slope[rows]
        ).astype(BF16)


def window_bias(kept, rows, width, tiles):
    frame_at = lax.axis_index("frame")
    row_at = lax.axis_index("row")
    kept_pad = jnp.pad(kept, ((0, 0), (1, 1), (0, 0)))
    kept_win = lax.dynamic_slice_in_dim(kept_pad, row_at * rows, rows + 2, 1)
    kept_win = jnp.where(frame_at == 0, kept_win, kept_win[::-1])
    key_kept = jnp.repeat(kept_win.reshape(-1), width // tiles)
    query_at = jnp.arange(2 * rows * width)
    key_at = jnp.arange(2 * (rows + 2) * width)
    query_row, query_tile = (query_at // width, query_at % width // TC)
    key_row, key_tile = (key_at // width, key_at % width // TC)
    near_cols = jnp.abs(query_tile[:, None] - key_tile[None, :]) <= 1
    near_rows = jnp.abs((query_row % rows)[:, None] + 1 - (key_row % (rows + 2))[None, :]) <= 1
    same_line = (query_row // rows * (rows + 2) + query_row % rows + 1)[:, None] == key_row[None, :]
    same = same_line & (query_tile[:, None] == key_tile[None, :])
    allowed = near_cols & near_rows & ((key_kept > 0)[None, :] | same)
    return jnp.where(allowed, 0.0, -1e30).astype(F32)


def swapped_device(q_pre, k_pre, values, target, gain_q, gain_k, kept):
    frames, rows, width, feat_dev = q_pre.shape
    tokens = rows * width
    half = feat_dev // 2
    half_heads = half // HD
    row_blocks = lax.axis_size("row")
    q_all, k_all, v_all, t_all = (
        array.reshape(tokens, feat_dev) for array in (q_pre, k_pre, values, target)
    )
    gain_q = gain_q.reshape(1, feat_dev)
    gain_k = gain_k.reshape(1, feat_dev)
    up = [(r, r + 1) for r in range(row_blocks - 1)]
    down = [(r + 1, r) for r in range(row_blocks - 1)]
    swap_up, swap_down = (
        [(f * row_blocks + a, (1 - f) * row_blocks + b) for f in range(2) for a, b in pairs]
        for pairs in (up, down)
    )

    def shape(first, last, dtype=BF16):
        return jax.ShapeDtypeStruct((first, last), dtype)

    sums, vt_out = call(squares_kernel, (shape(2 * tokens, 1, F32), shape(2 * tokens, half)))(
        q_all, k_all, v_all, t_all
    )
    swap_vt = lax.ppermute(vt_out, "frame", SWAP)
    peer = lax.ppermute(sums, "head", SWAP)
    scale, own_qk, qk_out, last, first, swap_last, swap_first = call(
        functools.partial(norm_kernel, width),
        (shape(2 * tokens, 1, F32),)
        + (shape(2 * tokens, half),) * 2
        + (shape(2 * width, half),) * 4,
    )(q_all, k_all, v_all, sums, peer, gain_q, gain_k)
    swap_qk = lax.ppermute(qk_out, "frame", SWAP)
    swap_before = lax.ppermute(swap_last, ("frame", "row"), swap_up)
    swap_after = lax.ppermute(swap_first, ("frame", "row"), swap_down)
    before = lax.ppermute(last, "row", up)
    after = lax.ppermute(first, "row", down)
    bias = window_bias(kept, rows, width, kept.shape[-1])
    frame_at = lax.axis_index("frame").reshape(1).astype(jnp.int32)

    def by_head(size):
        return pl.BlockSpec((size, HD), lambda h, f: (0, h))

    own_half = pl.BlockSpec((tokens, HD), lambda h, f: (0, f[0] * half_heads + h))
    own_grad, swap_grad, before_grad, after_grad, swap_before_grad, swap_after_grad = call(
        functools.partial(attend_kernel, width),
        (shape(3 * tokens, half, F32), shape(3 * tokens, half))
        + (shape(2 * width, half),) * 4,
        grid_spec=pltpu.PrefetchScalarGridSpec(
            num_scalar_prefetch=1,
            grid=(half_heads,),
            in_specs=[
                by_head(2 * tokens),
                own_half,
                own_half,
                by_head(2 * tokens),
                by_head(2 * tokens),
                by_head(2 * width),
                by_head(2 * width),
                by_head(2 * width),
                by_head(2 * width),
                pl.BlockSpec(bias.shape, lambda h, f: (0, 0)),
            ],
            out_specs=[by_head(3 * tokens)] * 2 + [by_head(2 * width)] * 4,
        ),
        flops=10**9,
        moved=4 * 10**6,
    )(
        frame_at,
        own_qk,
        v_all,
        t_all,
        swap_qk,
        swap_vt,
        before,
        after,
        swap_before,
        swap_after,
        bias,
    )
    swap_total = lax.ppermute(swap_grad, "frame", SWAP)
    swap_last_in = lax.ppermute(swap_before_grad, ("frame", "row"), swap_down)
    swap_first_in = lax.ppermute(swap_after_grad, ("frame", "row"), swap_up)
    last_in = lax.ppermute(before_grad, "row", down)
    first_in = lax.ppermute(after_grad, "row", up)
    gated_q, gated_k, grad_v, sum_terms = call(
        functools.partial(gather_kernel, width),
        (shape(tokens, feat_dev, F32),) * 2
        + (shape(tokens, feat_dev), shape(2 * tokens, 1, F32)),
    )(
        q_all,
        k_all,
        gain_q,
        gain_k,
        own_grad,
        swap_total,
        first_in,
        last_in,
        swap_first_in,
        swap_last_in,
    )
    sum_peer = lax.ppermute(sum_terms, "head", SWAP)
    grad_q, grad_k = call(finish_kernel, (shape(tokens, feat_dev),) * 2)(
        q_all, k_all, gated_q, gated_k, scale, sum_terms, sum_peer
    )
    return tuple(
        array.reshape(frames, rows, width, feat_dev) for array in (grad_q, grad_k, grad_v)
    )


def solution(mesh):
    return jax.shard_map(
        swapped_device if mesh.shape["frame"] == 2 else per_device,
        mesh=mesh,
        in_specs=(
            P("frame", "row", None, "head"),
            P("frame", "row", None, "head"),
            P("frame", "row", None, "head"),
            P("frame", "row", None, "head"),
            P("head"),
            P("head"),
            P(),
        ),
        out_specs=(
            P("frame", "row", None, "head"),
            P("frame", "row", None, "head"),
            P("frame", "row", None, "head"),
        ),
        check_vma=False,
    )
```

```python
import functools

import jax
import jax.numpy as jnp
from jax import lax
from jax.experimental import pallas as pl
from jax.experimental.pallas import tpu as pltpu
from jax.sharding import PartitionSpec as P

TC = 16
HEADS = 20
HD = 128


norm_eps = 1e-06


def padded(x, sides, width):
    for axis, dim in sides:
        size, length = (lax.axis_size(axis), x.shape[dim])
        up = [(i, (i + 1) % size) for i in range(size - 1)]
        down = [(j, i) for i, j in up]
        last = lax.slice_in_dim(x, length - width, length, axis=dim)
        first = lax.slice_in_dim(x, 0, width, axis=dim)
        before = lax.ppermute(last, axis, up)
        after = lax.ppermute(first, axis, down)
        x = jnp.concatenate([before, x, after], axis=dim)
    return x


def from_behind(value, axis, steps):
    count = lax.axis_size(axis)
    first, last = (max(0, -steps), min(count, count - steps))
    return lax.ppermute(value, axis, [(source, source + steps) for source in range(first, last)])


def query_mask(kept_win, col_tile, tiles):
    near_cols = jnp.abs(col_tile[:, None] - col_tile[None, :]) <= 1
    same_tile = col_tile[:, None] == col_tile[None, :]
    one_hot = col_tile[:, None] == jnp.arange(tiles)[None, :]
    key_kept = jnp.any(one_hot[None, None] & (kept_win[:, :, None, :] > 0), axis=-1)
    centre = (jnp.arange(3)[:, None] == 1) & (jnp.arange(3)[None, :] == 1)
    allowed = near_cols[:, None, None, :] & (
        key_kept[None] | centre[None, :, :, None] & same_tile[:, None, None, :]
    )
    return allowed.reshape(col_tile.shape[0], -1)


def attend_line(query, kv_win, t_line, allowed):
    width, heads_dev, _ = query.shape
    score_scale = HD ** (-0.5)
    key_block = kv_win[0].reshape(9 * width, heads_dev, HD)
    value_block = kv_win[1].reshape(9 * width, heads_dev, HD)
    mask = allowed[None]
    scores = (
        jnp.einsum("qhd,khd->hqk", query, key_block, preferred_element_type=jnp.float32)
        * score_scale
    )
    scores = jnp.where(mask, scores, -jnp.inf)
    row_max = jnp.max(scores, -1, keepdims=True)
    expo = jnp.where(mask, jnp.exp(scores - row_max), 0.0)
    denominator = jnp.sum(expo, -1, keepdims=True)
    probability = expo / denominator
    prob_b = probability.astype(jnp.bfloat16)
    attended = jnp.einsum("hqk,khd->qhd", prob_b, value_block, preferred_element_type=jnp.float32)
    d_out = (attended - t_line.astype(jnp.float32)).astype(jnp.bfloat16)
    delta_sum = jnp.sum(d_out.astype(jnp.float32) * attended, -1).T
    prob_grad = jnp.einsum("qhd,khd->hqk", d_out, value_block, preferred_element_type=jnp.float32)
    score_grad = (probability * (prob_grad - delta_sum[:, :, None]) * score_scale).astype(
        jnp.bfloat16
    )
    dq_line = jnp.einsum("hqk,khd->qhd", score_grad, key_block, preferred_element_type=jnp.float32)
    log_total = row_max[..., 0] + jnp.log(denominator[..., 0])
    return (dq_line.reshape(width, heads_dev * HD), d_out, log_total, delta_sum, prob_b, score_grad)


def per_device(q_pre, k_pre, values, target, gain_q, gain_k, kept):
    frames, rows, width, feat_dev = q_pre.shape
    heads_dev = feat_dev // HD
    tiles = width // TC
    features = HEADS * HD
    line_count = frames * rows
    col_tile = jnp.arange(width) // TC
    q_float = q_pre.astype(jnp.float32)
    k_float = k_pre.astype(jnp.float32)
    square_q, square_k = lax.psum(
        (jnp.sum(q_float * q_float, -1), jnp.sum(k_float * k_float, -1)), "head"
    )
    scale_q = lax.rsqrt(square_q[..., None] / features + norm_eps)
    scale_k = lax.rsqrt(square_k[..., None] / features + norm_eps)
    q_norm = (q_float * scale_q * gain_q).astype(jnp.bfloat16)
    k_norm = (k_float * scale_k * gain_k).astype(jnp.bfloat16)
    kv_ext = padded(jnp.stack([k_norm, values]), (("frame", 1), ("row", 2)), 1)
    frame_at = lax.axis_index("frame")
    row_at = lax.axis_index("row")
    zero = jnp.int32(0)
    kept_pad = jnp.pad(kept, ((1, 1), (1, 1), (0, 0)))
    kept_ext = lax.dynamic_slice(
        kept_pad, (frame_at * frames, row_at * rows, zero), (frames + 2, rows + 2, tiles)
    )
    line_ids = jnp.arange(line_count, dtype=jnp.int32)
    q_lines = q_norm.reshape(line_count, width, heads_dev, HD)
    t_lines = target.reshape(line_count, width, heads_dev, HD)

    def query_window(line):
        f_at = line // rows
        r_at = line % rows
        kv_win = lax.dynamic_slice(
            kv_ext, (zero, f_at, r_at, zero, zero), (2, 3, 3, width, feat_dev)
        )
        kept_win = lax.dynamic_slice(kept_ext, (f_at, r_at, zero), (3, 3, tiles))
        return (f_at, r_at, kv_win, query_mask(kept_win, col_tile, tiles))

    def returned_step(totals, inputs):
        line, query, t_line = inputs
        f_at, r_at, kv_win, allowed = query_window(line)
        dq_line, d_out, log_total, delta_sum, prob_b, score_grad = attend_line(
            query, kv_win, t_line, allowed
        )
        key_grad = jnp.einsum("hqk,qhd->khd", score_grad, query, preferred_element_type=jnp.float32)
        value_grad = jnp.einsum("hqk,qhd->khd", prob_b, d_out, preferred_element_type=jnp.float32)
        both = jnp.stack(
            [key_grad.reshape(3, 3, width, feat_dev), value_grad.reshape(3, 3, width, feat_dev)]
        )
        start = (zero, f_at, r_at, zero, zero)
        current = lax.dynamic_slice(totals, start, (2, 3, 3, width, feat_dev))
        totals = lax.dynamic_update_slice(totals, current + both, start)
        return (totals, dq_line)

    empty = jnp.zeros((2, frames + 2, rows + 2, width, feat_dev), jnp.float32)
    totals, dq_lines = lax.scan(returned_step, empty, (line_ids, q_lines, t_lines))
    inner = totals[:, :, 1 : rows + 1]
    row_edges = (totals[:, :, 0:1], totals[:, :, rows + 1 : rows + 2])
    row_moved = [
        from_behind(row_edges[side], "row", by_value) for side, by_value in ((0, -1), (1, 1))
    ]
    inner = inner.at[:, :, rows - 1 : rows].add(row_moved[0])
    inner = inner.at[:, :, 0:1].add(row_moved[1])
    middle = inner[:, 1 : frames + 1]
    frame_edges = (inner[:, 0:1], inner[:, frames + 1 : frames + 2])
    frame_moved = [
        from_behind(frame_edges[side], "frame", by_value) for side, by_value in ((0, -1), (1, 1))
    ]
    middle = middle.at[:, frames - 1 : frames].add(frame_moved[0])
    middle = middle.at[:, 0:1].add(frame_moved[1])
    dk_norm = middle[0]
    value_total = middle[1]
    dq_norm = dq_lines.reshape(frames, rows, width, feat_dev)
    gated_q = gain_q * dq_norm
    gated_k = gain_k * dk_norm
    sum_q, sum_k = lax.psum(
        (jnp.sum(q_float * gated_q, -1), jnp.sum(k_float * gated_k, -1)), "head"
    )
    grad_q = (scale_q * gated_q - q_float * scale_q**3 * sum_q[..., None] / features).astype(
        jnp.bfloat16
    )
    grad_k = (scale_k * gated_k - k_float * scale_k**3 * sum_k[..., None] / features).astype(
        jnp.bfloat16
    )
    return (grad_q, grad_k, value_total.astype(jnp.bfloat16))


SWAP = [(0, 1), (1, 0)]
F32 = jnp.float32
BF16 = jnp.bfloat16
VMEM_LIMIT = 48 * 1024 * 1024


def call(body, out_shape, flops=10**6, moved=10**6, **kw):
    return pl.pallas_call(
        body,
        out_shape=out_shape,
        compiler_params=pltpu.CompilerParams(vmem_limit_bytes=VMEM_LIMIT),
        cost_estimate=pl.CostEstimate(flops=flops, bytes_accessed=moved, transcendentals=0),
        **kw,
    )


def halves(half):
    frame_at = lax.axis_index("frame")
    mine = pl.multiple_of(frame_at * half, HD)
    theirs = pl.multiple_of((1 - frame_at) * half, HD)
    return (pl.ds(mine, half), pl.ds(theirs, half))


def sides(width):
    odd = lax.rem(lax.axis_index("row"), 2)
    near = pl.multiple_of((1 - odd) * width, width)
    far = pl.multiple_of(odd * width, width)
    return (pl.ds(near, width), pl.ds(far, width))


def load_kernel(q_in, k_in, v_in, t_in, q_ref, k_ref, v_ref, t_ref, sums_ref, v_out_ref, sems):
    tokens, feat_dev = q_ref.shape
    _, theirs = halves(feat_dev // 2)
    pairs = ((v_in, v_ref), (q_in, q_ref), (k_in, k_ref), (t_in, t_ref))
    copies = [pltpu.make_async_copy(a, b, sems.at[i]) for i, (a, b) in enumerate(pairs)]
    for copy in copies:
        copy.start()
    copies[0].wait()
    v_out_ref[...] = v_ref[:, theirs]
    copies[1].wait()
    q_float = q_ref[...].astype(F32)
    sums_ref[:tokens] = jnp.sum(q_float * q_float, -1, keepdims=True)
    copies[2].wait()
    k_float = k_ref[...].astype(F32)
    sums_ref[tokens:] = jnp.sum(k_float * k_float, -1, keepdims=True)
    copies[3].wait()


def norm_kernel(
    width,
    q_ref,
    k_ref,
    v_ref,
    t_ref,
    sums_ref,
    peer_ref,
    gain_q_ref,
    gain_k_ref,
    scale_ref,
    own_ref,
    k_out_ref,
    qt_out_ref,
    near_ref,
    far_ref,
):
    tokens, feat_dev = q_ref.shape
    features = HEADS * HD
    mine, theirs = halves(feat_dev // 2)
    near, far = sides(width)
    scale = lax.rsqrt((sums_ref[...] + peer_ref[...]) / features + norm_eps)
    scale_ref[...] = scale
    scale_q, scale_k = (scale[:tokens], scale[tokens:])

    def normed(ref, part, scales, gain_ref):
        return (ref[:, part].astype(F32) * scales * gain_ref[:, part]).astype(BF16)

    k_out_ref[...] = normed(k_ref, theirs, scale_k, gain_k_ref)
    qt_out_ref[:tokens] = normed(q_ref, theirs, scale_q, gain_q_ref)
    qt_out_ref[tokens:] = t_ref[:, theirs]
    own_ref[:tokens] = normed(k_ref, mine, scale_k, gain_k_ref)
    own_ref[tokens:] = normed(q_ref, mine, scale_q, gain_q_ref)
    for out_ref, rows in ((near_ref, near), (far_ref, far)):
        out_ref[:width] = own_ref[rows]
        out_ref[width:] = v_ref[rows, mine]


def relay_kernel(width, k_ref, v_ref, near_ref, far_ref):
    for out_ref, rows in zip((near_ref, far_ref), sides(width)):
        out_ref[:width] = k_ref[rows]
        out_ref[width:] = v_ref[rows]


def attend_kernel(
    width,
    near_ref,
    far_ref,
    swap_near_ref,
    swap_far_ref,
    own_ref,
    v_ref,
    t_ref,
    swap_k_ref,
    swap_v_ref,
    swap_qt_ref,
    bias_ref,
    own_grad_ref,
    swap_first_ref,
    swap_last_ref,
    near_grad_ref,
    far_grad_ref,
    swap_near_grad_ref,
    swap_far_grad_ref,
):
    tokens, half = swap_k_ref.shape
    score_scale = HD ** (-0.5)
    mine = lax.axis_index("frame") * half
    odd = lax.rem(lax.axis_index("row"), 2)
    bias = bias_ref[...]
    own_rows = slice(width, width + tokens)
    side = tokens + 2 * width

    def product(a, b, a_dim, b_dim):
        return lax.dot_general(a, b, (((a_dim,), (b_dim,)), ((), ())), preferred_element_type=F32)

    for head in range(half // HD):
        at = slice(head * HD, (head + 1) * HD)
        mine_at = pl.ds(pl.multiple_of(mine + head * HD, HD), HD)
        query = jnp.concatenate([own_ref[tokens:, at], swap_qt_ref[:tokens, at]], 0)
        target = jnp.concatenate([t_ref[:, mine_at], swap_qt_ref[tokens:, at]], 0)
        key = jnp.concatenate(
            [
                near_ref[:width, at],
                own_ref[:tokens, at],
                far_ref[:width, at],
                swap_near_ref[:width, at],
                swap_k_ref[:, at],
                swap_far_ref[:width, at],
            ],
            0,
        )
        value = jnp.concatenate(
            [
                near_ref[width:, at],
                v_ref[:, mine_at],
                far_ref[width:, at],
                swap_near_ref[width:, at],
                swap_v_ref[:, at],
                swap_far_ref[width:, at],
            ],
            0,
        )
        scores = product(query, key, 1, 1) * score_scale + bias
        row_max = jnp.max(scores, -1, keepdims=True)
        expo = jnp.exp(scores - row_max)
        probability = expo * (1.0 / jnp.sum(expo, -1, keepdims=True))
        prob_b = probability.astype(BF16)
        attended = product(prob_b, value, 1, 0)
        d_out = (attended - target.astype(F32)).astype(BF16)
        delta_sum = jnp.sum(d_out.astype(F32) * attended, -1, keepdims=True)
        prob_grad = product(d_out, value, 1, 1)
        score_grad = (probability * (prob_grad - delta_sum) * score_scale).astype(BF16)
        dq = product(score_grad, key, 1, 0)
        own_grad_ref[:tokens, at] = dq[:tokens]
        swap_first_ref[:tokens, at] = dq[tokens:].astype(BF16)
        dk = product(score_grad, query, 0, 0)
        dv = product(prob_b, d_out, 0, 0)
        for place, grad in ((0, dk), (1, dv)):
            own_at = slice((1 + place) * tokens, (2 + place) * tokens)
            own_grad_ref[own_at, at] = grad[own_rows]
            to = slice(place * width, (place + 1) * width)
            near_grad_ref[to, at] = grad[:width].astype(BF16)
            far_grad_ref[to, at] = grad[width + tokens : side].astype(BF16)
            other = grad[side:]
            swap_near_grad_ref[to, at] = other[:width].astype(BF16)
            swap_far_grad_ref[to, at] = other[width + tokens :].astype(BF16)
            first, last = (other[width : 2 * width], other[2 * width : 3 * width])
            first_to = slice(tokens + place * width, tokens + (place + 1) * width)
            swap_first_ref[first_to, at] = jnp.where(odd == 0, last, first).astype(BF16)
            swap_last_ref[to, at] = jnp.where(odd == 0, first, last)


def add_kernel(a_ref, b_ref, out_ref):
    out_ref[...] = (a_ref[...] + b_ref[...].astype(F32)).astype(BF16)


def gather_kernel(
    width,
    q_ref,
    k_ref,
    gain_q_ref,
    gain_k_ref,
    own_ref,
    near_ref,
    far_ref,
    swap_first_ref,
    swap_last_ref,
    swap_near_ref,
    gated_q_ref,
    gated_k_ref,
    grad_v_ref,
    sums_ref,
    total_ref,
):
    tokens, feat_dev = q_ref.shape
    mine, theirs = halves(feat_dev // 2)
    near, far = sides(width)
    k_at, v_at = (slice(0, width), slice(width, 2 * width))

    def total(own_base, near_terms, far_terms):
        for rows, terms in ((near, near_terms), (far, far_terms)):
            value = sum(terms[1:], terms[0])
            total_ref[rows] = value if own_base is None else value + own_base[rows]
        return total_ref[...]

    def term(ref, at):
        return ref[at].astype(F32)

    own_dk = total(own_ref.at[tokens : 2 * tokens], [term(near_ref, k_at)], [term(far_ref, k_at)])
    gated_k_mine = gain_k_ref[:, mine] * own_dk
    own_dv = total(own_ref.at[2 * tokens :], [term(near_ref, v_at)], [term(far_ref, v_at)])
    grad_v_ref[:, mine] = own_dv.astype(BF16)
    gated_q_mine = gain_q_ref[:, mine] * own_ref[:tokens]
    first_k = term(swap_first_ref, slice(tokens, tokens + width))
    first_v = term(swap_first_ref, slice(tokens + width, tokens + 2 * width))
    swap_dk = total(
        None, [first_k, term(swap_near_ref, k_at)], [term(swap_last_ref, k_at)]
    )
    gated_k_theirs = gain_k_ref[:, theirs] * swap_dk
    swap_dv = total(
        None, [first_v, term(swap_near_ref, v_at)], [term(swap_last_ref, v_at)]
    )
    grad_v_ref[:, theirs] = swap_dv.astype(BF16)
    gated_q_theirs = gain_q_ref[:, theirs] * term(swap_first_ref, slice(0, tokens))
    gated_q_ref[:, mine] = gated_q_mine
    gated_q_ref[:, theirs] = gated_q_theirs
    gated_k_ref[:, mine] = gated_k_mine
    gated_k_ref[:, theirs] = gated_k_theirs
    sums_ref[:tokens] = jnp.sum(q_ref[...].astype(F32) * gated_q_ref[...], -1, keepdims=True)
    sums_ref[tokens:] = jnp.sum(k_ref[...].astype(F32) * gated_k_ref[...], -1, keepdims=True)


def finish_kernel(
    q_ref, k_ref, gated_q_ref, gated_k_ref, scale_ref, sums_ref, peer_ref, grad_q_ref, grad_k_ref
):
    tokens = q_ref.shape[0]
    features = HEADS * HD
    scale = scale_ref[...]
    slope = scale * scale * scale * (sums_ref[...] + peer_ref[...]) / features
    for rows, pre_ref, gated_ref, out_ref in (
        (slice(0, tokens), q_ref, gated_q_ref, grad_q_ref),
        (slice(tokens, 2 * tokens), k_ref, gated_k_ref, grad_k_ref),
    ):
        out_ref[...] = (
            scale[rows] * gated_ref[...] - pre_ref[...].astype(F32) * slope[rows]
        ).astype(BF16)


def window_bias(kept, rows, width, tiles):
    frame_at = lax.axis_index("frame")
    row_at = lax.axis_index("row")
    odd = lax.rem(row_at, 2)
    kept_pad = jnp.pad(kept, ((0, 0), (1, 1), (0, 0)))
    kept_win = lax.dynamic_slice_in_dim(kept_pad, row_at * rows, rows + 2, 1)
    kept_win = jnp.where(frame_at == 0, kept_win, kept_win[::-1])
    turned = jnp.concatenate([kept_win[:, 3:], kept_win[:, 1:3], kept_win[:, :1]], 1)
    kept_win = jnp.where(odd == 0, turned, kept_win)
    key_kept = jnp.repeat(kept_win.reshape(-1), width // tiles)
    query_at = jnp.arange(2 * rows * width)
    key_at = jnp.arange(2 * (rows + 2) * width)
    query_row, query_tile = (query_at // width, query_at % width // TC)
    key_slot, key_tile = (key_at // width, key_at % width // TC)
    key_row = key_slot % (rows + 2) - 1
    outer = (key_row < 0) | (key_row >= rows)
    key_row = jnp.where(outer & (odd == 0), rows - 1 - key_row, key_row)
    near_cols = jnp.abs(query_tile[:, None] - key_tile[None, :]) <= 1
    near_rows = jnp.abs((query_row % rows)[:, None] - key_row[None, :]) <= 1
    same_line = (query_row // rows * (rows + 2) + query_row % rows + 1)[:, None] == key_slot[None, :]
    same = same_line & (query_tile[:, None] == key_tile[None, :])
    allowed = near_cols & near_rows & ((key_kept > 0)[None, :] | same)
    return jnp.where(allowed, 0.0, -1e30).astype(F32)


def swapped_device(q_pre, k_pre, values, target, gain_q, gain_k, kept):
    frames, rows, width, feat_dev = q_pre.shape
    tokens = rows * width
    half = feat_dev // 2
    row_blocks = lax.axis_size("row")
    inputs = [array.reshape(tokens, feat_dev) for array in (q_pre, k_pre, values, target)]
    gain_q = gain_q.reshape(1, feat_dev)
    gain_k = gain_k.reshape(1, feat_dev)
    near_pairs = [(r, r + 1) for r in range(0, row_blocks - 1, 2)]
    far_pairs = [(r, r + 1) for r in range(1, row_blocks - 1, 2)]
    near, far = (pairs + [(b, a) for a, b in pairs] for pairs in (near_pairs, far_pairs))
    swap_near = [
        (f * row_blocks + a, (1 - f) * row_blocks + b) for f in range(2) for a, b in near
    ]

    def shape(first, last, dtype=BF16):
        return jax.ShapeDtypeStruct((first, last), dtype)

    block = shape(tokens, feat_dev)
    sum_pair = shape(2 * tokens, 1, F32)
    tokens_half = shape(tokens, half)
    edge = shape(2 * width, half)

    q_all, k_all, v_all, t_all, sums, v_out = call(
        load_kernel,
        (block,) * 4 + (sum_pair, tokens_half),
        in_specs=[pl.BlockSpec(memory_space=pltpu.HBM)] * 4,
        scratch_shapes=[pltpu.SemaphoreType.DMA((4,))],
    )(*inputs)
    swap_v = lax.ppermute(v_out, "frame", SWAP)
    peer = lax.ppermute(sums, "head", SWAP)
    scale, own_kq, k_out, qt_out, near_out, far_out = call(
        functools.partial(norm_kernel, width),
        (sum_pair, shape(2 * tokens, half), tokens_half, shape(2 * tokens, half), edge, edge),
    )(q_all, k_all, v_all, t_all, sums, peer, gain_q, gain_k)
    swap_k = lax.ppermute(k_out, "frame", SWAP)
    near_in = lax.ppermute(near_out, "row", near)
    far_in = lax.ppermute(far_out, "row", far)
    swap_qt = lax.ppermute(qt_out, "frame", SWAP)
    relay_near, relay_far = call(functools.partial(relay_kernel, width), (edge, edge))(
        swap_k, swap_v
    )
    swap_near_in = lax.ppermute(relay_near, "row", near)
    swap_far_in = lax.ppermute(relay_far, "row", far)
    bias = window_bias(kept, rows, width, kept.shape[-1])
    own_grad, first_out, last_terms, near_out, far_out, swap_near_out, swap_far_out = call(
        functools.partial(attend_kernel, width),
        (shape(3 * tokens, half, F32), shape(2 * tokens, half), shape(2 * width, half, F32))
        + (edge,) * 4,
        flops=10**9,
        moved=4 * 10**6,
    )(
        near_in,
        far_in,
        swap_near_in,
        swap_far_in,
        own_kq,
        v_all,
        t_all,
        swap_k,
        swap_v,
        swap_qt,
        bias,
    )
    swap_first = lax.ppermute(first_out, "frame", SWAP)
    far_terms = lax.ppermute(swap_far_out, "row", far)
    last_out = call(add_kernel, edge)(last_terms, far_terms)
    swap_near_total = lax.ppermute(swap_near_out, ("frame", "row"), swap_near)
    far_total = lax.ppermute(far_out, "row", far)
    near_total = lax.ppermute(near_out, "row", near)
    swap_last = lax.ppermute(last_out, "frame", SWAP)
    gated_q, gated_k, grad_v, sum_terms = call(
        functools.partial(gather_kernel, width),
        (shape(tokens, feat_dev, F32),) * 2 + (block, sum_pair),
        scratch_shapes=[pltpu.VMEM((tokens, half), F32)],
    )(
        q_all,
        k_all,
        gain_q,
        gain_k,
        own_grad,
        near_total,
        far_total,
        swap_first,
        swap_last,
        swap_near_total,
    )
    sum_peer = lax.ppermute(sum_terms, "head", SWAP)
    grad_q, grad_k = call(finish_kernel, (block, block))(
        q_all, k_all, gated_q, gated_k, scale, sum_terms, sum_peer
    )
    return tuple(
        array.reshape(frames, rows, width, feat_dev) for array in (grad_q, grad_k, grad_v)
    )


def on_device(q_pre, *rest):
    frames, rows, _, feat_dev = q_pre.shape
    paired = lax.axis_size("frame") == 2 and frames == 1 and rows == 2
    if paired and feat_dev % (2 * HD) == 0:
        return swapped_device(q_pre, *rest)
    return per_device(q_pre, *rest)


def solution(mesh):
    return jax.shard_map(
        on_device,
        mesh=mesh,
        in_specs=(
            P("frame", "row", None, "head"),
            P("frame", "row", None, "head"),
            P("frame", "row", None, "head"),
            P("frame", "row", None, "head"),
            P("head"),
            P("head"),
            P(),
        ),
        out_specs=(
            P("frame", "row", None, "head"),
            P("frame", "row", None, "head"),
            P("frame", "row", None, "head"),
        ),
        check_vma=False,
    )
```

```python
import functools

import jax
import jax.numpy as jnp
from jax import lax
from jax.experimental import pallas as pl
from jax.experimental.pallas import tpu as pltpu
from jax.sharding import PartitionSpec as P

TC = 16
HEADS = 20
HD = 128


norm_eps = 1e-06


def padded(x, sides, width):
    for axis, dim in sides:
        size, length = (lax.axis_size(axis), x.shape[dim])
        up = [(i, (i + 1) % size) for i in range(size - 1)]
        down = [(j, i) for i, j in up]
        last = lax.slice_in_dim(x, length - width, length, axis=dim)
        first = lax.slice_in_dim(x, 0, width, axis=dim)
        before = lax.ppermute(last, axis, up)
        after = lax.ppermute(first, axis, down)
        x = jnp.concatenate([before, x, after], axis=dim)
    return x


def from_behind(value, axis, steps):
    count = lax.axis_size(axis)
    first, last = (max(0, -steps), min(count, count - steps))
    return lax.ppermute(value, axis, [(source, source + steps) for source in range(first, last)])


def query_mask(kept_win, col_tile, tiles):
    near_cols = jnp.abs(col_tile[:, None] - col_tile[None, :]) <= 1
    same_tile = col_tile[:, None] == col_tile[None, :]
    one_hot = col_tile[:, None] == jnp.arange(tiles)[None, :]
    key_kept = jnp.any(one_hot[None, None] & (kept_win[:, :, None, :] > 0), axis=-1)
    centre = (jnp.arange(3)[:, None] == 1) & (jnp.arange(3)[None, :] == 1)
    allowed = near_cols[:, None, None, :] & (
        key_kept[None] | centre[None, :, :, None] & same_tile[:, None, None, :]
    )
    return allowed.reshape(col_tile.shape[0], -1)


def attend_line(query, kv_win, t_line, allowed):
    width, heads_dev, _ = query.shape
    score_scale = HD ** (-0.5)
    key_block = kv_win[0].reshape(9 * width, heads_dev, HD)
    value_block = kv_win[1].reshape(9 * width, heads_dev, HD)
    mask = allowed[None]
    scores = (
        jnp.einsum("qhd,khd->hqk", query, key_block, preferred_element_type=jnp.float32)
        * score_scale
    )
    scores = jnp.where(mask, scores, -jnp.inf)
    row_max = jnp.max(scores, -1, keepdims=True)
    expo = jnp.where(mask, jnp.exp(scores - row_max), 0.0)
    denominator = jnp.sum(expo, -1, keepdims=True)
    probability = expo / denominator
    prob_b = probability.astype(jnp.bfloat16)
    attended = jnp.einsum("hqk,khd->qhd", prob_b, value_block, preferred_element_type=jnp.float32)
    d_out = (attended - t_line.astype(jnp.float32)).astype(jnp.bfloat16)
    delta_sum = jnp.sum(d_out.astype(jnp.float32) * attended, -1).T
    prob_grad = jnp.einsum("qhd,khd->hqk", d_out, value_block, preferred_element_type=jnp.float32)
    score_grad = (probability * (prob_grad - delta_sum[:, :, None]) * score_scale).astype(
        jnp.bfloat16
    )
    dq_line = jnp.einsum("hqk,khd->qhd", score_grad, key_block, preferred_element_type=jnp.float32)
    log_total = row_max[..., 0] + jnp.log(denominator[..., 0])
    return (dq_line.reshape(width, heads_dev * HD), d_out, log_total, delta_sum, prob_b, score_grad)


def per_device(q_pre, k_pre, values, target, gain_q, gain_k, kept):
    frames, rows, width, feat_dev = q_pre.shape
    heads_dev = feat_dev // HD
    tiles = width // TC
    features = HEADS * HD
    line_count = frames * rows
    col_tile = jnp.arange(width) // TC
    q_float = q_pre.astype(jnp.float32)
    k_float = k_pre.astype(jnp.float32)
    square_q, square_k = lax.psum(
        (jnp.sum(q_float * q_float, -1), jnp.sum(k_float * k_float, -1)), "head"
    )
    scale_q = lax.rsqrt(square_q[..., None] / features + norm_eps)
    scale_k = lax.rsqrt(square_k[..., None] / features + norm_eps)
    q_norm = (q_float * scale_q * gain_q).astype(jnp.bfloat16)
    k_norm = (k_float * scale_k * gain_k).astype(jnp.bfloat16)
    kv_ext = padded(jnp.stack([k_norm, values]), (("frame", 1), ("row", 2)), 1)
    frame_at = lax.axis_index("frame")
    row_at = lax.axis_index("row")
    zero = jnp.int32(0)
    kept_pad = jnp.pad(kept, ((1, 1), (1, 1), (0, 0)))
    kept_ext = lax.dynamic_slice(
        kept_pad, (frame_at * frames, row_at * rows, zero), (frames + 2, rows + 2, tiles)
    )
    line_ids = jnp.arange(line_count, dtype=jnp.int32)
    q_lines = q_norm.reshape(line_count, width, heads_dev, HD)
    t_lines = target.reshape(line_count, width, heads_dev, HD)

    def query_window(line):
        f_at = line // rows
        r_at = line % rows
        kv_win = lax.dynamic_slice(
            kv_ext, (zero, f_at, r_at, zero, zero), (2, 3, 3, width, feat_dev)
        )
        kept_win = lax.dynamic_slice(kept_ext, (f_at, r_at, zero), (3, 3, tiles))
        return (f_at, r_at, kv_win, query_mask(kept_win, col_tile, tiles))

    def returned_step(totals, inputs):
        line, query, t_line = inputs
        f_at, r_at, kv_win, allowed = query_window(line)
        dq_line, d_out, log_total, delta_sum, prob_b, score_grad = attend_line(
            query, kv_win, t_line, allowed
        )
        key_grad = jnp.einsum("hqk,qhd->khd", score_grad, query, preferred_element_type=jnp.float32)
        value_grad = jnp.einsum("hqk,qhd->khd", prob_b, d_out, preferred_element_type=jnp.float32)
        both = jnp.stack(
            [key_grad.reshape(3, 3, width, feat_dev), value_grad.reshape(3, 3, width, feat_dev)]
        )
        start = (zero, f_at, r_at, zero, zero)
        current = lax.dynamic_slice(totals, start, (2, 3, 3, width, feat_dev))
        totals = lax.dynamic_update_slice(totals, current + both, start)
        return (totals, dq_line)

    empty = jnp.zeros((2, frames + 2, rows + 2, width, feat_dev), jnp.float32)
    totals, dq_lines = lax.scan(returned_step, empty, (line_ids, q_lines, t_lines))
    inner = totals[:, :, 1 : rows + 1]
    row_edges = (totals[:, :, 0:1], totals[:, :, rows + 1 : rows + 2])
    row_moved = [
        from_behind(row_edges[side], "row", by_value) for side, by_value in ((0, -1), (1, 1))
    ]
    inner = inner.at[:, :, rows - 1 : rows].add(row_moved[0])
    inner = inner.at[:, :, 0:1].add(row_moved[1])
    middle = inner[:, 1 : frames + 1]
    frame_edges = (inner[:, 0:1], inner[:, frames + 1 : frames + 2])
    frame_moved = [
        from_behind(frame_edges[side], "frame", by_value) for side, by_value in ((0, -1), (1, 1))
    ]
    middle = middle.at[:, frames - 1 : frames].add(frame_moved[0])
    middle = middle.at[:, 0:1].add(frame_moved[1])
    dk_norm = middle[0]
    value_total = middle[1]
    dq_norm = dq_lines.reshape(frames, rows, width, feat_dev)
    gated_q = gain_q * dq_norm
    gated_k = gain_k * dk_norm
    sum_q, sum_k = lax.psum(
        (jnp.sum(q_float * gated_q, -1), jnp.sum(k_float * gated_k, -1)), "head"
    )
    grad_q = (scale_q * gated_q - q_float * scale_q**3 * sum_q[..., None] / features).astype(
        jnp.bfloat16
    )
    grad_k = (scale_k * gated_k - k_float * scale_k**3 * sum_k[..., None] / features).astype(
        jnp.bfloat16
    )
    return (grad_q, grad_k, value_total.astype(jnp.bfloat16))


SWAP = [(0, 1), (1, 0)]
F32 = jnp.float32
BF16 = jnp.bfloat16
VMEM_LIMIT = 48 * 1024 * 1024


def call(body, out_shape, flops=10**6, moved=10**6, **kw):
    return pl.pallas_call(
        body,
        out_shape=out_shape,
        compiler_params=pltpu.CompilerParams(vmem_limit_bytes=VMEM_LIMIT),
        cost_estimate=pl.CostEstimate(flops=flops, bytes_accessed=moved, transcendentals=0),
        **kw,
    )


def halves(half):
    frame_at = lax.axis_index("frame")
    mine = pl.multiple_of(frame_at * half, HD)
    theirs = pl.multiple_of((1 - frame_at) * half, HD)
    return (pl.ds(mine, half), pl.ds(theirs, half))


def sides(width):
    odd = lax.rem(lax.axis_index("row"), 2)
    near = pl.multiple_of((1 - odd) * width, width)
    far = pl.multiple_of(odd * width, width)
    return (pl.ds(near, width), pl.ds(far, width))


def load_kernel(
    q_in,
    k_in,
    v_in,
    t_in,
    gain_q_in,
    gain_k_in,
    q_ref,
    k_ref,
    v_ref,
    t_ref,
    gain_q_ref,
    gain_k_ref,
    sums_ref,
    v_out_ref,
    sems,
):
    tokens, feat_dev = q_ref.shape
    _, theirs = halves(feat_dev // 2)
    pairs = (
        (q_in, q_ref),
        (k_in, k_ref),
        (v_in, v_ref),
        (t_in, t_ref),
        (gain_q_in, gain_q_ref.at[0]),
        (gain_k_in, gain_k_ref.at[0]),
    )
    copies = [pltpu.make_async_copy(a, b, sems.at[i]) for i, (a, b) in enumerate(pairs)]
    for copy in copies:
        copy.start()
    copies[0].wait()
    q_float = q_ref[...].astype(F32)
    sums_ref[:tokens] = jnp.sum(q_float * q_float, -1, keepdims=True)
    copies[1].wait()
    k_float = k_ref[...].astype(F32)
    sums_ref[tokens:] = jnp.sum(k_float * k_float, -1, keepdims=True)
    copies[2].wait()
    v_out_ref[...] = v_ref[:, theirs]
    for copy in copies[3:]:
        copy.wait()


def norm_kernel(
    width,
    q_ref,
    k_ref,
    v_ref,
    t_ref,
    sums_ref,
    peer_ref,
    gain_q_ref,
    gain_k_ref,
    scale_ref,
    own_ref,
    k_out_ref,
    qt_out_ref,
    near_ref,
    far_ref,
):
    tokens, feat_dev = q_ref.shape
    features = HEADS * HD
    mine, theirs = halves(feat_dev // 2)
    near, far = sides(width)
    scale = lax.rsqrt((sums_ref[...] + peer_ref[...]) / features + norm_eps)
    scale_ref[...] = scale
    scale_q, scale_k = (scale[:tokens], scale[tokens:])

    def normed(ref, part, scales, gain_ref):
        return (ref[:, part].astype(F32) * scales * gain_ref[:, part]).astype(BF16)

    k_out_ref[...] = normed(k_ref, theirs, scale_k, gain_k_ref)
    qt_out_ref[:tokens] = normed(q_ref, theirs, scale_q, gain_q_ref)
    qt_out_ref[tokens:] = t_ref[:, theirs]
    own_ref[:tokens] = normed(k_ref, mine, scale_k, gain_k_ref)
    own_ref[tokens:] = normed(q_ref, mine, scale_q, gain_q_ref)
    for out_ref, rows in ((near_ref, near), (far_ref, far)):
        out_ref[:width] = own_ref[rows]
        out_ref[width:] = v_ref[rows, mine]


def relay_kernel(width, k_ref, v_ref, earlier_ref, near_ref, far_ref):
    for out_ref, rows in zip((near_ref, far_ref), sides(width)):
        out_ref[:width] = k_ref[rows]
        out_ref[width:] = v_ref[rows]


def mask_kernel(width, kept_ref, near_ref, far_ref):
    rows = 2
    count = kept_ref.shape[2]
    tiles = width // TC
    frame_at = lax.axis_index("frame")
    first_row = lax.axis_index("row") * rows
    odd = lax.rem(lax.axis_index("row"), 2)
    shape = near_ref.shape
    key_at = lax.broadcasted_iota(jnp.int32, shape, 1)
    query_at = lax.broadcasted_iota(jnp.int32, shape, 0)
    key_tile = lax.rem(key_at, width) // TC
    query_tile = lax.rem(query_at, width) // TC
    near_cols = jnp.abs(query_tile - key_tile) <= 1
    same = (query_tile == key_tile) & (key_at // width == 3 * (query_at // width) + 1)
    lane = lax.broadcasted_iota(jnp.int32, (1, shape[1]), 1) // TC
    for out_ref, row in ((near_ref, 1 - odd), (far_ref, odd)):
        places = (3 * row - 1, row, 1 - row)
        key_kept = jnp.zeros((1, shape[1]), jnp.int32)
        for part in range(2):
            frame = frame_at if part == 0 else 1 - frame_at
            for slot, place in enumerate(places):
                at = first_row + place
                inside = (at >= 0) & (at < count)
                at = jnp.clip(at, 0, count - 1)
                for tile in range(tiles):
                    value = jnp.where(inside, kept_ref[frame, tile, at], 0)
                    here = (part * 3 + slot) * tiles + tile
                    key_kept = jnp.where(lane == here, value, key_kept)
        allowed = near_cols & (same | (key_kept > 0))
        out_ref[...] = jnp.where(allowed, 0.0, -1e30)


def attend(width, row, halo_ref, swap_halo_ref, own_ref, v_ref, t_ref, swap_k_ref, swap_v_ref,
           swap_qt_ref, bias_ref, store):
    tokens, half = swap_k_ref.shape
    score_scale = HD ** (-0.5)
    mine = lax.axis_index("frame") * half
    bias = bias_ref[...]
    own_at = pl.multiple_of(row * width, width)
    other_at = pl.multiple_of((1 - row) * width, width)
    rows = (pl.ds(own_at, width), pl.ds(other_at, width))
    query_at = pl.ds(pl.multiple_of(tokens + own_at, width), width)

    def product(a, b, a_dim, b_dim):
        return lax.dot_general(a, b, (((a_dim,), (b_dim,)), ((), ())), preferred_element_type=F32)

    for head in range(half // HD):
        at = slice(head * HD, (head + 1) * HD)
        mine_at = pl.ds(pl.multiple_of(mine + head * HD, HD), HD)
        query = jnp.concatenate([own_ref[query_at, at], swap_qt_ref[rows[0], at]], 0)
        target = jnp.concatenate([t_ref[rows[0], mine_at], swap_qt_ref[query_at, at]], 0)
        key = jnp.concatenate(
            [halo_ref[:width, at]]
            + [own_ref[r, at] for r in rows]
            + [swap_halo_ref[:width, at]]
            + [swap_k_ref[r, at] for r in rows],
            0,
        )
        value = jnp.concatenate(
            [halo_ref[width:, at]]
            + [v_ref[r, mine_at] for r in rows]
            + [swap_halo_ref[width:, at]]
            + [swap_v_ref[r, at] for r in rows],
            0,
        )
        scores = product(query, key, 1, 1) * score_scale + bias
        row_max = jnp.max(scores, -1, keepdims=True)
        expo = jnp.exp(scores - row_max)
        probability = expo * (1.0 / jnp.sum(expo, -1, keepdims=True))
        prob_b = probability.astype(BF16)
        attended = product(prob_b, value, 1, 0)
        d_out = (attended - target.astype(F32)).astype(BF16)
        delta_sum = jnp.sum(d_out.astype(F32) * attended, -1, keepdims=True)
        prob_grad = product(d_out, value, 1, 1)
        score_grad = (probability * (prob_grad - delta_sum) * score_scale).astype(BF16)
        dq = product(score_grad, key, 1, 0)
        dk = product(score_grad, query, 0, 0)
        dv = product(prob_b, d_out, 0, 0)
        store(at, dq, dk, dv)


def attend_near_kernel(
    width,
    halo_ref,
    swap_halo_ref,
    own_ref,
    v_ref,
    t_ref,
    swap_k_ref,
    swap_v_ref,
    swap_qt_ref,
    bias_ref,
    earlier_ref,
    halo_grad_ref,
    swap_halo_grad_ref,
    grad_ref,
):
    def store(at, dq, dk, dv):
        for place, grad in ((0, dk), (1, dv)):
            to = slice(place * width, (place + 1) * width)
            halo_grad_ref[to, at] = grad[:width].astype(BF16)
            swap_halo_grad_ref[to, at] = grad[3 * width : 4 * width].astype(BF16)
            for part in range(2):
                start = (5 * part + 1 + 2 * place) * width
                first = (3 * part + 1) * width
                grad_ref[start : start + 2 * width, at] = grad[first : first + 2 * width]
        for part in range(2):
            start = 5 * part * width
            grad_ref[start : start + width, at] = dq[part * width : (part + 1) * width]

    row = 1 - lax.rem(lax.axis_index("row"), 2)
    attend(width, row, halo_ref, swap_halo_ref, own_ref, v_ref, t_ref, swap_k_ref, swap_v_ref,
           swap_qt_ref, bias_ref, store)


def attend_far_kernel(
    width,
    halo_ref,
    swap_halo_ref,
    own_ref,
    v_ref,
    t_ref,
    swap_k_ref,
    swap_v_ref,
    swap_qt_ref,
    bias_ref,
    grad_ref,
    halo_grad_ref,
    swap_halo_grad_ref,
    total_ref,
    swap_first_ref,
    swap_last_ref,
):
    def block(ref, index, at):
        return ref[index * width : (index + 1) * width, at]

    def put(ref, index, at, value):
        ref[index * width : (index + 1) * width, at] = value.astype(ref.dtype)

    def store(at, dq, dk, dv):
        put(total_ref, 0, at, block(grad_ref, 0, at))
        put(total_ref, 1, at, dq[:width])
        put(swap_first_ref, 0, at, block(grad_ref, 5, at))
        put(swap_first_ref, 1, at, dq[width:])
        for place, grad in ((0, dk), (1, dv)):
            parts = [grad[i * width : (i + 1) * width] for i in range(6)]
            put(halo_grad_ref, place, at, parts[0])
            put(swap_halo_grad_ref, place, at, parts[3])
            put(total_ref, 2 + 2 * place, at, parts[2] + block(grad_ref, 1 + 2 * place, at))
            put(total_ref, 3 + 2 * place, at, parts[1] + block(grad_ref, 2 + 2 * place, at))
            put(swap_first_ref, 2 + place, at, parts[5] + block(grad_ref, 6 + 2 * place, at))
            put(swap_last_ref, place, at, parts[4] + block(grad_ref, 7 + 2 * place, at))

    row = lax.rem(lax.axis_index("row"), 2)
    attend(width, row, halo_ref, swap_halo_ref, own_ref, v_ref, t_ref, swap_k_ref, swap_v_ref,
           swap_qt_ref, bias_ref, store)


def near_kernel(width, own_ref, near_ref, swap_near_ref, out_ref, swap_out_ref):
    for place in range(2):
        rows = slice(place * width, (place + 1) * width)
        at = 2 + 2 * place
        own = own_ref[at * width : (at + 1) * width]
        out_ref[rows] = own + near_ref[rows].astype(F32)
    swap_out_ref[...] = swap_near_ref[...].astype(F32)


def add_kernel(a_ref, b_ref, earlier_ref, out_ref):
    out_ref[...] = (a_ref[...] + b_ref[...].astype(F32)).astype(BF16)


def gather_kernel(
    width,
    q_ref,
    k_ref,
    gain_q_ref,
    gain_k_ref,
    own_ref,
    near_ref,
    far_ref,
    swap_first_ref,
    swap_near_ref,
    swap_last_ref,
    gated_q_ref,
    gated_k_ref,
    grad_v_ref,
    sums_ref,
):
    tokens, feat_dev = q_ref.shape
    mine, theirs = halves(feat_dev // 2)
    near, far = sides(width)

    def term(ref, index):
        return ref[index * width : (index + 1) * width].astype(F32)

    for index, rows in enumerate((near, far)):
        gated_q_ref[rows, mine] = gain_q_ref[:, mine] * term(own_ref, index)
        gated_q_ref[rows, theirs] = gain_q_ref[:, theirs] * term(swap_first_ref, index)
    gated_k_ref[near, mine] = gain_k_ref[:, mine] * term(near_ref, 0)
    gated_k_ref[far, mine] = gain_k_ref[:, mine] * (term(own_ref, 3) + term(far_ref, 0))
    grad_v_ref[near, mine] = term(near_ref, 1).astype(BF16)
    grad_v_ref[far, mine] = (term(own_ref, 5) + term(far_ref, 1)).astype(BF16)
    near_dk = term(swap_first_ref, 2) + term(swap_near_ref, 0)
    near_dv = term(swap_first_ref, 3) + term(swap_near_ref, 1)
    gated_k_ref[near, theirs] = gain_k_ref[:, theirs] * near_dk
    gated_k_ref[far, theirs] = gain_k_ref[:, theirs] * term(swap_last_ref, 0)
    grad_v_ref[near, theirs] = near_dv.astype(BF16)
    grad_v_ref[far, theirs] = swap_last_ref[width:]
    sums_ref[:tokens] = jnp.sum(q_ref[...].astype(F32) * gated_q_ref[...], -1, keepdims=True)
    sums_ref[tokens:] = jnp.sum(k_ref[...].astype(F32) * gated_k_ref[...], -1, keepdims=True)


def finish_kernel(
    q_ref, k_ref, gated_q_ref, gated_k_ref, scale_ref, sums_ref, peer_ref, grad_q_ref, grad_k_ref
):
    tokens = q_ref.shape[0]
    features = HEADS * HD
    scale = scale_ref[...]
    slope = scale * scale * scale * (sums_ref[...] + peer_ref[...]) / features
    for rows, pre_ref, gated_ref, out_ref in (
        (slice(0, tokens), q_ref, gated_q_ref, grad_q_ref),
        (slice(tokens, 2 * tokens), k_ref, gated_k_ref, grad_k_ref),
    ):
        out_ref[...] = (
            scale[rows] * gated_ref[...] - pre_ref[...].astype(F32) * slope[rows]
        ).astype(BF16)


def swapped_device(q_pre, k_pre, values, target, gain_q, gain_k, kept):
    frames, rows, width, feat_dev = q_pre.shape
    tokens = rows * width
    half = feat_dev // 2
    row_blocks = lax.axis_size("row")
    inputs = [array.reshape(tokens, feat_dev) for array in (q_pre, k_pre, values, target)]
    inputs += [gain_q, gain_k]
    inputs = [pltpu.with_memory_space_constraint(array, pltpu.HBM) for array in inputs]
    near_pairs = [(r, r + 1) for r in range(0, row_blocks - 1, 2)]
    far_pairs = [(r, r + 1) for r in range(1, row_blocks - 1, 2)]
    near, far = (pairs + [(b, a) for a, b in pairs] for pairs in (near_pairs, far_pairs))
    swap_near = [
        (f * row_blocks + a, (1 - f) * row_blocks + b) for f in range(2) for a, b in near
    ]

    def shape(first, last, dtype=BF16):
        return jax.ShapeDtypeStruct((first, last), dtype)

    block = shape(tokens, feat_dev)
    sum_pair = shape(2 * tokens, 1, F32)
    tokens_half = shape(tokens, half)
    gain = shape(1, feat_dev, F32)
    edge = shape(2 * width, half)
    bias = shape(2 * width, 6 * width, F32)

    q_all, k_all, v_all, t_all, gain_q, gain_k, sums, v_out = call(
        load_kernel,
        (block,) * 4 + (gain,) * 2 + (sum_pair, tokens_half),
        in_specs=[pl.BlockSpec(memory_space=pltpu.HBM)] * 6,
        scratch_shapes=[pltpu.SemaphoreType.DMA((6,))],
    )(*inputs)
    swap_v = lax.ppermute(v_out, "frame", SWAP)
    peer = lax.ppermute(sums, "head", SWAP)
    scale, own_kq, k_out, qt_out, near_out, far_out = call(
        functools.partial(norm_kernel, width),
        (sum_pair, shape(2 * tokens, half), tokens_half, shape(2 * tokens, half), edge, edge),
    )(q_all, k_all, v_all, t_all, sums, peer, gain_q, gain_k)
    near_in = lax.ppermute(near_out, "row", near)
    swap_k = lax.ppermute(k_out, "frame", SWAP)
    swap_qt = lax.ppermute(qt_out, "frame", SWAP)
    far_in = lax.ppermute(far_out, "row", far)
    relay_near, relay_far = call(functools.partial(relay_kernel, width), (edge, edge))(
        swap_k, swap_v, near_in
    )
    swap_near_in = lax.ppermute(relay_near, "row", near)
    swap_far_in = lax.ppermute(relay_far, "row", far)
    near_bias, far_bias = call(
        functools.partial(mask_kernel, width),
        (bias, bias),
        in_specs=[pl.BlockSpec(memory_space=pltpu.SMEM)],
    )(kept.transpose(0, 2, 1))
    shared = (own_kq, v_all, t_all, swap_k, swap_v, swap_qt)
    near_out, swap_near_out, near_terms = call(
        functools.partial(attend_near_kernel, width),
        (edge, edge, shape(10 * width, half, F32)),
        flops=5 * 10**8,
        moved=2 * 10**6,
    )(near_in, swap_near_in, *shared, near_bias, far_in)
    near_total = lax.ppermute(near_out, "row", near)
    swap_near_total = lax.ppermute(swap_near_out, ("frame", "row"), swap_near)
    far_out, swap_far_out, own_total, first_out, last_terms = call(
        functools.partial(attend_far_kernel, width),
        (edge, edge, shape(3 * tokens, half, F32), shape(4 * width, half))
        + (shape(2 * width, half, F32),),
        flops=5 * 10**8,
        moved=2 * 10**6,
    )(far_in, swap_far_in, *shared, far_bias, near_terms)
    far_terms = lax.ppermute(swap_far_out, "row", far)
    swap_first = lax.ppermute(first_out, "frame", SWAP)
    far_total = lax.ppermute(far_out, "row", far)
    near_total, swap_near_total = call(
        functools.partial(near_kernel, width), (shape(2 * width, half, F32),) * 2
    )(own_total, near_total, swap_near_total)
    last_out = call(add_kernel, edge)(last_terms, far_terms, near_total)
    swap_last = lax.ppermute(last_out, "frame", SWAP)
    gated_q, gated_k, grad_v, sum_terms = call(
        functools.partial(gather_kernel, width),
        (shape(tokens, feat_dev, F32),) * 2 + (block, sum_pair),
    )(
        q_all,
        k_all,
        gain_q,
        gain_k,
        own_total,
        near_total,
        far_total,
        swap_first,
        swap_near_total,
        swap_last,
    )
    sum_peer = lax.ppermute(sum_terms, "head", SWAP)
    grad_q, grad_k = call(finish_kernel, (block, block))(
        q_all, k_all, gated_q, gated_k, scale, sum_terms, sum_peer
    )
    return tuple(
        array.reshape(frames, rows, width, feat_dev) for array in (grad_q, grad_k, grad_v)
    )


def on_device(q_pre, *rest):
    frames, rows, _, feat_dev = q_pre.shape
    paired = lax.axis_size("frame") == 2 and frames == 1 and rows == 2
    if paired and feat_dev % (2 * HD) == 0:
        return swapped_device(q_pre, *rest)
    return per_device(q_pre, *rest)


def solution(mesh):
    return jax.shard_map(
        on_device,
        mesh=mesh,
        in_specs=(
            P("frame", "row", None, "head"),
            P("frame", "row", None, "head"),
            P("frame", "row", None, "head"),
            P("frame", "row", None, "head"),
            P("head"),
            P("head"),
            P(),
        ),
        out_specs=(
            P("frame", "row", None, "head"),
            P("frame", "row", None, "head"),
            P("frame", "row", None, "head"),
        ),
        check_vma=False,
    )
```

```python
import functools

import jax
import jax.numpy as jnp
from jax import lax
from jax.experimental import pallas as pl
from jax.experimental.pallas import tpu as pltpu
from jax.sharding import PartitionSpec as P

TC = 16
HEADS = 20
HD = 128


norm_eps = 1e-06


def padded(x, sides, width):
    for axis, dim in sides:
        size, length = (lax.axis_size(axis), x.shape[dim])
        up = [(i, (i + 1) % size) for i in range(size - 1)]
        down = [(j, i) for i, j in up]
        last = lax.slice_in_dim(x, length - width, length, axis=dim)
        first = lax.slice_in_dim(x, 0, width, axis=dim)
        before = lax.ppermute(last, axis, up)
        after = lax.ppermute(first, axis, down)
        x = jnp.concatenate([before, x, after], axis=dim)
    return x


def from_behind(value, axis, steps):
    count = lax.axis_size(axis)
    first, last = (max(0, -steps), min(count, count - steps))
    return lax.ppermute(value, axis, [(source, source + steps) for source in range(first, last)])


def query_mask(kept_win, col_tile, tiles):
    near_cols = jnp.abs(col_tile[:, None] - col_tile[None, :]) <= 1
    same_tile = col_tile[:, None] == col_tile[None, :]
    one_hot = col_tile[:, None] == jnp.arange(tiles)[None, :]
    key_kept = jnp.any(one_hot[None, None] & (kept_win[:, :, None, :] > 0), axis=-1)
    centre = (jnp.arange(3)[:, None] == 1) & (jnp.arange(3)[None, :] == 1)
    allowed = near_cols[:, None, None, :] & (
        key_kept[None] | centre[None, :, :, None] & same_tile[:, None, None, :]
    )
    return allowed.reshape(col_tile.shape[0], -1)


def attend_line(query, kv_win, t_line, allowed):
    width, heads_dev, _ = query.shape
    score_scale = HD ** (-0.5)
    key_block = kv_win[0].reshape(9 * width, heads_dev, HD)
    value_block = kv_win[1].reshape(9 * width, heads_dev, HD)
    mask = allowed[None]
    scores = (
        jnp.einsum("qhd,khd->hqk", query, key_block, preferred_element_type=jnp.float32)
        * score_scale
    )
    scores = jnp.where(mask, scores, -jnp.inf)
    row_max = jnp.max(scores, -1, keepdims=True)
    expo = jnp.where(mask, jnp.exp(scores - row_max), 0.0)
    denominator = jnp.sum(expo, -1, keepdims=True)
    probability = expo / denominator
    prob_b = probability.astype(jnp.bfloat16)
    attended = jnp.einsum("hqk,khd->qhd", prob_b, value_block, preferred_element_type=jnp.float32)
    d_out = (attended - t_line.astype(jnp.float32)).astype(jnp.bfloat16)
    delta_sum = jnp.sum(d_out.astype(jnp.float32) * attended, -1).T
    prob_grad = jnp.einsum("qhd,khd->hqk", d_out, value_block, preferred_element_type=jnp.float32)
    score_grad = (probability * (prob_grad - delta_sum[:, :, None]) * score_scale).astype(
        jnp.bfloat16
    )
    dq_line = jnp.einsum("hqk,khd->qhd", score_grad, key_block, preferred_element_type=jnp.float32)
    log_total = row_max[..., 0] + jnp.log(denominator[..., 0])
    return (dq_line.reshape(width, heads_dev * HD), d_out, log_total, delta_sum, prob_b, score_grad)


def per_device(q_pre, k_pre, values, target, gain_q, gain_k, kept):
    frames, rows, width, feat_dev = q_pre.shape
    heads_dev = feat_dev // HD
    tiles = width // TC
    features = HEADS * HD
    line_count = frames * rows
    col_tile = jnp.arange(width) // TC
    q_float = q_pre.astype(jnp.float32)
    k_float = k_pre.astype(jnp.float32)
    square_q, square_k = lax.psum(
        (jnp.sum(q_float * q_float, -1), jnp.sum(k_float * k_float, -1)), "head"
    )
    scale_q = lax.rsqrt(square_q[..., None] / features + norm_eps)
    scale_k = lax.rsqrt(square_k[..., None] / features + norm_eps)
    q_norm = (q_float * scale_q * gain_q).astype(jnp.bfloat16)
    k_norm = (k_float * scale_k * gain_k).astype(jnp.bfloat16)
    kv_ext = padded(jnp.stack([k_norm, values]), (("frame", 1), ("row", 2)), 1)
    frame_at = lax.axis_index("frame")
    row_at = lax.axis_index("row")
    zero = jnp.int32(0)
    kept_pad = jnp.pad(kept, ((1, 1), (1, 1), (0, 0)))
    kept_ext = lax.dynamic_slice(
        kept_pad, (frame_at * frames, row_at * rows, zero), (frames + 2, rows + 2, tiles)
    )
    line_ids = jnp.arange(line_count, dtype=jnp.int32)
    q_lines = q_norm.reshape(line_count, width, heads_dev, HD)
    t_lines = target.reshape(line_count, width, heads_dev, HD)

    def query_window(line):
        f_at = line // rows
        r_at = line % rows
        kv_win = lax.dynamic_slice(
            kv_ext, (zero, f_at, r_at, zero, zero), (2, 3, 3, width, feat_dev)
        )
        kept_win = lax.dynamic_slice(kept_ext, (f_at, r_at, zero), (3, 3, tiles))
        return (f_at, r_at, kv_win, query_mask(kept_win, col_tile, tiles))

    def returned_step(totals, inputs):
        line, query, t_line = inputs
        f_at, r_at, kv_win, allowed = query_window(line)
        dq_line, d_out, log_total, delta_sum, prob_b, score_grad = attend_line(
            query, kv_win, t_line, allowed
        )
        key_grad = jnp.einsum("hqk,qhd->khd", score_grad, query, preferred_element_type=jnp.float32)
        value_grad = jnp.einsum("hqk,qhd->khd", prob_b, d_out, preferred_element_type=jnp.float32)
        both = jnp.stack(
            [key_grad.reshape(3, 3, width, feat_dev), value_grad.reshape(3, 3, width, feat_dev)]
        )
        start = (zero, f_at, r_at, zero, zero)
        current = lax.dynamic_slice(totals, start, (2, 3, 3, width, feat_dev))
        totals = lax.dynamic_update_slice(totals, current + both, start)
        return (totals, dq_line)

    empty = jnp.zeros((2, frames + 2, rows + 2, width, feat_dev), jnp.float32)
    totals, dq_lines = lax.scan(returned_step, empty, (line_ids, q_lines, t_lines))
    inner = totals[:, :, 1 : rows + 1]
    row_edges = (totals[:, :, 0:1], totals[:, :, rows + 1 : rows + 2])
    row_moved = [
        from_behind(row_edges[side], "row", by_value) for side, by_value in ((0, -1), (1, 1))
    ]
    inner = inner.at[:, :, rows - 1 : rows].add(row_moved[0])
    inner = inner.at[:, :, 0:1].add(row_moved[1])
    middle = inner[:, 1 : frames + 1]
    frame_edges = (inner[:, 0:1], inner[:, frames + 1 : frames + 2])
    frame_moved = [
        from_behind(frame_edges[side], "frame", by_value) for side, by_value in ((0, -1), (1, 1))
    ]
    middle = middle.at[:, frames - 1 : frames].add(frame_moved[0])
    middle = middle.at[:, 0:1].add(frame_moved[1])
    dk_norm = middle[0]
    value_total = middle[1]
    dq_norm = dq_lines.reshape(frames, rows, width, feat_dev)
    gated_q = gain_q * dq_norm
    gated_k = gain_k * dk_norm
    sum_q, sum_k = lax.psum(
        (jnp.sum(q_float * gated_q, -1), jnp.sum(k_float * gated_k, -1)), "head"
    )
    grad_q = (scale_q * gated_q - q_float * scale_q**3 * sum_q[..., None] / features).astype(
        jnp.bfloat16
    )
    grad_k = (scale_k * gated_k - k_float * scale_k**3 * sum_k[..., None] / features).astype(
        jnp.bfloat16
    )
    return (grad_q, grad_k, value_total.astype(jnp.bfloat16))


SWAP = [(0, 1), (1, 0)]
F32 = jnp.float32
BF16 = jnp.bfloat16
VMEM_LIMIT = 48 * 1024 * 1024


def call(body, out_shape, flops=10**6, moved=10**6, **kw):
    return pl.pallas_call(
        body,
        out_shape=out_shape,
        compiler_params=pltpu.CompilerParams(vmem_limit_bytes=VMEM_LIMIT),
        cost_estimate=pl.CostEstimate(flops=flops, bytes_accessed=moved, transcendentals=0),
        **kw,
    )


def halves(half):
    frame_at = lax.axis_index("frame")
    mine = pl.multiple_of(frame_at * half, HD)
    theirs = pl.multiple_of((1 - frame_at) * half, HD)
    return (pl.ds(mine, half), pl.ds(theirs, half))


def sides(width):
    odd = lax.rem(lax.axis_index("row"), 2)
    near = pl.multiple_of((1 - odd) * width, width)
    far = pl.multiple_of(odd * width, width)
    return (pl.ds(near, width), pl.ds(far, width))


def load_kernel(
    q_in,
    k_in,
    v_in,
    t_in,
    gain_q_in,
    gain_k_in,
    q_ref,
    k_ref,
    v_ref,
    t_ref,
    gain_q_ref,
    gain_k_ref,
    sums_ref,
    v_out_ref,
    sems,
):
    tokens, feat_dev = q_ref.shape
    _, theirs = halves(feat_dev // 2)
    pairs = (
        (q_in, q_ref),
        (k_in, k_ref),
        (v_in, v_ref),
        (t_in, t_ref),
        (gain_q_in, gain_q_ref.at[0]),
        (gain_k_in, gain_k_ref.at[0]),
    )
    copies = [pltpu.make_async_copy(a, b, sems.at[i]) for i, (a, b) in enumerate(pairs)]
    for copy in copies:
        copy.start()
    copies[0].wait()
    q_float = q_ref[...].astype(F32)
    sums_ref[:tokens] = jnp.sum(q_float * q_float, -1, keepdims=True)
    copies[1].wait()
    k_float = k_ref[...].astype(F32)
    sums_ref[tokens:] = jnp.sum(k_float * k_float, -1, keepdims=True)
    copies[2].wait()
    v_out_ref[...] = v_ref[:, theirs]
    for copy in copies[3:]:
        copy.wait()


def norm_kernel(
    width,
    q_ref,
    k_ref,
    v_ref,
    t_ref,
    sums_ref,
    peer_ref,
    gain_q_ref,
    gain_k_ref,
    scale_ref,
    own_ref,
    k_out_ref,
    qt_out_ref,
    near_ref,
    far_ref,
):
    tokens, feat_dev = q_ref.shape
    features = HEADS * HD
    mine, theirs = halves(feat_dev // 2)
    near, far = sides(width)
    scale = lax.rsqrt((sums_ref[...] + peer_ref[...]) / features + norm_eps)
    scale_ref[...] = scale
    scale_q, scale_k = (scale[:tokens], scale[tokens:])

    def normed(ref, part, scales, gain_ref):
        return (ref[:, part].astype(F32) * scales * gain_ref[:, part]).astype(BF16)

    k_out_ref[...] = normed(k_ref, theirs, scale_k, gain_k_ref)
    qt_out_ref[:tokens] = normed(q_ref, theirs, scale_q, gain_q_ref)
    qt_out_ref[tokens:] = t_ref[:, theirs]
    own_ref[:tokens] = normed(k_ref, mine, scale_k, gain_k_ref)
    own_ref[tokens:] = normed(q_ref, mine, scale_q, gain_q_ref)
    for out_ref, rows in ((near_ref, near), (far_ref, far)):
        out_ref[:width] = own_ref[rows]
        out_ref[width:] = v_ref[rows, mine]


def relay_kernel(width, k_ref, v_ref, earlier_ref, near_ref, far_ref):
    for out_ref, rows in zip((near_ref, far_ref), sides(width)):
        out_ref[:width] = k_ref[rows]
        out_ref[width:] = v_ref[rows]


def mask_kernel(width, kept_ref, near_ref, far_ref):
    rows = 2
    count = kept_ref.shape[2]
    tiles = width // TC
    frame_at = lax.axis_index("frame")
    first_row = lax.axis_index("row") * rows
    odd = lax.rem(lax.axis_index("row"), 2)
    query_at = lax.broadcasted_iota(jnp.int32, (TC, near_ref.shape[1]), 1)
    query_tile = lax.rem(query_at, width) // TC
    for out_ref, row in ((near_ref, 1 - odd), (far_ref, odd)):
        for part in range(2):
            frame = frame_at if part == 0 else 1 - frame_at
            for slot, place in enumerate((3 * row - 1, row, 1 - row)):
                at = first_row + place
                inside = (at >= 0) & (at < count)
                at = jnp.clip(at, 0, count - 1)
                for tile in range(tiles):
                    value = jnp.where(inside, kept_ref[frame, tile, at], 0)
                    allowed = (jnp.abs(query_tile - tile) <= 1) & (value > 0)
                    if slot == 1:
                        allowed |= (query_tile == tile) & (query_at // width == part)
                    here = ((part * 3 + slot) * tiles + tile) * TC
                    out_ref[here : here + TC] = jnp.where(allowed, 0.0, -1e30)


def attend(width, row, halo_ref, swap_halo_ref, own_ref, v_ref, t_ref, swap_k_ref, swap_v_ref,
           swap_qt_ref, bias_ref, store):
    tokens, half = swap_k_ref.shape
    score_scale = HD ** (-0.5)
    mine = lax.axis_index("frame") * half
    bias = bias_ref[...]
    own_at = pl.multiple_of(row * width, width)
    other_at = pl.multiple_of((1 - row) * width, width)
    rows = (pl.ds(own_at, width), pl.ds(other_at, width))
    query_at = pl.ds(pl.multiple_of(tokens + own_at, width), width)

    def product(a, b, a_dim, b_dim):
        return lax.dot_general(a, b, (((a_dim,), (b_dim,)), ((), ())), preferred_element_type=F32)

    def load(head):
        at = slice(head * HD, (head + 1) * HD)
        mine_at = pl.ds(pl.multiple_of(mine + head * HD, HD), HD)
        query = jnp.concatenate([own_ref[query_at, at], swap_qt_ref[rows[0], at]], 0)
        target = jnp.concatenate([t_ref[rows[0], mine_at], swap_qt_ref[query_at, at]], 0)
        key = jnp.concatenate(
            [halo_ref[:width, at]]
            + [own_ref[r, at] for r in rows]
            + [swap_halo_ref[:width, at]]
            + [swap_k_ref[r, at] for r in rows],
            0,
        )
        value = jnp.concatenate(
            [halo_ref[width:, at]]
            + [v_ref[r, mine_at] for r in rows]
            + [swap_halo_ref[width:, at]]
            + [swap_v_ref[r, at] for r in rows],
            0,
        )
        return (query, target, key, value)

    def weights(query, key):
        scores = product(key, query, 1, 1) * score_scale + bias
        expo = jnp.exp(scores - jnp.max(scores, 0, keepdims=True))
        return expo * (1.0 / jnp.sum(expo, 0, keepdims=True))

    def output_grad(prob_b, target, value):
        attended = product(value, prob_b, 0, 0)
        d_out = (attended - target.astype(F32).T).astype(BF16)
        return (d_out, jnp.sum(d_out.astype(F32) * attended, 0, keepdims=True))

    def score_grads(probability, d_out, delta_sum, value):
        prob_grad = product(value, d_out, 1, 0)
        return (probability * (prob_grad - delta_sum) * score_scale).astype(BF16)

    def grads(score_grad, prob_b, d_out, query, key):
        dq = product(key, score_grad, 0, 0).T
        dk = product(score_grad, query, 1, 0)
        return (dq, dk, product(prob_b, d_out, 1, 1))

    heads = range(half // HD)
    loaded = [load(head) for head in heads]
    probability = [weights(query, key) for query, _, key, _ in loaded]
    prob_b = [p.astype(BF16) for p in probability]
    outs = [output_grad(p, t, v) for p, (_, t, _, v) in zip(prob_b, loaded)]
    score_grad = [score_grads(p, *o, x[3]) for p, o, x in zip(probability, outs, loaded)]
    for head in heads:
        query, _, key, _ = loaded[head]
        at = slice(head * HD, (head + 1) * HD)
        store(at, *grads(score_grad[head], prob_b[head], outs[head][0], query, key))


def attend_near_kernel(
    width,
    halo_ref,
    swap_halo_ref,
    own_ref,
    v_ref,
    t_ref,
    swap_k_ref,
    swap_v_ref,
    swap_qt_ref,
    bias_ref,
    earlier_ref,
    halo_grad_ref,
    swap_halo_grad_ref,
    grad_ref,
):
    def store(at, dq, dk, dv):
        for place, grad in ((0, dk), (1, dv)):
            to = slice(place * width, (place + 1) * width)
            halo_grad_ref[to, at] = grad[:width].astype(BF16)
            swap_halo_grad_ref[to, at] = grad[3 * width : 4 * width].astype(BF16)
            for part in range(2):
                start = (5 * part + 1 + 2 * place) * width
                first = (3 * part + 1) * width
                grad_ref[start : start + 2 * width, at] = grad[first : first + 2 * width]
        for part in range(2):
            start = 5 * part * width
            grad_ref[start : start + width, at] = dq[part * width : (part + 1) * width]

    row = 1 - lax.rem(lax.axis_index("row"), 2)
    attend(width, row, halo_ref, swap_halo_ref, own_ref, v_ref, t_ref, swap_k_ref, swap_v_ref,
           swap_qt_ref, bias_ref, store)


def attend_far_kernel(
    width,
    halo_ref,
    swap_halo_ref,
    own_ref,
    v_ref,
    t_ref,
    swap_k_ref,
    swap_v_ref,
    swap_qt_ref,
    bias_ref,
    grad_ref,
    halo_grad_ref,
    swap_halo_grad_ref,
    total_ref,
    swap_first_ref,
    swap_last_ref,
):
    def block(ref, index, at):
        return ref[index * width : (index + 1) * width, at]

    def put(ref, index, at, value):
        ref[index * width : (index + 1) * width, at] = value.astype(ref.dtype)

    def store(at, dq, dk, dv):
        put(total_ref, 0, at, block(grad_ref, 0, at))
        put(total_ref, 1, at, dq[:width])
        put(swap_first_ref, 0, at, block(grad_ref, 5, at))
        put(swap_first_ref, 1, at, dq[width:])
        for place, grad in ((0, dk), (1, dv)):
            parts = [grad[i * width : (i + 1) * width] for i in range(6)]
            put(halo_grad_ref, place, at, parts[0])
            put(swap_halo_grad_ref, place, at, parts[3])
            put(total_ref, 2 + 2 * place, at, parts[2] + block(grad_ref, 1 + 2 * place, at))
            put(total_ref, 3 + 2 * place, at, parts[1] + block(grad_ref, 2 + 2 * place, at))
            put(swap_first_ref, 2 + place, at, parts[5] + block(grad_ref, 6 + 2 * place, at))
            put(swap_last_ref, place, at, parts[4] + block(grad_ref, 7 + 2 * place, at))

    row = lax.rem(lax.axis_index("row"), 2)
    attend(width, row, halo_ref, swap_halo_ref, own_ref, v_ref, t_ref, swap_k_ref, swap_v_ref,
           swap_qt_ref, bias_ref, store)


def near_kernel(width, own_ref, near_ref, swap_near_ref, out_ref, swap_out_ref):
    for place in range(2):
        rows = slice(place * width, (place + 1) * width)
        at = 2 + 2 * place
        own = own_ref[at * width : (at + 1) * width]
        out_ref[rows] = own + near_ref[rows].astype(F32)
    swap_out_ref[...] = swap_near_ref[...].astype(F32)


def add_kernel(a_ref, b_ref, earlier_ref, out_ref):
    out_ref[...] = (a_ref[...] + b_ref[...].astype(F32)).astype(BF16)


def gather_kernel(
    width,
    q_ref,
    k_ref,
    gain_q_ref,
    gain_k_ref,
    own_ref,
    near_ref,
    far_ref,
    swap_first_ref,
    swap_near_ref,
    swap_last_ref,
    gated_q_ref,
    gated_k_ref,
    grad_v_ref,
    sums_ref,
):
    tokens, feat_dev = q_ref.shape
    mine, theirs = halves(feat_dev // 2)
    near, far = sides(width)

    def term(ref, index):
        return ref[index * width : (index + 1) * width].astype(F32)

    for index, rows in enumerate((near, far)):
        gated_q_ref[rows, mine] = gain_q_ref[:, mine] * term(own_ref, index)
        gated_q_ref[rows, theirs] = gain_q_ref[:, theirs] * term(swap_first_ref, index)
    gated_k_ref[near, mine] = gain_k_ref[:, mine] * term(near_ref, 0)
    gated_k_ref[far, mine] = gain_k_ref[:, mine] * (term(own_ref, 3) + term(far_ref, 0))
    grad_v_ref[near, mine] = term(near_ref, 1).astype(BF16)
    grad_v_ref[far, mine] = (term(own_ref, 5) + term(far_ref, 1)).astype(BF16)
    near_dk = term(swap_first_ref, 2) + term(swap_near_ref, 0)
    near_dv = term(swap_first_ref, 3) + term(swap_near_ref, 1)
    gated_k_ref[near, theirs] = gain_k_ref[:, theirs] * near_dk
    gated_k_ref[far, theirs] = gain_k_ref[:, theirs] * term(swap_last_ref, 0)
    grad_v_ref[near, theirs] = near_dv.astype(BF16)
    grad_v_ref[far, theirs] = swap_last_ref[width:]
    sums_ref[:tokens] = jnp.sum(q_ref[...].astype(F32) * gated_q_ref[...], -1, keepdims=True)
    sums_ref[tokens:] = jnp.sum(k_ref[...].astype(F32) * gated_k_ref[...], -1, keepdims=True)


def finish_kernel(
    q_ref, k_ref, gated_q_ref, gated_k_ref, scale_ref, sums_ref, peer_ref, grad_q_ref, grad_k_ref
):
    tokens = q_ref.shape[0]
    features = HEADS * HD
    scale = scale_ref[...]
    slope = scale * scale * scale * (sums_ref[...] + peer_ref[...]) / features
    for rows, pre_ref, gated_ref, out_ref in (
        (slice(0, tokens), q_ref, gated_q_ref, grad_q_ref),
        (slice(tokens, 2 * tokens), k_ref, gated_k_ref, grad_k_ref),
    ):
        out_ref[...] = (
            scale[rows] * gated_ref[...] - pre_ref[...].astype(F32) * slope[rows]
        ).astype(BF16)


def swapped_device(q_pre, k_pre, values, target, gain_q, gain_k, kept):
    frames, rows, width, feat_dev = q_pre.shape
    tokens = rows * width
    half = feat_dev // 2
    row_blocks = lax.axis_size("row")
    inputs = [array.reshape(tokens, feat_dev) for array in (q_pre, k_pre, values, target)]
    inputs += [gain_q, gain_k]
    inputs = [pltpu.with_memory_space_constraint(array, pltpu.HBM) for array in inputs]
    near_pairs = [(r, r + 1) for r in range(0, row_blocks - 1, 2)]
    far_pairs = [(r, r + 1) for r in range(1, row_blocks - 1, 2)]
    near, far = (pairs + [(b, a) for a, b in pairs] for pairs in (near_pairs, far_pairs))
    swap_near = [
        (f * row_blocks + a, (1 - f) * row_blocks + b) for f in range(2) for a, b in near
    ]

    def shape(first, last, dtype=BF16):
        return jax.ShapeDtypeStruct((first, last), dtype)

    block = shape(tokens, feat_dev)
    sum_pair = shape(2 * tokens, 1, F32)
    tokens_half = shape(tokens, half)
    gain = shape(1, feat_dev, F32)
    edge = shape(2 * width, half)
    bias = shape(6 * width, 2 * width, F32)

    q_all, k_all, v_all, t_all, gain_q, gain_k, sums, v_out = call(
        load_kernel,
        (block,) * 4 + (gain,) * 2 + (sum_pair, tokens_half),
        in_specs=[pl.BlockSpec(memory_space=pltpu.HBM)] * 6,
        scratch_shapes=[pltpu.SemaphoreType.DMA((6,))],
    )(*inputs)
    swap_v = lax.ppermute(v_out, "frame", SWAP)
    peer = lax.ppermute(sums, "head", SWAP)
    scale, own_kq, k_out, qt_out, near_out, far_out = call(
        functools.partial(norm_kernel, width),
        (sum_pair, shape(2 * tokens, half), tokens_half, shape(2 * tokens, half), edge, edge),
    )(q_all, k_all, v_all, t_all, sums, peer, gain_q, gain_k)
    near_in = lax.ppermute(near_out, "row", near)
    swap_k = lax.ppermute(k_out, "frame", SWAP)
    swap_qt = lax.ppermute(qt_out, "frame", SWAP)
    far_in = lax.ppermute(far_out, "row", far)
    relay_near, relay_far = call(functools.partial(relay_kernel, width), (edge, edge))(
        swap_k, swap_v, near_in
    )
    swap_near_in = lax.ppermute(relay_near, "row", near)
    swap_far_in = lax.ppermute(relay_far, "row", far)
    near_bias, far_bias = call(
        functools.partial(mask_kernel, width),
        (bias, bias),
        in_specs=[pl.BlockSpec(memory_space=pltpu.SMEM)],
    )(kept.transpose(0, 2, 1))
    shared = (own_kq, v_all, t_all, swap_k, swap_v, swap_qt)
    near_out, swap_near_out, near_terms = call(
        functools.partial(attend_near_kernel, width),
        (edge, edge, shape(10 * width, half, F32)),
        flops=5 * 10**8,
        moved=2 * 10**6,
    )(near_in, swap_near_in, *shared, near_bias, far_in)
    near_total = lax.ppermute(near_out, "row", near)
    swap_near_total = lax.ppermute(swap_near_out, ("frame", "row"), swap_near)
    far_out, swap_far_out, own_total, first_out, last_terms = call(
        functools.partial(attend_far_kernel, width),
        (edge, edge, shape(3 * tokens, half, F32), shape(4 * width, half))
        + (shape(2 * width, half, F32),),
        flops=5 * 10**8,
        moved=2 * 10**6,
    )(far_in, swap_far_in, *shared, far_bias, near_terms)
    far_terms = lax.ppermute(swap_far_out, "row", far)
    swap_first = lax.ppermute(first_out, "frame", SWAP)
    far_total = lax.ppermute(far_out, "row", far)
    near_total, swap_near_total = call(
        functools.partial(near_kernel, width), (shape(2 * width, half, F32),) * 2
    )(own_total, near_total, swap_near_total)
    last_out = call(add_kernel, edge)(last_terms, far_terms, near_total)
    swap_last = lax.ppermute(last_out, "frame", SWAP)
    gated_q, gated_k, grad_v, sum_terms = call(
        functools.partial(gather_kernel, width),
        (shape(tokens, feat_dev, F32),) * 2 + (block, sum_pair),
    )(
        q_all,
        k_all,
        gain_q,
        gain_k,
        own_total,
        near_total,
        far_total,
        swap_first,
        swap_near_total,
        swap_last,
    )
    sum_peer = lax.ppermute(sum_terms, "head", SWAP)
    grad_q, grad_k = call(finish_kernel, (block, block))(
        q_all, k_all, gated_q, gated_k, scale, sum_terms, sum_peer
    )
    return tuple(
        array.reshape(frames, rows, width, feat_dev) for array in (grad_q, grad_k, grad_v)
    )


def on_device(q_pre, *rest):
    frames, rows, _, feat_dev = q_pre.shape
    paired = lax.axis_size("frame") == 2 and frames == 1 and rows == 2
    if paired and feat_dev % (2 * HD) == 0:
        return swapped_device(q_pre, *rest)
    return per_device(q_pre, *rest)


def solution(mesh):
    return jax.shard_map(
        on_device,
        mesh=mesh,
        in_specs=(
            P("frame", "row", None, "head"),
            P("frame", "row", None, "head"),
            P("frame", "row", None, "head"),
            P("frame", "row", None, "head"),
            P("head"),
            P("head"),
            P(),
        ),
        out_specs=(
            P("frame", "row", None, "head"),
            P("frame", "row", None, "head"),
            P("frame", "row", None, "head"),
        ),
        check_vma=False,
    )
```

```python
import functools

import jax
import jax.numpy as jnp
from jax import lax
from jax.experimental import pallas as pl
from jax.experimental.pallas import tpu as pltpu
from jax.sharding import PartitionSpec as P

TC = 16
HEADS = 20
HD = 128


norm_eps = 1e-06


def padded(x, sides, width):
    for axis, dim in sides:
        size, length = (lax.axis_size(axis), x.shape[dim])
        up = [(i, (i + 1) % size) for i in range(size - 1)]
        down = [(j, i) for i, j in up]
        last = lax.slice_in_dim(x, length - width, length, axis=dim)
        first = lax.slice_in_dim(x, 0, width, axis=dim)
        before = lax.ppermute(last, axis, up)
        after = lax.ppermute(first, axis, down)
        x = jnp.concatenate([before, x, after], axis=dim)
    return x


def from_behind(value, axis, steps):
    count = lax.axis_size(axis)
    first, last = (max(0, -steps), min(count, count - steps))
    return lax.ppermute(value, axis, [(source, source + steps) for source in range(first, last)])


def query_mask(kept_win, col_tile, tiles):
    near_cols = jnp.abs(col_tile[:, None] - col_tile[None, :]) <= 1
    same_tile = col_tile[:, None] == col_tile[None, :]
    one_hot = col_tile[:, None] == jnp.arange(tiles)[None, :]
    key_kept = jnp.any(one_hot[None, None] & (kept_win[:, :, None, :] > 0), axis=-1)
    centre = (jnp.arange(3)[:, None] == 1) & (jnp.arange(3)[None, :] == 1)
    allowed = near_cols[:, None, None, :] & (
        key_kept[None] | centre[None, :, :, None] & same_tile[:, None, None, :]
    )
    return allowed.reshape(col_tile.shape[0], -1)


def attend_line(query, kv_win, t_line, allowed):
    width, heads_dev, _ = query.shape
    score_scale = HD ** (-0.5)
    key_block = kv_win[0].reshape(9 * width, heads_dev, HD)
    value_block = kv_win[1].reshape(9 * width, heads_dev, HD)
    mask = allowed[None]
    scores = (
        jnp.einsum("qhd,khd->hqk", query, key_block, preferred_element_type=jnp.float32)
        * score_scale
    )
    scores = jnp.where(mask, scores, -jnp.inf)
    row_max = jnp.max(scores, -1, keepdims=True)
    expo = jnp.where(mask, jnp.exp(scores - row_max), 0.0)
    denominator = jnp.sum(expo, -1, keepdims=True)
    probability = expo / denominator
    prob_b = probability.astype(jnp.bfloat16)
    attended = jnp.einsum("hqk,khd->qhd", prob_b, value_block, preferred_element_type=jnp.float32)
    d_out = (attended - t_line.astype(jnp.float32)).astype(jnp.bfloat16)
    delta_sum = jnp.sum(d_out.astype(jnp.float32) * attended, -1).T
    prob_grad = jnp.einsum("qhd,khd->hqk", d_out, value_block, preferred_element_type=jnp.float32)
    score_grad = (probability * (prob_grad - delta_sum[:, :, None]) * score_scale).astype(
        jnp.bfloat16
    )
    dq_line = jnp.einsum("hqk,khd->qhd", score_grad, key_block, preferred_element_type=jnp.float32)
    log_total = row_max[..., 0] + jnp.log(denominator[..., 0])
    return (dq_line.reshape(width, heads_dev * HD), d_out, log_total, delta_sum, prob_b, score_grad)


def per_device(q_pre, k_pre, values, target, gain_q, gain_k, kept):
    frames, rows, width, feat_dev = q_pre.shape
    heads_dev = feat_dev // HD
    tiles = width // TC
    features = HEADS * HD
    line_count = frames * rows
    col_tile = jnp.arange(width) // TC
    q_float = q_pre.astype(jnp.float32)
    k_float = k_pre.astype(jnp.float32)
    square_q, square_k = lax.psum(
        (jnp.sum(q_float * q_float, -1), jnp.sum(k_float * k_float, -1)), "head"
    )
    scale_q = lax.rsqrt(square_q[..., None] / features + norm_eps)
    scale_k = lax.rsqrt(square_k[..., None] / features + norm_eps)
    q_norm = (q_float * scale_q * gain_q).astype(jnp.bfloat16)
    k_norm = (k_float * scale_k * gain_k).astype(jnp.bfloat16)
    kv_ext = padded(jnp.stack([k_norm, values]), (("frame", 1), ("row", 2)), 1)
    frame_at = lax.axis_index("frame")
    row_at = lax.axis_index("row")
    zero = jnp.int32(0)
    kept_pad = jnp.pad(kept, ((1, 1), (1, 1), (0, 0)))
    kept_ext = lax.dynamic_slice(
        kept_pad, (frame_at * frames, row_at * rows, zero), (frames + 2, rows + 2, tiles)
    )
    line_ids = jnp.arange(line_count, dtype=jnp.int32)
    q_lines = q_norm.reshape(line_count, width, heads_dev, HD)
    t_lines = target.reshape(line_count, width, heads_dev, HD)

    def query_window(line):
        f_at = line // rows
        r_at = line % rows
        kv_win = lax.dynamic_slice(
            kv_ext, (zero, f_at, r_at, zero, zero), (2, 3, 3, width, feat_dev)
        )
        kept_win = lax.dynamic_slice(kept_ext, (f_at, r_at, zero), (3, 3, tiles))
        return (f_at, r_at, kv_win, query_mask(kept_win, col_tile, tiles))

    def returned_step(totals, inputs):
        line, query, t_line = inputs
        f_at, r_at, kv_win, allowed = query_window(line)
        dq_line, d_out, log_total, delta_sum, prob_b, score_grad = attend_line(
            query, kv_win, t_line, allowed
        )
        key_grad = jnp.einsum("hqk,qhd->khd", score_grad, query, preferred_element_type=jnp.float32)
        value_grad = jnp.einsum("hqk,qhd->khd", prob_b, d_out, preferred_element_type=jnp.float32)
        both = jnp.stack(
            [key_grad.reshape(3, 3, width, feat_dev), value_grad.reshape(3, 3, width, feat_dev)]
        )
        start = (zero, f_at, r_at, zero, zero)
        current = lax.dynamic_slice(totals, start, (2, 3, 3, width, feat_dev))
        totals = lax.dynamic_update_slice(totals, current + both, start)
        return (totals, dq_line)

    empty = jnp.zeros((2, frames + 2, rows + 2, width, feat_dev), jnp.float32)
    totals, dq_lines = lax.scan(returned_step, empty, (line_ids, q_lines, t_lines))
    inner = totals[:, :, 1 : rows + 1]
    row_edges = (totals[:, :, 0:1], totals[:, :, rows + 1 : rows + 2])
    row_moved = [
        from_behind(row_edges[side], "row", by_value) for side, by_value in ((0, -1), (1, 1))
    ]
    inner = inner.at[:, :, rows - 1 : rows].add(row_moved[0])
    inner = inner.at[:, :, 0:1].add(row_moved[1])
    middle = inner[:, 1 : frames + 1]
    frame_edges = (inner[:, 0:1], inner[:, frames + 1 : frames + 2])
    frame_moved = [
        from_behind(frame_edges[side], "frame", by_value) for side, by_value in ((0, -1), (1, 1))
    ]
    middle = middle.at[:, frames - 1 : frames].add(frame_moved[0])
    middle = middle.at[:, 0:1].add(frame_moved[1])
    dk_norm = middle[0]
    value_total = middle[1]
    dq_norm = dq_lines.reshape(frames, rows, width, feat_dev)
    gated_q = gain_q * dq_norm
    gated_k = gain_k * dk_norm
    sum_q, sum_k = lax.psum(
        (jnp.sum(q_float * gated_q, -1), jnp.sum(k_float * gated_k, -1)), "head"
    )
    grad_q = (scale_q * gated_q - q_float * scale_q**3 * sum_q[..., None] / features).astype(
        jnp.bfloat16
    )
    grad_k = (scale_k * gated_k - k_float * scale_k**3 * sum_k[..., None] / features).astype(
        jnp.bfloat16
    )
    return (grad_q, grad_k, value_total.astype(jnp.bfloat16))


SWAP = [(0, 1), (1, 0)]
F32 = jnp.float32
BF16 = jnp.bfloat16
VMEM_LIMIT = 48 * 1024 * 1024


def call(body, out_shape, flops=10**6, moved=10**6, **kw):
    return pl.pallas_call(
        body,
        out_shape=out_shape,
        compiler_params=pltpu.CompilerParams(vmem_limit_bytes=VMEM_LIMIT),
        cost_estimate=pl.CostEstimate(flops=flops, bytes_accessed=moved, transcendentals=0),
        **kw,
    )


def halves(half):
    frame_at = lax.axis_index("frame")
    mine = pl.multiple_of(frame_at * half, HD)
    theirs = pl.multiple_of((1 - frame_at) * half, HD)
    return (pl.ds(mine, half), pl.ds(theirs, half))


def sides(width):
    odd = lax.rem(lax.axis_index("row"), 2)
    near = pl.multiple_of((1 - odd) * width, width)
    far = pl.multiple_of(odd * width, width)
    return (pl.ds(near, width), pl.ds(far, width))


def load_kernel(
    q_in,
    k_in,
    v_in,
    t_in,
    gain_q_in,
    gain_k_in,
    q_ref,
    k_ref,
    v_ref,
    t_ref,
    gain_q_ref,
    gain_k_ref,
    sums_ref,
    v_out_ref,
    sems,
):
    tokens, feat_dev = q_ref.shape
    _, theirs = halves(feat_dev // 2)
    pairs = (
        (q_in, q_ref),
        (k_in, k_ref),
        (v_in, v_ref),
        (t_in, t_ref),
        (gain_q_in, gain_q_ref.at[0]),
        (gain_k_in, gain_k_ref.at[0]),
    )
    copies = [pltpu.make_async_copy(a, b, sems.at[i]) for i, (a, b) in enumerate(pairs)]
    for copy in copies:
        copy.start()
    copies[0].wait()
    q_float = q_ref[...].astype(F32)
    sums_ref[:tokens] = jnp.sum(q_float * q_float, -1, keepdims=True)
    copies[1].wait()
    k_float = k_ref[...].astype(F32)
    sums_ref[tokens:] = jnp.sum(k_float * k_float, -1, keepdims=True)
    copies[2].wait()
    v_out_ref[...] = v_ref[:, theirs]
    for copy in copies[3:]:
        copy.wait()


def norm_kernel(
    width,
    q_ref,
    k_ref,
    v_ref,
    t_ref,
    sums_ref,
    peer_ref,
    gain_q_ref,
    gain_k_ref,
    scale_ref,
    own_ref,
    k_out_ref,
    qt_out_ref,
    near_ref,
    far_ref,
):
    tokens, feat_dev = q_ref.shape
    features = HEADS * HD
    mine, theirs = halves(feat_dev // 2)
    near, far = sides(width)
    scale = lax.rsqrt((sums_ref[...] + peer_ref[...]) / features + norm_eps)
    scale_ref[...] = scale
    scale_q, scale_k = (scale[:tokens], scale[tokens:])

    def normed(ref, part, scales, gain_ref):
        return (ref[:, part].astype(F32) * scales * gain_ref[:, part]).astype(BF16)

    k_out_ref[...] = normed(k_ref, theirs, scale_k, gain_k_ref)
    qt_out_ref[:tokens] = normed(q_ref, theirs, scale_q, gain_q_ref)
    qt_out_ref[tokens:] = t_ref[:, theirs]
    own_ref[:tokens] = normed(k_ref, mine, scale_k, gain_k_ref)
    own_ref[tokens:] = normed(q_ref, mine, scale_q, gain_q_ref)
    for out_ref, rows in ((near_ref, near), (far_ref, far)):
        out_ref[:width] = own_ref[rows]
        out_ref[width:] = v_ref[rows, mine]


def relay_near_kernel(width, k_ref, v_ref, earlier_ref, out_ref):
    near, _ = sides(width)
    out_ref[:width] = k_ref[near]
    out_ref[width:] = v_ref[near]


def relay_far_kernel(width, kept_ref, k_ref, v_ref, earlier_ref, out_ref, near_ref, far_ref):
    _, far = sides(width)
    out_ref[:width] = k_ref[far]
    out_ref[width:] = v_ref[far]
    rows = 2
    count = kept_ref.shape[2]
    tiles = width // TC
    frame_at = lax.axis_index("frame")
    first_row = lax.axis_index("row") * rows
    odd = lax.rem(lax.axis_index("row"), 2)
    query_at = lax.broadcasted_iota(jnp.int32, (TC, near_ref.shape[1]), 1)
    query_tile = lax.rem(query_at, width) // TC
    for out_ref, row in ((near_ref, 1 - odd), (far_ref, odd)):
        for part in range(2):
            frame = frame_at if part == 0 else 1 - frame_at
            for slot, place in enumerate((3 * row - 1, row, 1 - row)):
                at = first_row + place
                inside = (at >= 0) & (at < count)
                at = jnp.clip(at, 0, count - 1)
                for tile in range(tiles):
                    value = jnp.where(inside, kept_ref[frame, tile, at], 0)
                    allowed = (jnp.abs(query_tile - tile) <= 1) & (value > 0)
                    if slot == 1:
                        allowed |= (query_tile == tile) & (query_at // width == part)
                    here = ((part * 3 + slot) * tiles + tile) * TC
                    out_ref[here : here + TC] = jnp.where(allowed, 0.0, -1e30)


def attend(width, row, halo_ref, swap_halo_ref, own_ref, v_ref, t_ref, swap_k_ref, swap_v_ref,
           swap_qt_ref, bias_ref, store):
    tokens, half = swap_k_ref.shape
    score_scale = HD ** (-0.5)
    mine = lax.axis_index("frame") * half
    bias = bias_ref[...]
    own_at = pl.multiple_of(row * width, width)
    other_at = pl.multiple_of((1 - row) * width, width)
    rows = (pl.ds(own_at, width), pl.ds(other_at, width))
    query_at = pl.ds(pl.multiple_of(tokens + own_at, width), width)

    def product(a, b, a_dim, b_dim):
        return lax.dot_general(a, b, (((a_dim,), (b_dim,)), ((), ())), preferred_element_type=F32)

    def load(head):
        at = slice(head * HD, (head + 1) * HD)
        mine_at = pl.ds(pl.multiple_of(mine + head * HD, HD), HD)
        query = jnp.concatenate([own_ref[query_at, at], swap_qt_ref[rows[0], at]], 0)
        target = jnp.concatenate([t_ref[rows[0], mine_at], swap_qt_ref[query_at, at]], 0)
        key = jnp.concatenate(
            [halo_ref[:width, at]]
            + [own_ref[r, at] for r in rows]
            + [swap_halo_ref[:width, at]]
            + [swap_k_ref[r, at] for r in rows],
            0,
        )
        value = jnp.concatenate(
            [halo_ref[width:, at]]
            + [v_ref[r, mine_at] for r in rows]
            + [swap_halo_ref[width:, at]]
            + [swap_v_ref[r, at] for r in rows],
            0,
        )
        return (query, target, key, value)

    def weights(query, key):
        scores = product(key, query, 1, 1) * score_scale + bias
        expo = jnp.exp(scores - jnp.max(scores, 0, keepdims=True))
        return expo * (1.0 / jnp.sum(expo, 0, keepdims=True))

    def output_grad(prob_b, target, value):
        attended = product(value, prob_b, 0, 0)
        d_out = (attended - target.astype(F32).T).astype(BF16)
        return (d_out, jnp.sum(d_out.astype(F32) * attended, 0, keepdims=True))

    def score_grads(probability, d_out, delta_sum, value):
        prob_grad = product(value, d_out, 1, 0)
        return (probability * (prob_grad - delta_sum) * score_scale).astype(BF16)

    def grads(score_grad, prob_b, d_out, query, key):
        dq = product(key, score_grad, 0, 0).T
        dk = product(score_grad, query, 1, 0)
        return (dq, dk, product(prob_b, d_out, 1, 1))

    heads = range(half // HD)
    loaded = [load(head) for head in heads]
    probability = [weights(query, key) for query, _, key, _ in loaded]
    prob_b = [p.astype(BF16) for p in probability]
    outs = [output_grad(p, t, v) for p, (_, t, _, v) in zip(prob_b, loaded)]
    score_grad = [score_grads(p, *o, x[3]) for p, o, x in zip(probability, outs, loaded)]
    for head in heads:
        query, _, key, _ = loaded[head]
        at = slice(head * HD, (head + 1) * HD)
        store(at, *grads(score_grad[head], prob_b[head], outs[head][0], query, key))


def attend_near_kernel(
    width,
    halo_ref,
    swap_halo_ref,
    own_ref,
    v_ref,
    t_ref,
    swap_k_ref,
    swap_v_ref,
    swap_qt_ref,
    bias_ref,
    earlier_ref,
    halo_grad_ref,
    swap_halo_grad_ref,
    grad_ref,
):
    def store(at, dq, dk, dv):
        for place, grad in ((0, dk), (1, dv)):
            to = slice(place * width, (place + 1) * width)
            halo_grad_ref[to, at] = grad[:width].astype(BF16)
            swap_halo_grad_ref[to, at] = grad[3 * width : 4 * width].astype(BF16)
            for part in range(2):
                start = (5 * part + 1 + 2 * place) * width
                first = (3 * part + 1) * width
                grad_ref[start : start + 2 * width, at] = grad[first : first + 2 * width]
        for part in range(2):
            start = 5 * part * width
            grad_ref[start : start + width, at] = dq[part * width : (part + 1) * width]

    row = 1 - lax.rem(lax.axis_index("row"), 2)
    attend(width, row, halo_ref, swap_halo_ref, own_ref, v_ref, t_ref, swap_k_ref, swap_v_ref,
           swap_qt_ref, bias_ref, store)


def attend_far_kernel(
    width,
    halo_ref,
    swap_halo_ref,
    own_ref,
    v_ref,
    t_ref,
    swap_k_ref,
    swap_v_ref,
    swap_qt_ref,
    bias_ref,
    grad_ref,
    halo_grad_ref,
    swap_halo_grad_ref,
    total_ref,
    swap_first_ref,
    swap_last_ref,
):
    def block(ref, index, at):
        return ref[index * width : (index + 1) * width, at]

    def put(ref, index, at, value):
        ref[index * width : (index + 1) * width, at] = value.astype(ref.dtype)

    def store(at, dq, dk, dv):
        put(total_ref, 0, at, block(grad_ref, 0, at))
        put(total_ref, 1, at, dq[:width])
        put(swap_first_ref, 0, at, block(grad_ref, 5, at))
        put(swap_first_ref, 1, at, dq[width:])
        for place, grad in ((0, dk), (1, dv)):
            parts = [grad[i * width : (i + 1) * width] for i in range(6)]
            put(halo_grad_ref, place, at, parts[0])
            put(swap_halo_grad_ref, place, at, parts[3])
            put(total_ref, 2 + 2 * place, at, parts[2] + block(grad_ref, 1 + 2 * place, at))
            put(total_ref, 3 + 2 * place, at, parts[1] + block(grad_ref, 2 + 2 * place, at))
            put(swap_first_ref, 2 + place, at, parts[5] + block(grad_ref, 6 + 2 * place, at))
            put(swap_last_ref, place, at, parts[4] + block(grad_ref, 7 + 2 * place, at))

    row = lax.rem(lax.axis_index("row"), 2)
    attend(width, row, halo_ref, swap_halo_ref, own_ref, v_ref, t_ref, swap_k_ref, swap_v_ref,
           swap_qt_ref, bias_ref, store)


def near_kernel(width, own_ref, near_ref, swap_near_ref, out_ref, swap_out_ref):
    for place in range(2):
        rows = slice(place * width, (place + 1) * width)
        at = 2 + 2 * place
        own = own_ref[at * width : (at + 1) * width]
        out_ref[rows] = own + near_ref[rows].astype(F32)
    swap_out_ref[...] = swap_near_ref[: 2 * width].astype(F32)


def add_kernel(a_ref, b_ref, out_ref):
    out_ref[...] = (a_ref[...] + b_ref[...].astype(F32)).astype(BF16)


def gather_kernel(
    width,
    q_ref,
    k_ref,
    gain_q_ref,
    gain_k_ref,
    own_ref,
    near_ref,
    far_ref,
    swap_first_ref,
    swap_near_ref,
    swap_last_ref,
    gated_q_ref,
    gated_k_ref,
    grad_v_ref,
    sums_ref,
):
    tokens, feat_dev = q_ref.shape
    mine, theirs = halves(feat_dev // 2)
    near, far = sides(width)

    def term(ref, index):
        return ref[index * width : (index + 1) * width].astype(F32)

    for index, rows in enumerate((near, far)):
        gated_q_ref[rows, mine] = gain_q_ref[:, mine] * term(own_ref, index)
        gated_q_ref[rows, theirs] = gain_q_ref[:, theirs] * term(swap_first_ref, index)
    gated_k_ref[near, mine] = gain_k_ref[:, mine] * term(near_ref, 0)
    gated_k_ref[far, mine] = gain_k_ref[:, mine] * (term(own_ref, 3) + term(far_ref, 0))
    grad_v_ref[near, mine] = term(near_ref, 1).astype(BF16)
    grad_v_ref[far, mine] = (term(own_ref, 5) + term(far_ref, 1)).astype(BF16)
    near_dk = term(swap_first_ref, 2) + term(swap_near_ref, 0)
    near_dv = term(swap_first_ref, 3) + term(swap_near_ref, 1)
    gated_k_ref[near, theirs] = gain_k_ref[:, theirs] * near_dk
    gated_k_ref[far, theirs] = gain_k_ref[:, theirs] * term(swap_last_ref, 0)
    grad_v_ref[near, theirs] = near_dv.astype(BF16)
    grad_v_ref[far, theirs] = swap_last_ref[width:]
    sums_ref[:tokens] = jnp.sum(q_ref[...].astype(F32) * gated_q_ref[...], -1, keepdims=True)
    sums_ref[tokens:] = jnp.sum(k_ref[...].astype(F32) * gated_k_ref[...], -1, keepdims=True)


def finish_kernel(
    q_ref, k_ref, gated_q_ref, gated_k_ref, scale_ref, sums_ref, peer_ref, grad_q_ref, grad_k_ref
):
    tokens = q_ref.shape[0]
    features = HEADS * HD
    scale = scale_ref[...]
    slope = scale * scale * scale * (sums_ref[...] + peer_ref[...]) / features
    for rows, pre_ref, gated_ref, out_ref in (
        (slice(0, tokens), q_ref, gated_q_ref, grad_q_ref),
        (slice(tokens, 2 * tokens), k_ref, gated_k_ref, grad_k_ref),
    ):
        out_ref[...] = (
            scale[rows] * gated_ref[...] - pre_ref[...].astype(F32) * slope[rows]
        ).astype(BF16)


def swapped_device(q_pre, k_pre, values, target, gain_q, gain_k, kept):
    frames, rows, width, feat_dev = q_pre.shape
    tokens = rows * width
    half = feat_dev // 2
    row_blocks = lax.axis_size("row")
    inputs = [array.reshape(tokens, feat_dev) for array in (q_pre, k_pre, values, target)]
    inputs += [gain_q, gain_k]
    inputs = [pltpu.with_memory_space_constraint(array, pltpu.HBM) for array in inputs]
    near_pairs = [(r, r + 1) for r in range(0, row_blocks - 1, 2)]
    far_pairs = [(r, r + 1) for r in range(1, row_blocks - 1, 2)]
    near, far = (pairs + [(b, a) for a, b in pairs] for pairs in (near_pairs, far_pairs))
    swap_near = [
        (f * row_blocks + a, (1 - f) * row_blocks + b) for f in range(2) for a, b in near
    ]

    def shape(first, last, dtype=BF16):
        return jax.ShapeDtypeStruct((first, last), dtype)

    block = shape(tokens, feat_dev)
    sum_pair = shape(2 * tokens, 1, F32)
    tokens_half = shape(tokens, half)
    gain = shape(1, feat_dev, F32)
    edge = shape(2 * width, half)
    padded_edge = shape(2 * width + 16, half)
    bias = shape(6 * width, 2 * width, F32)

    q_all, k_all, v_all, t_all, gain_q, gain_k, sums, v_out = call(
        load_kernel,
        (block,) * 4 + (gain,) * 2 + (sum_pair, tokens_half),
        in_specs=[pl.BlockSpec(memory_space=pltpu.HBM)] * 6,
        scratch_shapes=[pltpu.SemaphoreType.DMA((6,))],
    )(*inputs)
    swap_v = lax.ppermute(v_out, "frame", SWAP)
    peer = lax.ppermute(sums, "head", SWAP)
    scale, own_kq, k_out, qt_out, near_out, far_out = call(
        functools.partial(norm_kernel, width),
        (sum_pair, shape(2 * tokens, half), tokens_half, shape(2 * tokens, half), edge, edge),
    )(q_all, k_all, v_all, t_all, sums, peer, gain_q, gain_k)
    near_in = lax.ppermute(near_out, "row", near)
    swap_k = lax.ppermute(k_out, "frame", SWAP)
    swap_qt = lax.ppermute(qt_out, "frame", SWAP)
    far_in = lax.ppermute(far_out, "row", far)
    relay_near = call(functools.partial(relay_near_kernel, width), edge)(swap_k, swap_v, near_in)
    swap_near_in = lax.ppermute(relay_near, "row", near)
    relay_far, near_bias, far_bias = call(
        functools.partial(relay_far_kernel, width),
        (edge, bias, bias),
        in_specs=[pl.BlockSpec(memory_space=pltpu.SMEM)]
        + [pl.BlockSpec(memory_space=pltpu.VMEM)] * 3,
    )(kept.transpose(0, 2, 1), swap_k, swap_v, relay_near)
    swap_far_in = lax.ppermute(relay_far, "row", far)
    shared = (own_kq, v_all, t_all, swap_k, swap_v, swap_qt)
    near_out, swap_near_out, near_terms = call(
        functools.partial(attend_near_kernel, width),
        (padded_edge, padded_edge, shape(10 * width, half, F32)),
        flops=5 * 10**8,
        moved=2 * 10**6,
    )(near_in, swap_near_in, *shared, near_bias, far_in)
    near_total = lax.ppermute(near_out, "row", near)
    swap_near_total = lax.ppermute(swap_near_out, ("frame", "row"), swap_near)
    far_out, swap_far_out, own_total, first_out, last_terms = call(
        functools.partial(attend_far_kernel, width),
        (edge, edge, shape(3 * tokens, half, F32), shape(4 * width, half))
        + (shape(2 * width, half, F32),),
        flops=5 * 10**8,
        moved=2 * 10**6,
    )(far_in, swap_far_in, *shared, far_bias, near_terms)
    far_terms = lax.ppermute(swap_far_out, "row", far)
    swap_first = lax.ppermute(first_out, "frame", SWAP)
    far_total = lax.ppermute(far_out, "row", far)
    near_total, swap_near_total = call(
        functools.partial(near_kernel, width),
        (shape(2 * width, half, F32),) * 2,
        flops=3 * 10**9,
    )(own_total, near_total, swap_near_total)
    last_out = call(add_kernel, edge, flops=1, moved=1)(last_terms, far_terms)
    swap_last = lax.ppermute(last_out, "frame", SWAP)
    gated_q, gated_k, grad_v, sum_terms = call(
        functools.partial(gather_kernel, width),
        (shape(tokens, feat_dev, F32),) * 2 + (block, sum_pair),
    )(
        q_all,
        k_all,
        gain_q,
        gain_k,
        own_total,
        near_total,
        far_total,
        swap_first,
        swap_near_total,
        swap_last,
    )
    sum_peer = lax.ppermute(sum_terms, "head", SWAP)
    grad_q, grad_k = call(finish_kernel, (block, block))(
        q_all, k_all, gated_q, gated_k, scale, sum_terms, sum_peer
    )
    return tuple(
        array.reshape(frames, rows, width, feat_dev) for array in (grad_q, grad_k, grad_v)
    )


def on_device(q_pre, *rest):
    frames, rows, _, feat_dev = q_pre.shape
    paired = lax.axis_size("frame") == 2 and frames == 1 and rows == 2
    if paired and feat_dev % (2 * HD) == 0:
        return swapped_device(q_pre, *rest)
    return per_device(q_pre, *rest)


def solution(mesh):
    return jax.shard_map(
        on_device,
        mesh=mesh,
        in_specs=(
            P("frame", "row", None, "head"),
            P("frame", "row", None, "head"),
            P("frame", "row", None, "head"),
            P("frame", "row", None, "head"),
            P("head"),
            P("head"),
            P(),
        ),
        out_specs=(
            P("frame", "row", None, "head"),
            P("frame", "row", None, "head"),
            P("frame", "row", None, "head"),
        ),
        check_vma=False,
    )
```

```python
import functools

import jax
import jax.numpy as jnp
from jax import lax
from jax.experimental import pallas as pl
from jax.experimental.pallas import tpu as pltpu
from jax.sharding import PartitionSpec as P

TC = 16
HEADS = 20
HD = 128


norm_eps = 1e-06


def padded(x, sides, width):
    for axis, dim in sides:
        size, length = (lax.axis_size(axis), x.shape[dim])
        up = [(i, (i + 1) % size) for i in range(size - 1)]
        down = [(j, i) for i, j in up]
        last = lax.slice_in_dim(x, length - width, length, axis=dim)
        first = lax.slice_in_dim(x, 0, width, axis=dim)
        before = lax.ppermute(last, axis, up)
        after = lax.ppermute(first, axis, down)
        x = jnp.concatenate([before, x, after], axis=dim)
    return x


def from_behind(value, axis, steps):
    count = lax.axis_size(axis)
    first, last = (max(0, -steps), min(count, count - steps))
    return lax.ppermute(value, axis, [(source, source + steps) for source in range(first, last)])


def query_mask(kept_win, col_tile, tiles):
    near_cols = jnp.abs(col_tile[:, None] - col_tile[None, :]) <= 1
    same_tile = col_tile[:, None] == col_tile[None, :]
    one_hot = col_tile[:, None] == jnp.arange(tiles)[None, :]
    key_kept = jnp.any(one_hot[None, None] & (kept_win[:, :, None, :] > 0), axis=-1)
    centre = (jnp.arange(3)[:, None] == 1) & (jnp.arange(3)[None, :] == 1)
    allowed = near_cols[:, None, None, :] & (
        key_kept[None] | centre[None, :, :, None] & same_tile[:, None, None, :]
    )
    return allowed.reshape(col_tile.shape[0], -1)


def attend_line(query, kv_win, t_line, allowed):
    width, heads_dev, _ = query.shape
    score_scale = HD ** (-0.5)
    key_block = kv_win[0].reshape(9 * width, heads_dev, HD)
    value_block = kv_win[1].reshape(9 * width, heads_dev, HD)
    mask = allowed[None]
    scores = (
        jnp.einsum("qhd,khd->hqk", query, key_block, preferred_element_type=jnp.float32)
        * score_scale
    )
    scores = jnp.where(mask, scores, -jnp.inf)
    row_max = jnp.max(scores, -1, keepdims=True)
    expo = jnp.where(mask, jnp.exp(scores - row_max), 0.0)
    denominator = jnp.sum(expo, -1, keepdims=True)
    probability = expo / denominator
    prob_b = probability.astype(jnp.bfloat16)
    attended = jnp.einsum("hqk,khd->qhd", prob_b, value_block, preferred_element_type=jnp.float32)
    d_out = (attended - t_line.astype(jnp.float32)).astype(jnp.bfloat16)
    delta_sum = jnp.sum(d_out.astype(jnp.float32) * attended, -1).T
    prob_grad = jnp.einsum("qhd,khd->hqk", d_out, value_block, preferred_element_type=jnp.float32)
    score_grad = (probability * (prob_grad - delta_sum[:, :, None]) * score_scale).astype(
        jnp.bfloat16
    )
    dq_line = jnp.einsum("hqk,khd->qhd", score_grad, key_block, preferred_element_type=jnp.float32)
    log_total = row_max[..., 0] + jnp.log(denominator[..., 0])
    return (dq_line.reshape(width, heads_dev * HD), d_out, log_total, delta_sum, prob_b, score_grad)


def per_device(q_pre, k_pre, values, target, gain_q, gain_k, kept):
    frames, rows, width, feat_dev = q_pre.shape
    heads_dev = feat_dev // HD
    tiles = width // TC
    features = HEADS * HD
    line_count = frames * rows
    col_tile = jnp.arange(width) // TC
    q_float = q_pre.astype(jnp.float32)
    k_float = k_pre.astype(jnp.float32)
    square_q, square_k = lax.psum(
        (jnp.sum(q_float * q_float, -1), jnp.sum(k_float * k_float, -1)), "head"
    )
    scale_q = lax.rsqrt(square_q[..., None] / features + norm_eps)
    scale_k = lax.rsqrt(square_k[..., None] / features + norm_eps)
    q_norm = (q_float * scale_q * gain_q).astype(jnp.bfloat16)
    k_norm = (k_float * scale_k * gain_k).astype(jnp.bfloat16)
    kv_ext = padded(jnp.stack([k_norm, values]), (("frame", 1), ("row", 2)), 1)
    frame_at = lax.axis_index("frame")
    row_at = lax.axis_index("row")
    zero = jnp.int32(0)
    kept_pad = jnp.pad(kept, ((1, 1), (1, 1), (0, 0)))
    kept_ext = lax.dynamic_slice(
        kept_pad, (frame_at * frames, row_at * rows, zero), (frames + 2, rows + 2, tiles)
    )
    line_ids = jnp.arange(line_count, dtype=jnp.int32)
    q_lines = q_norm.reshape(line_count, width, heads_dev, HD)
    t_lines = target.reshape(line_count, width, heads_dev, HD)

    def query_window(line):
        f_at = line // rows
        r_at = line % rows
        kv_win = lax.dynamic_slice(
            kv_ext, (zero, f_at, r_at, zero, zero), (2, 3, 3, width, feat_dev)
        )
        kept_win = lax.dynamic_slice(kept_ext, (f_at, r_at, zero), (3, 3, tiles))
        return (f_at, r_at, kv_win, query_mask(kept_win, col_tile, tiles))

    def returned_step(totals, inputs):
        line, query, t_line = inputs
        f_at, r_at, kv_win, allowed = query_window(line)
        dq_line, d_out, log_total, delta_sum, prob_b, score_grad = attend_line(
            query, kv_win, t_line, allowed
        )
        key_grad = jnp.einsum("hqk,qhd->khd", score_grad, query, preferred_element_type=jnp.float32)
        value_grad = jnp.einsum("hqk,qhd->khd", prob_b, d_out, preferred_element_type=jnp.float32)
        both = jnp.stack(
            [key_grad.reshape(3, 3, width, feat_dev), value_grad.reshape(3, 3, width, feat_dev)]
        )
        start = (zero, f_at, r_at, zero, zero)
        current = lax.dynamic_slice(totals, start, (2, 3, 3, width, feat_dev))
        totals = lax.dynamic_update_slice(totals, current + both, start)
        return (totals, dq_line)

    empty = jnp.zeros((2, frames + 2, rows + 2, width, feat_dev), jnp.float32)
    totals, dq_lines = lax.scan(returned_step, empty, (line_ids, q_lines, t_lines))
    inner = totals[:, :, 1 : rows + 1]
    row_edges = (totals[:, :, 0:1], totals[:, :, rows + 1 : rows + 2])
    row_moved = [
        from_behind(row_edges[side], "row", by_value) for side, by_value in ((0, -1), (1, 1))
    ]
    inner = inner.at[:, :, rows - 1 : rows].add(row_moved[0])
    inner = inner.at[:, :, 0:1].add(row_moved[1])
    middle = inner[:, 1 : frames + 1]
    frame_edges = (inner[:, 0:1], inner[:, frames + 1 : frames + 2])
    frame_moved = [
        from_behind(frame_edges[side], "frame", by_value) for side, by_value in ((0, -1), (1, 1))
    ]
    middle = middle.at[:, frames - 1 : frames].add(frame_moved[0])
    middle = middle.at[:, 0:1].add(frame_moved[1])
    dk_norm = middle[0]
    value_total = middle[1]
    dq_norm = dq_lines.reshape(frames, rows, width, feat_dev)
    gated_q = gain_q * dq_norm
    gated_k = gain_k * dk_norm
    sum_q, sum_k = lax.psum(
        (jnp.sum(q_float * gated_q, -1), jnp.sum(k_float * gated_k, -1)), "head"
    )
    grad_q = (scale_q * gated_q - q_float * scale_q**3 * sum_q[..., None] / features).astype(
        jnp.bfloat16
    )
    grad_k = (scale_k * gated_k - k_float * scale_k**3 * sum_k[..., None] / features).astype(
        jnp.bfloat16
    )
    return (grad_q, grad_k, value_total.astype(jnp.bfloat16))


SWAP = [(0, 1), (1, 0)]
F32 = jnp.float32
BF16 = jnp.bfloat16
VMEM_LIMIT = 48 * 1024 * 1024


def call(body, out_shape, flops=10**6, moved=10**6, **kw):
    return pl.pallas_call(
        body,
        out_shape=out_shape,
        compiler_params=pltpu.CompilerParams(vmem_limit_bytes=VMEM_LIMIT),
        cost_estimate=pl.CostEstimate(flops=flops, bytes_accessed=moved, transcendentals=0),
        **kw,
    )


def halves(half):
    frame_at = lax.axis_index("frame")
    mine = pl.multiple_of(frame_at * half, HD)
    theirs = pl.multiple_of((1 - frame_at) * half, HD)
    return (pl.ds(mine, half), pl.ds(theirs, half))


def sides(width):
    odd = lax.rem(lax.axis_index("row"), 2)
    near = pl.multiple_of((1 - odd) * width, width)
    far = pl.multiple_of(odd * width, width)
    return (pl.ds(near, width), pl.ds(far, width))


def load_kernel(
    q_in,
    k_in,
    v_in,
    t_in,
    gain_q_in,
    gain_k_in,
    q_ref,
    k_ref,
    v_ref,
    t_ref,
    gain_q_ref,
    gain_k_ref,
    sums_ref,
    v_out_ref,
    sems,
):
    tokens, feat_dev = q_ref.shape
    _, theirs = halves(feat_dev // 2)
    pairs = (
        (q_in, q_ref),
        (k_in, k_ref),
        (v_in, v_ref),
        (t_in, t_ref),
        (gain_q_in, gain_q_ref.at[0]),
        (gain_k_in, gain_k_ref.at[0]),
    )
    copies = [pltpu.make_async_copy(a, b, sems.at[i]) for i, (a, b) in enumerate(pairs)]
    for copy in copies:
        copy.start()
    copies[0].wait()
    q_float = q_ref[...].astype(F32)
    sums_ref[:tokens] = jnp.sum(q_float * q_float, -1, keepdims=True)
    copies[1].wait()
    k_float = k_ref[...].astype(F32)
    sums_ref[tokens:] = jnp.sum(k_float * k_float, -1, keepdims=True)
    copies[2].wait()
    v_out_ref[...] = v_ref[:, theirs]
    for copy in copies[3:]:
        copy.wait()


def norm_kernel(
    width,
    q_ref,
    k_ref,
    v_ref,
    t_ref,
    sums_ref,
    peer_ref,
    gain_q_ref,
    gain_k_ref,
    scale_ref,
    own_ref,
    k_out_ref,
    qt_out_ref,
    near_ref,
    far_ref,
):
    tokens, feat_dev = q_ref.shape
    features = HEADS * HD
    mine, theirs = halves(feat_dev // 2)
    near, far = sides(width)
    scale = lax.rsqrt((sums_ref[...] + peer_ref[...]) / features + norm_eps)
    scale_ref[...] = scale
    scale_q, scale_k = (scale[:tokens], scale[tokens:])

    def normed(ref, part, scales, gain_ref):
        return (ref[:, part].astype(F32) * scales * gain_ref[:, part]).astype(BF16)

    k_out_ref[...] = normed(k_ref, theirs, scale_k, gain_k_ref)
    qt_out_ref[:tokens] = normed(q_ref, theirs, scale_q, gain_q_ref)
    qt_out_ref[tokens:] = t_ref[:, theirs]
    own_ref[:tokens] = normed(k_ref, mine, scale_k, gain_k_ref)
    own_ref[tokens:] = normed(q_ref, mine, scale_q, gain_q_ref)
    for out_ref, rows in ((near_ref, near), (far_ref, far)):
        out_ref[:width] = own_ref[rows]
        out_ref[width:] = v_ref[rows, mine]


def relay_near_kernel(width, k_ref, v_ref, earlier_ref, out_ref):
    near, _ = sides(width)
    out_ref[:width] = k_ref[near]
    out_ref[width:] = v_ref[near]


def relay_far_kernel(width, kept_ref, k_ref, v_ref, earlier_ref, out_ref, near_ref, far_ref):
    _, far = sides(width)
    out_ref[:width] = k_ref[far]
    out_ref[width:] = v_ref[far]
    rows = 2
    count = kept_ref.shape[2]
    tiles = width // TC
    frame_at = lax.axis_index("frame")
    first_row = lax.axis_index("row") * rows
    odd = lax.rem(lax.axis_index("row"), 2)
    query_at = lax.broadcasted_iota(jnp.int32, (TC, near_ref.shape[1]), 1)
    query_tile = lax.rem(query_at, width) // TC
    for out_ref, row in ((near_ref, 1 - odd), (far_ref, odd)):
        for part in range(2):
            frame = frame_at if part == 0 else 1 - frame_at
            for slot, place in enumerate((3 * row - 1, row, 1 - row)):
                at = first_row + place
                inside = (at >= 0) & (at < count)
                at = jnp.clip(at, 0, count - 1)
                for tile in range(tiles):
                    value = jnp.where(inside, kept_ref[frame, tile, at], 0)
                    allowed = (jnp.abs(query_tile - tile) <= 1) & (value > 0)
                    if slot == 1:
                        allowed |= (query_tile == tile) & (query_at // width == part)
                    here = ((part * 3 + slot) * tiles + tile) * TC
                    out_ref[here : here + TC] = jnp.where(allowed, 0.0, -1e30)


def attend(width, row, halo_ref, swap_halo_ref, own_ref, v_ref, t_ref, swap_k_ref, swap_v_ref,
           swap_qt_ref, bias_ref, store):
    tokens, half = swap_k_ref.shape
    score_scale = HD ** (-0.5)
    mine = lax.axis_index("frame") * half
    bias = bias_ref[...]
    own_at = pl.multiple_of(row * width, width)
    other_at = pl.multiple_of((1 - row) * width, width)
    rows = (pl.ds(own_at, width), pl.ds(other_at, width))
    query_at = pl.ds(pl.multiple_of(tokens + own_at, width), width)

    def product(a, b, a_dim, b_dim):
        return lax.dot_general(a, b, (((a_dim,), (b_dim,)), ((), ())), preferred_element_type=F32)

    def load(head):
        at = slice(head * HD, (head + 1) * HD)
        mine_at = pl.ds(pl.multiple_of(mine + head * HD, HD), HD)
        query = jnp.concatenate([own_ref[query_at, at], swap_qt_ref[rows[0], at]], 0)
        target = jnp.concatenate([t_ref[rows[0], mine_at], swap_qt_ref[query_at, at]], 0)
        key = jnp.concatenate(
            [halo_ref[:width, at]]
            + [own_ref[r, at] for r in rows]
            + [swap_halo_ref[:width, at]]
            + [swap_k_ref[r, at] for r in rows],
            0,
        )
        value = jnp.concatenate(
            [halo_ref[width:, at]]
            + [v_ref[r, mine_at] for r in rows]
            + [swap_halo_ref[width:, at]]
            + [swap_v_ref[r, at] for r in rows],
            0,
        )
        return (query, target, key, value)

    def weights(query, key):
        scores = product(key, query, 1, 1) * score_scale + bias
        expo = jnp.exp(scores - jnp.max(scores, 0, keepdims=True))
        return expo * (1.0 / jnp.sum(expo, 0, keepdims=True))

    def output_grad(prob_b, target, value):
        attended = product(value, prob_b, 0, 0)
        d_out = (attended - target.astype(F32).T).astype(BF16)
        return (d_out, jnp.sum(d_out.astype(F32) * attended, 0, keepdims=True))

    def score_grads(probability, d_out, delta_sum, value):
        prob_grad = product(value, d_out, 1, 0)
        return (probability * (prob_grad - delta_sum) * score_scale).astype(BF16)

    def grads(score_grad, prob_b, d_out, query, key):
        dq = product(key, score_grad, 0, 0).T
        dk = product(score_grad, query, 1, 0)
        return (dq, dk, product(prob_b, d_out, 1, 1))

    heads = range(half // HD)
    loaded = [load(head) for head in heads]
    probability = [weights(query, key) for query, _, key, _ in loaded]
    prob_b = [p.astype(BF16) for p in probability]
    outs = [output_grad(p, t, v) for p, (_, t, _, v) in zip(prob_b, loaded)]
    score_grad = [score_grads(p, *o, x[3]) for p, o, x in zip(probability, outs, loaded)]
    for head in heads:
        query, _, key, _ = loaded[head]
        at = slice(head * HD, (head + 1) * HD)
        store(at, *grads(score_grad[head], prob_b[head], outs[head][0], query, key))


def attend_near_kernel(
    width,
    halo_ref,
    swap_halo_ref,
    own_ref,
    v_ref,
    t_ref,
    swap_k_ref,
    swap_v_ref,
    swap_qt_ref,
    bias_ref,
    earlier_ref,
    halo_grad_ref,
    swap_halo_grad_ref,
    grad_ref,
):
    def store(at, dq, dk, dv):
        for place, grad in ((0, dk), (1, dv)):
            to = slice(place * width, (place + 1) * width)
            halo_grad_ref[to, at] = grad[:width].astype(BF16)
            swap_halo_grad_ref[to, at] = grad[3 * width : 4 * width].astype(BF16)
            for part in range(2):
                start = (5 * part + 1 + 2 * place) * width
                first = (3 * part + 1) * width
                grad_ref[start : start + 2 * width, at] = grad[first : first + 2 * width]
        for part in range(2):
            start = 5 * part * width
            grad_ref[start : start + width, at] = dq[part * width : (part + 1) * width]

    row = 1 - lax.rem(lax.axis_index("row"), 2)
    attend(width, row, halo_ref, swap_halo_ref, own_ref, v_ref, t_ref, swap_k_ref, swap_v_ref,
           swap_qt_ref, bias_ref, store)


def attend_far_kernel(
    width,
    halo_ref,
    swap_halo_ref,
    own_ref,
    v_ref,
    t_ref,
    swap_k_ref,
    swap_v_ref,
    swap_qt_ref,
    bias_ref,
    grad_ref,
    halo_grad_ref,
    swap_halo_grad_ref,
    total_ref,
    swap_first_ref,
    swap_last_ref,
):
    def block(ref, index, at):
        return ref[index * width : (index + 1) * width, at]

    def put(ref, index, at, value):
        ref[index * width : (index + 1) * width, at] = value.astype(ref.dtype)

    def store(at, dq, dk, dv):
        put(total_ref, 0, at, block(grad_ref, 0, at))
        put(total_ref, 1, at, dq[:width])
        put(swap_first_ref, 0, at, block(grad_ref, 5, at))
        put(swap_first_ref, 1, at, dq[width:])
        for place, grad in ((0, dk), (1, dv)):
            parts = [grad[i * width : (i + 1) * width] for i in range(6)]
            put(halo_grad_ref, place, at, parts[0])
            put(swap_halo_grad_ref, place, at, parts[3])
            put(total_ref, 2 + 2 * place, at, parts[2] + block(grad_ref, 1 + 2 * place, at))
            put(total_ref, 3 + 2 * place, at, parts[1] + block(grad_ref, 2 + 2 * place, at))
            put(swap_first_ref, 2 + place, at, parts[5] + block(grad_ref, 6 + 2 * place, at))
            put(swap_last_ref, place, at, parts[4] + block(grad_ref, 7 + 2 * place, at))

    row = lax.rem(lax.axis_index("row"), 2)
    attend(width, row, halo_ref, swap_halo_ref, own_ref, v_ref, t_ref, swap_k_ref, swap_v_ref,
           swap_qt_ref, bias_ref, store)


def near_kernel(width, own_ref, near_ref, swap_near_ref, out_ref, swap_out_ref):
    for place in range(2):
        rows = slice(place * width, (place + 1) * width)
        at = 2 + 2 * place
        own = own_ref[at * width : (at + 1) * width]
        out_ref[rows] = own + near_ref[rows].astype(F32)
    swap_out_ref[...] = swap_near_ref[: 2 * width].astype(F32)


def add_kernel(a_ref, b_ref, out_ref):
    out_ref[...] = (a_ref[...] + b_ref[...].astype(F32)).astype(BF16)


def gather_kernel(
    width,
    q_ref,
    k_ref,
    gain_q_ref,
    gain_k_ref,
    own_ref,
    near_ref,
    far_ref,
    swap_first_ref,
    swap_near_ref,
    swap_last_ref,
    gated_q_ref,
    gated_k_ref,
    sums_ref,
):
    tokens, feat_dev = q_ref.shape
    mine, theirs = halves(feat_dev // 2)
    near, far = sides(width)

    def term(ref, index):
        return ref[index * width : (index + 1) * width].astype(F32)

    for index, rows in enumerate((near, far)):
        gated_q_ref[rows, mine] = gain_q_ref[:, mine] * term(own_ref, index)
        gated_q_ref[rows, theirs] = gain_q_ref[:, theirs] * term(swap_first_ref, index)
    gated_k_ref[near, mine] = gain_k_ref[:, mine] * term(near_ref, 0)
    gated_k_ref[far, mine] = gain_k_ref[:, mine] * (term(own_ref, 3) + term(far_ref, 0))
    near_dk = term(swap_first_ref, 2) + term(swap_near_ref, 0)
    gated_k_ref[near, theirs] = gain_k_ref[:, theirs] * near_dk
    gated_k_ref[far, theirs] = gain_k_ref[:, theirs] * term(swap_last_ref, 0)
    sums_ref[:tokens] = jnp.sum(q_ref[...].astype(F32) * gated_q_ref[...], -1, keepdims=True)
    sums_ref[tokens:] = jnp.sum(k_ref[...].astype(F32) * gated_k_ref[...], -1, keepdims=True)


def value_kernel(
    width,
    own_ref,
    near_ref,
    far_ref,
    swap_first_ref,
    swap_near_ref,
    swap_last_ref,
    earlier_ref,
    out_ref,
):
    mine, theirs = halves(out_ref.shape[1] // 2)
    near, far = sides(width)

    def term(ref, index):
        return ref[index * width : (index + 1) * width].astype(F32)

    out_ref[near, mine] = term(near_ref, 1).astype(BF16)
    out_ref[far, mine] = (term(own_ref, 5) + term(far_ref, 1)).astype(BF16)
    near_dv = term(swap_first_ref, 3) + term(swap_near_ref, 1)
    out_ref[near, theirs] = near_dv.astype(BF16)
    out_ref[far, theirs] = swap_last_ref[width:]


def finish_kernel(
    q_ref,
    k_ref,
    gated_q_ref,
    gated_k_ref,
    scale_ref,
    sums_ref,
    peer_ref,
    grad_q_out,
    grad_k_out,
    grad_q_ref,
    grad_k_ref,
    sems,
):
    tokens = q_ref.shape[0]
    features = HEADS * HD
    half = tokens // 2
    copies = []
    for base, pre_ref, gated_ref, out_ref, out in (
        (0, q_ref, gated_q_ref, grad_q_ref, grad_q_out),
        (tokens, k_ref, gated_k_ref, grad_k_ref, grad_k_out),
    ):
        for start in (0, half):
            rows, at = (slice(start, start + half), slice(base + start, base + start + half))
            scale = scale_ref[at]
            slope = scale * scale * scale * (sums_ref[at] + peer_ref[at]) / features
            out_ref[rows] = (
                scale * gated_ref[rows] - pre_ref[rows].astype(F32) * slope
            ).astype(BF16)
            copy = pltpu.make_async_copy(out_ref.at[rows], out.at[rows], sems.at[len(copies)])
            copy.start()
            copies.append(copy)
    for copy in copies:
        copy.wait()


def swapped_device(q_pre, k_pre, values, target, gain_q, gain_k, kept):
    frames, rows, width, feat_dev = q_pre.shape
    tokens = rows * width
    half = feat_dev // 2
    row_blocks = lax.axis_size("row")
    inputs = [array.reshape(tokens, feat_dev) for array in (q_pre, k_pre, values, target)]
    inputs += [gain_q, gain_k]
    inputs = [pltpu.with_memory_space_constraint(array, pltpu.HBM) for array in inputs]
    near_pairs = [(r, r + 1) for r in range(0, row_blocks - 1, 2)]
    far_pairs = [(r, r + 1) for r in range(1, row_blocks - 1, 2)]
    near, far = (pairs + [(b, a) for a, b in pairs] for pairs in (near_pairs, far_pairs))
    swap_near = [
        (f * row_blocks + a, (1 - f) * row_blocks + b) for f in range(2) for a, b in near
    ]

    def shape(first, last, dtype=BF16):
        return jax.ShapeDtypeStruct((first, last), dtype)

    block = shape(tokens, feat_dev)
    sum_pair = shape(2 * tokens, 1, F32)
    tokens_half = shape(tokens, half)
    gain = shape(1, feat_dev, F32)
    edge = shape(2 * width, half)
    padded_edge = shape(2 * width + 16, half)
    bias = shape(6 * width, 2 * width, F32)

    q_all, k_all, v_all, t_all, gain_q, gain_k, sums, v_out = call(
        load_kernel,
        (block,) * 4 + (gain,) * 2 + (sum_pair, tokens_half),
        in_specs=[pl.BlockSpec(memory_space=pltpu.HBM)] * 6,
        scratch_shapes=[pltpu.SemaphoreType.DMA((6,))],
    )(*inputs)
    swap_v = lax.ppermute(v_out, "frame", SWAP)
    peer = lax.ppermute(sums, "head", SWAP)
    scale, own_kq, k_out, qt_out, near_out, far_out = call(
        functools.partial(norm_kernel, width),
        (sum_pair, shape(2 * tokens, half), tokens_half, shape(2 * tokens, half), edge, edge),
    )(q_all, k_all, v_all, t_all, sums, peer, gain_q, gain_k)
    near_in = lax.ppermute(near_out, "row", near)
    swap_k = lax.ppermute(k_out, "frame", SWAP)
    swap_qt = lax.ppermute(qt_out, "frame", SWAP)
    far_in = lax.ppermute(far_out, "row", far)
    relay_near = call(functools.partial(relay_near_kernel, width), edge)(swap_k, swap_v, near_in)
    swap_near_in = lax.ppermute(relay_near, "row", near)
    relay_far, near_bias, far_bias = call(
        functools.partial(relay_far_kernel, width),
        (edge, bias, bias),
        in_specs=[pl.BlockSpec(memory_space=pltpu.SMEM)]
        + [pl.BlockSpec(memory_space=pltpu.VMEM)] * 3,
    )(kept.transpose(0, 2, 1), swap_k, swap_v, relay_near)
    swap_far_in = lax.ppermute(relay_far, "row", far)
    shared = (own_kq, v_all, t_all, swap_k, swap_v, swap_qt)
    near_out, swap_near_out, near_terms = call(
        functools.partial(attend_near_kernel, width),
        (padded_edge, padded_edge, shape(10 * width, half, F32)),
        flops=5 * 10**8,
        moved=2 * 10**6,
    )(near_in, swap_near_in, *shared, near_bias, far_in)
    near_total = lax.ppermute(near_out, "row", near)
    swap_near_total = lax.ppermute(swap_near_out, ("frame", "row"), swap_near)
    far_out, swap_far_out, own_total, first_out, last_terms = call(
        functools.partial(attend_far_kernel, width),
        (edge, edge, shape(3 * tokens, half, F32), shape(4 * width, half))
        + (shape(2 * width, half, F32),),
        flops=5 * 10**8,
        moved=2 * 10**6,
    )(far_in, swap_far_in, *shared, far_bias, near_terms)
    far_terms = lax.ppermute(swap_far_out, "row", far)
    swap_first = lax.ppermute(first_out, "frame", SWAP)
    far_total = lax.ppermute(far_out, "row", far)
    near_total, swap_near_total = call(
        functools.partial(near_kernel, width),
        (shape(2 * width, half, F32),) * 2,
        flops=3 * 10**9,
    )(own_total, near_total, swap_near_total)
    last_out = call(add_kernel, edge, flops=1, moved=1)(last_terms, far_terms)
    swap_last = lax.ppermute(last_out, "frame", SWAP)
    terms = (own_total, near_total, far_total, swap_first, swap_near_total, swap_last)
    gated_q, gated_k, sum_terms = call(
        functools.partial(gather_kernel, width),
        (shape(tokens, feat_dev, F32),) * 2 + (sum_pair,),
    )(q_all, k_all, gain_q, gain_k, *terms)
    sum_peer = lax.ppermute(sum_terms, "head", SWAP)
    grad_v = call(functools.partial(value_kernel, width), block)(*terms, sum_terms)
    grad_q, grad_k = call(
        finish_kernel,
        (block, block),
        out_specs=[pl.BlockSpec(memory_space=pltpu.HBM)] * 2,
        scratch_shapes=[pltpu.VMEM((tokens, feat_dev), BF16)] * 2 + [pltpu.SemaphoreType.DMA((4,))],
    )(
        q_all, k_all, gated_q, gated_k, scale, sum_terms, sum_peer
    )
    return tuple(
        array.reshape(frames, rows, width, feat_dev) for array in (grad_q, grad_k, grad_v)
    )


def on_device(q_pre, *rest):
    frames, rows, _, feat_dev = q_pre.shape
    paired = lax.axis_size("frame") == 2 and frames == 1 and rows == 2
    if paired and feat_dev % (2 * HD) == 0:
        return swapped_device(q_pre, *rest)
    return per_device(q_pre, *rest)


def solution(mesh):
    return jax.shard_map(
        on_device,
        mesh=mesh,
        in_specs=(
            P("frame", "row", None, "head"),
            P("frame", "row", None, "head"),
            P("frame", "row", None, "head"),
            P("frame", "row", None, "head"),
            P("head"),
            P("head"),
            P(),
        ),
        out_specs=(
            P("frame", "row", None, "head"),
            P("frame", "row", None, "head"),
            P("frame", "row", None, "head"),
        ),
        check_vma=False,
    )
```

```python
import functools

import jax
import jax.numpy as jnp
from jax import lax
from jax.experimental import pallas as pl
from jax.experimental.pallas import tpu as pltpu
from jax.sharding import PartitionSpec as P

TC = 16
HEADS = 20
HD = 128


norm_eps = 1e-06


def padded(x, sides, width):
    for axis, dim in sides:
        size, length = (lax.axis_size(axis), x.shape[dim])
        up = [(i, (i + 1) % size) for i in range(size - 1)]
        down = [(j, i) for i, j in up]
        last = lax.slice_in_dim(x, length - width, length, axis=dim)
        first = lax.slice_in_dim(x, 0, width, axis=dim)
        before = lax.ppermute(last, axis, up)
        after = lax.ppermute(first, axis, down)
        x = jnp.concatenate([before, x, after], axis=dim)
    return x


def from_behind(value, axis, steps):
    count = lax.axis_size(axis)
    first, last = (max(0, -steps), min(count, count - steps))
    return lax.ppermute(value, axis, [(source, source + steps) for source in range(first, last)])


def query_mask(kept_win, col_tile, tiles):
    near_cols = jnp.abs(col_tile[:, None] - col_tile[None, :]) <= 1
    same_tile = col_tile[:, None] == col_tile[None, :]
    one_hot = col_tile[:, None] == jnp.arange(tiles)[None, :]
    key_kept = jnp.any(one_hot[None, None] & (kept_win[:, :, None, :] > 0), axis=-1)
    centre = (jnp.arange(3)[:, None] == 1) & (jnp.arange(3)[None, :] == 1)
    allowed = near_cols[:, None, None, :] & (
        key_kept[None] | centre[None, :, :, None] & same_tile[:, None, None, :]
    )
    return allowed.reshape(col_tile.shape[0], -1)


def attend_line(query, kv_win, t_line, allowed):
    width, heads_dev, _ = query.shape
    score_scale = HD ** (-0.5)
    key_block = kv_win[0].reshape(9 * width, heads_dev, HD)
    value_block = kv_win[1].reshape(9 * width, heads_dev, HD)
    mask = allowed[None]
    scores = (
        jnp.einsum("qhd,khd->hqk", query, key_block, preferred_element_type=jnp.float32)
        * score_scale
    )
    scores = jnp.where(mask, scores, -jnp.inf)
    row_max = jnp.max(scores, -1, keepdims=True)
    expo = jnp.where(mask, jnp.exp(scores - row_max), 0.0)
    denominator = jnp.sum(expo, -1, keepdims=True)
    probability = expo / denominator
    prob_b = probability.astype(jnp.bfloat16)
    attended = jnp.einsum("hqk,khd->qhd", prob_b, value_block, preferred_element_type=jnp.float32)
    d_out = (attended - t_line.astype(jnp.float32)).astype(jnp.bfloat16)
    delta_sum = jnp.sum(d_out.astype(jnp.float32) * attended, -1).T
    prob_grad = jnp.einsum("qhd,khd->hqk", d_out, value_block, preferred_element_type=jnp.float32)
    score_grad = (probability * (prob_grad - delta_sum[:, :, None]) * score_scale).astype(
        jnp.bfloat16
    )
    dq_line = jnp.einsum("hqk,khd->qhd", score_grad, key_block, preferred_element_type=jnp.float32)
    log_total = row_max[..., 0] + jnp.log(denominator[..., 0])
    return (dq_line.reshape(width, heads_dev * HD), d_out, log_total, delta_sum, prob_b, score_grad)


def per_device(q_pre, k_pre, values, target, gain_q, gain_k, kept):
    frames, rows, width, feat_dev = q_pre.shape
    heads_dev = feat_dev // HD
    tiles = width // TC
    features = HEADS * HD
    line_count = frames * rows
    col_tile = jnp.arange(width) // TC
    q_float = q_pre.astype(jnp.float32)
    k_float = k_pre.astype(jnp.float32)
    square_q, square_k = lax.psum(
        (jnp.sum(q_float * q_float, -1), jnp.sum(k_float * k_float, -1)), "head"
    )
    scale_q = lax.rsqrt(square_q[..., None] / features + norm_eps)
    scale_k = lax.rsqrt(square_k[..., None] / features + norm_eps)
    q_norm = (q_float * scale_q * gain_q).astype(jnp.bfloat16)
    k_norm = (k_float * scale_k * gain_k).astype(jnp.bfloat16)
    kv_ext = padded(jnp.stack([k_norm, values]), (("frame", 1), ("row", 2)), 1)
    frame_at = lax.axis_index("frame")
    row_at = lax.axis_index("row")
    zero = jnp.int32(0)
    kept_pad = jnp.pad(kept, ((1, 1), (1, 1), (0, 0)))
    kept_ext = lax.dynamic_slice(
        kept_pad, (frame_at * frames, row_at * rows, zero), (frames + 2, rows + 2, tiles)
    )
    line_ids = jnp.arange(line_count, dtype=jnp.int32)
    q_lines = q_norm.reshape(line_count, width, heads_dev, HD)
    t_lines = target.reshape(line_count, width, heads_dev, HD)

    def query_window(line):
        f_at = line // rows
        r_at = line % rows
        kv_win = lax.dynamic_slice(
            kv_ext, (zero, f_at, r_at, zero, zero), (2, 3, 3, width, feat_dev)
        )
        kept_win = lax.dynamic_slice(kept_ext, (f_at, r_at, zero), (3, 3, tiles))
        return (f_at, r_at, kv_win, query_mask(kept_win, col_tile, tiles))

    def returned_step(totals, inputs):
        line, query, t_line = inputs
        f_at, r_at, kv_win, allowed = query_window(line)
        dq_line, d_out, log_total, delta_sum, prob_b, score_grad = attend_line(
            query, kv_win, t_line, allowed
        )
        key_grad = jnp.einsum("hqk,qhd->khd", score_grad, query, preferred_element_type=jnp.float32)
        value_grad = jnp.einsum("hqk,qhd->khd", prob_b, d_out, preferred_element_type=jnp.float32)
        both = jnp.stack(
            [key_grad.reshape(3, 3, width, feat_dev), value_grad.reshape(3, 3, width, feat_dev)]
        )
        start = (zero, f_at, r_at, zero, zero)
        current = lax.dynamic_slice(totals, start, (2, 3, 3, width, feat_dev))
        totals = lax.dynamic_update_slice(totals, current + both, start)
        return (totals, dq_line)

    empty = jnp.zeros((2, frames + 2, rows + 2, width, feat_dev), jnp.float32)
    totals, dq_lines = lax.scan(returned_step, empty, (line_ids, q_lines, t_lines))
    inner = totals[:, :, 1 : rows + 1]
    row_edges = (totals[:, :, 0:1], totals[:, :, rows + 1 : rows + 2])
    row_moved = [
        from_behind(row_edges[side], "row", by_value) for side, by_value in ((0, -1), (1, 1))
    ]
    inner = inner.at[:, :, rows - 1 : rows].add(row_moved[0])
    inner = inner.at[:, :, 0:1].add(row_moved[1])
    middle = inner[:, 1 : frames + 1]
    frame_edges = (inner[:, 0:1], inner[:, frames + 1 : frames + 2])
    frame_moved = [
        from_behind(frame_edges[side], "frame", by_value) for side, by_value in ((0, -1), (1, 1))
    ]
    middle = middle.at[:, frames - 1 : frames].add(frame_moved[0])
    middle = middle.at[:, 0:1].add(frame_moved[1])
    dk_norm = middle[0]
    value_total = middle[1]
    dq_norm = dq_lines.reshape(frames, rows, width, feat_dev)
    gated_q = gain_q * dq_norm
    gated_k = gain_k * dk_norm
    sum_q, sum_k = lax.psum(
        (jnp.sum(q_float * gated_q, -1), jnp.sum(k_float * gated_k, -1)), "head"
    )
    grad_q = (scale_q * gated_q - q_float * scale_q**3 * sum_q[..., None] / features).astype(
        jnp.bfloat16
    )
    grad_k = (scale_k * gated_k - k_float * scale_k**3 * sum_k[..., None] / features).astype(
        jnp.bfloat16
    )
    return (grad_q, grad_k, value_total.astype(jnp.bfloat16))


SWAP = [(0, 1), (1, 0)]
F32 = jnp.float32
BF16 = jnp.bfloat16
VMEM_LIMIT = 48 * 1024 * 1024


def call(body, out_shape, flops=10**6, moved=10**6, **kw):
    return pl.pallas_call(
        body,
        out_shape=out_shape,
        compiler_params=pltpu.CompilerParams(vmem_limit_bytes=VMEM_LIMIT),
        cost_estimate=pl.CostEstimate(flops=flops, bytes_accessed=moved, transcendentals=0),
        **kw,
    )


def halves(half):
    frame_at = lax.axis_index("frame")
    mine = pl.multiple_of(frame_at * half, HD)
    theirs = pl.multiple_of((1 - frame_at) * half, HD)
    return (pl.ds(mine, half), pl.ds(theirs, half))


def sides(width):
    odd = lax.rem(lax.axis_index("row"), 2)
    near = pl.multiple_of((1 - odd) * width, width)
    far = pl.multiple_of(odd * width, width)
    return (pl.ds(near, width), pl.ds(far, width))


def load_kernel(
    q_in,
    k_in,
    v_in,
    t_in,
    gain_q_in,
    gain_k_in,
    q_ref,
    k_ref,
    v_ref,
    t_ref,
    gain_q_ref,
    gain_k_ref,
    sums_ref,
    v_out_ref,
    sems,
):
    tokens, feat_dev = q_ref.shape
    _, theirs = halves(feat_dev // 2)
    pairs = (
        (q_in, q_ref),
        (k_in, k_ref),
        (v_in, v_ref),
        (t_in, t_ref),
        (gain_q_in, gain_q_ref.at[0]),
        (gain_k_in, gain_k_ref.at[0]),
    )
    copies = [pltpu.make_async_copy(a, b, sems.at[i]) for i, (a, b) in enumerate(pairs)]
    for copy in copies:
        copy.start()
    copies[0].wait()
    q_float = q_ref[...].astype(F32)
    sums_ref[:tokens] = jnp.sum(q_float * q_float, -1, keepdims=True)
    copies[1].wait()
    k_float = k_ref[...].astype(F32)
    sums_ref[tokens:] = jnp.sum(k_float * k_float, -1, keepdims=True)
    copies[2].wait()
    v_out_ref[...] = v_ref[:, theirs]
    for copy in copies[3:]:
        copy.wait()


def norm_kernel(
    width,
    q_ref,
    k_ref,
    v_ref,
    t_ref,
    sums_ref,
    peer_ref,
    gain_q_ref,
    gain_k_ref,
    scale_ref,
    own_ref,
    k_out_ref,
    qt_out_ref,
    near_ref,
    far_ref,
):
    tokens, feat_dev = q_ref.shape
    features = HEADS * HD
    mine, theirs = halves(feat_dev // 2)
    near, far = sides(width)
    scale = lax.rsqrt((sums_ref[...] + peer_ref[...]) / features + norm_eps)
    scale_ref[...] = scale
    scale_q, scale_k = (scale[:tokens], scale[tokens:])

    def normed(ref, part, scales, gain_ref):
        return (ref[:, part].astype(F32) * scales * gain_ref[:, part]).astype(BF16)

    k_out_ref[...] = normed(k_ref, theirs, scale_k, gain_k_ref)
    qt_out_ref[:tokens] = normed(q_ref, theirs, scale_q, gain_q_ref)
    qt_out_ref[tokens:] = t_ref[:, theirs]
    own_ref[:tokens] = normed(k_ref, mine, scale_k, gain_k_ref)
    own_ref[tokens:] = normed(q_ref, mine, scale_q, gain_q_ref)
    for out_ref, rows in ((near_ref, near), (far_ref, far)):
        out_ref[:width] = own_ref[rows]
        out_ref[width:] = v_ref[rows, mine]


def relay_near_kernel(width, k_ref, v_ref, earlier_ref, out_ref):
    near, _ = sides(width)
    out_ref[:width] = k_ref[near]
    out_ref[width:] = v_ref[near]


def relay_far_kernel(width, kept_ref, k_ref, v_ref, earlier_ref, out_ref, near_ref, far_ref):
    _, far = sides(width)
    out_ref[:width] = k_ref[far]
    out_ref[width:] = v_ref[far]
    rows = 2
    count = kept_ref.shape[2]
    tiles = width // TC
    frame_at = lax.axis_index("frame")
    first_row = lax.axis_index("row") * rows
    odd = lax.rem(lax.axis_index("row"), 2)
    query_at = lax.broadcasted_iota(jnp.int32, (TC, near_ref.shape[1]), 1)
    query_tile = lax.rem(query_at, width) // TC
    for out_ref, row in ((near_ref, 1 - odd), (far_ref, odd)):
        for part in range(2):
            frame = frame_at if part == 0 else 1 - frame_at
            for slot, place in enumerate((3 * row - 1, row, 1 - row)):
                at = first_row + place
                inside = (at >= 0) & (at < count)
                at = jnp.clip(at, 0, count - 1)
                for tile in range(tiles):
                    value = jnp.where(inside, kept_ref[frame, tile, at], 0)
                    allowed = (jnp.abs(query_tile - tile) <= 1) & (value > 0)
                    if slot == 1:
                        allowed |= (query_tile == tile) & (query_at // width == part)
                    here = ((part * 3 + slot) * tiles + tile) * TC
                    out_ref[here : here + TC] = jnp.where(allowed, 0.0, -1e30)


def attend(width, row, halo_ref, swap_halo_ref, own_ref, v_ref, t_ref, swap_k_ref, swap_v_ref,
           swap_qt_ref, bias_ref, store):
    tokens, half = swap_k_ref.shape
    score_scale = HD ** (-0.5)
    mine = lax.axis_index("frame") * half
    bias = bias_ref[...]
    own_at = pl.multiple_of(row * width, width)
    other_at = pl.multiple_of((1 - row) * width, width)
    rows = (pl.ds(own_at, width), pl.ds(other_at, width))
    query_at = pl.ds(pl.multiple_of(tokens + own_at, width), width)

    def product(a, b, a_dim, b_dim):
        return lax.dot_general(a, b, (((a_dim,), (b_dim,)), ((), ())), preferred_element_type=F32)

    def load(head):
        at = slice(head * HD, (head + 1) * HD)
        mine_at = pl.ds(pl.multiple_of(mine + head * HD, HD), HD)
        query = jnp.concatenate([own_ref[query_at, at], swap_qt_ref[rows[0], at]], 0)
        target = jnp.concatenate([t_ref[rows[0], mine_at], swap_qt_ref[query_at, at]], 0)
        key = jnp.concatenate(
            [halo_ref[:width, at]]
            + [own_ref[r, at] for r in rows]
            + [swap_halo_ref[:width, at]]
            + [swap_k_ref[r, at] for r in rows],
            0,
        )
        value = jnp.concatenate(
            [halo_ref[width:, at]]
            + [v_ref[r, mine_at] for r in rows]
            + [swap_halo_ref[width:, at]]
            + [swap_v_ref[r, at] for r in rows],
            0,
        )
        return (query, target, key, value)

    def weights(query, key):
        scores = product(key, query, 1, 1) * score_scale + bias
        expo = jnp.exp(scores - jnp.max(scores, 0, keepdims=True))
        return expo * (1.0 / jnp.sum(expo, 0, keepdims=True))

    def output_grad(prob_b, target, value):
        attended = product(value, prob_b, 0, 0)
        d_out = (attended - target.astype(F32).T).astype(BF16)
        return (d_out, jnp.sum(d_out.astype(F32) * attended, 0, keepdims=True))

    def score_grads(probability, d_out, delta_sum, value):
        prob_grad = product(value, d_out, 1, 0)
        return (probability * (prob_grad - delta_sum) * score_scale).astype(BF16)

    def grads(score_grad, prob_b, d_out, query, key):
        dq = product(key, score_grad, 0, 0).T
        dk = product(score_grad, query, 1, 0)
        return (dq, dk, product(prob_b, d_out, 1, 1))

    heads = range(half // HD)
    loaded = [load(head) for head in heads]
    probability = [weights(query, key) for query, _, key, _ in loaded]
    prob_b = [p.astype(BF16) for p in probability]
    outs = [output_grad(p, t, v) for p, (_, t, _, v) in zip(prob_b, loaded)]
    score_grad = [score_grads(p, *o, x[3]) for p, o, x in zip(probability, outs, loaded)]
    for head in heads:
        query, _, key, _ = loaded[head]
        at = slice(head * HD, (head + 1) * HD)
        store(at, *grads(score_grad[head], prob_b[head], outs[head][0], query, key))


def attend_near_kernel(
    width,
    halo_ref,
    swap_halo_ref,
    own_ref,
    v_ref,
    t_ref,
    swap_k_ref,
    swap_v_ref,
    swap_qt_ref,
    bias_ref,
    earlier_ref,
    halo_grad_ref,
    swap_halo_grad_ref,
    grad_ref,
):
    def store(at, dq, dk, dv):
        for place, grad in ((0, dk), (1, dv)):
            to = slice(place * width, (place + 1) * width)
            halo_grad_ref[to, at] = grad[:width].astype(BF16)
            swap_halo_grad_ref[to, at] = grad[3 * width : 4 * width].astype(BF16)
            for part in range(2):
                start = (5 * part + 1 + 2 * place) * width
                first = (3 * part + 1) * width
                grad_ref[start : start + 2 * width, at] = grad[first : first + 2 * width]
        for part in range(2):
            start = 5 * part * width
            grad_ref[start : start + width, at] = dq[part * width : (part + 1) * width]

    row = 1 - lax.rem(lax.axis_index("row"), 2)
    attend(width, row, halo_ref, swap_halo_ref, own_ref, v_ref, t_ref, swap_k_ref, swap_v_ref,
           swap_qt_ref, bias_ref, store)


def attend_far_kernel(
    width,
    halo_ref,
    swap_halo_ref,
    own_ref,
    v_ref,
    t_ref,
    swap_k_ref,
    swap_v_ref,
    swap_qt_ref,
    bias_ref,
    grad_ref,
    halo_grad_ref,
    swap_halo_grad_ref,
    total_ref,
    swap_first_ref,
    swap_last_ref,
):
    def block(ref, index, at):
        return ref[index * width : (index + 1) * width, at]

    def put(ref, index, at, value):
        ref[index * width : (index + 1) * width, at] = value.astype(ref.dtype)

    def store(at, dq, dk, dv):
        put(total_ref, 0, at, block(grad_ref, 0, at))
        put(total_ref, 1, at, dq[:width])
        put(swap_first_ref, 0, at, block(grad_ref, 5, at))
        put(swap_first_ref, 1, at, dq[width:])
        for place, grad in ((0, dk), (1, dv)):
            parts = [grad[i * width : (i + 1) * width] for i in range(6)]
            put(halo_grad_ref, place, at, parts[0])
            put(swap_halo_grad_ref, place, at, parts[3])
            put(total_ref, 2 + 2 * place, at, parts[2] + block(grad_ref, 1 + 2 * place, at))
            put(total_ref, 3 + 2 * place, at, parts[1] + block(grad_ref, 2 + 2 * place, at))
            put(swap_first_ref, 2 + place, at, parts[5] + block(grad_ref, 6 + 2 * place, at))
            put(swap_last_ref, place, at, parts[4] + block(grad_ref, 7 + 2 * place, at))

    row = lax.rem(lax.axis_index("row"), 2)
    attend(width, row, halo_ref, swap_halo_ref, own_ref, v_ref, t_ref, swap_k_ref, swap_v_ref,
           swap_qt_ref, bias_ref, store)


def near_kernel(width, own_ref, near_ref, swap_near_ref, out_ref, swap_out_ref):
    for place in range(2):
        rows = slice(place * width, (place + 1) * width)
        at = 2 + 2 * place
        own = own_ref[at * width : (at + 1) * width]
        out_ref[rows] = own + near_ref[rows].astype(F32)
    swap_out_ref[...] = swap_near_ref[: 2 * width].astype(F32)


def add_kernel(a_ref, b_ref, out_ref):
    out_ref[...] = (a_ref[...] + b_ref[...].astype(F32)).astype(BF16)


def gather_q_kernel(
    width, q_ref, gain_ref, own_ref, swap_first_ref, earlier_ref, gated_ref, sums_ref
):
    mine, theirs = halves(q_ref.shape[1] // 2)
    for index, rows in enumerate(sides(width)):
        at = slice(index * width, (index + 1) * width)
        gated_ref[rows, mine] = gain_ref[:, mine] * own_ref[at]
        gated_ref[rows, theirs] = gain_ref[:, theirs] * swap_first_ref[at].astype(F32)
    sums_ref[...] = jnp.sum(q_ref[...].astype(F32) * gated_ref[...], -1, keepdims=True)


def gather_k_kernel(
    width,
    k_ref,
    gain_ref,
    own_ref,
    near_ref,
    far_ref,
    swap_first_ref,
    swap_near_ref,
    swap_last_ref,
    sum_q_ref,
    gated_ref,
    sums_ref,
):
    tokens = k_ref.shape[0]
    mine, theirs = halves(k_ref.shape[1] // 2)
    near, far = sides(width)

    def term(ref, index):
        return ref[index * width : (index + 1) * width].astype(F32)

    gated_ref[near, mine] = gain_ref[:, mine] * term(near_ref, 0)
    gated_ref[far, mine] = gain_ref[:, mine] * (term(own_ref, 3) + term(far_ref, 0))
    near_dk = term(swap_first_ref, 2) + term(swap_near_ref, 0)
    gated_ref[near, theirs] = gain_ref[:, theirs] * near_dk
    gated_ref[far, theirs] = gain_ref[:, theirs] * term(swap_last_ref, 0)
    sums_ref[:tokens] = sum_q_ref[...]
    sums_ref[tokens:] = jnp.sum(k_ref[...].astype(F32) * gated_ref[...], -1, keepdims=True)


def value_kernel(
    width,
    own_ref,
    near_ref,
    far_ref,
    swap_first_ref,
    swap_near_ref,
    swap_last_ref,
    earlier_ref,
    out_ref,
):
    mine, theirs = halves(out_ref.shape[1] // 2)
    near, far = sides(width)

    def term(ref, index):
        return ref[index * width : (index + 1) * width].astype(F32)

    out_ref[near, mine] = term(near_ref, 1).astype(BF16)
    out_ref[far, mine] = (term(own_ref, 5) + term(far_ref, 1)).astype(BF16)
    near_dv = term(swap_first_ref, 3) + term(swap_near_ref, 1)
    out_ref[near, theirs] = near_dv.astype(BF16)
    out_ref[far, theirs] = swap_last_ref[width:]


def finish_kernel(
    q_ref,
    k_ref,
    gated_q_ref,
    gated_k_ref,
    scale_ref,
    sums_ref,
    peer_ref,
    grad_q_out,
    grad_k_out,
    grad_q_ref,
    grad_k_ref,
    sems,
):
    tokens = q_ref.shape[0]
    features = HEADS * HD
    half = tokens // 2
    copies = []
    for base, pre_ref, gated_ref, out_ref, out in (
        (0, q_ref, gated_q_ref, grad_q_ref, grad_q_out),
        (tokens, k_ref, gated_k_ref, grad_k_ref, grad_k_out),
    ):
        for start in (0, half):
            rows, at = (slice(start, start + half), slice(base + start, base + start + half))
            scale = scale_ref[at]
            slope = scale * scale * scale * (sums_ref[at] + peer_ref[at]) / features
            out_ref[rows] = (
                scale * gated_ref[rows] - pre_ref[rows].astype(F32) * slope
            ).astype(BF16)
            copy = pltpu.make_async_copy(out_ref.at[rows], out.at[rows], sems.at[len(copies)])
            copy.start()
            copies.append(copy)
    for copy in copies:
        copy.wait()


def swapped_device(q_pre, k_pre, values, target, gain_q, gain_k, kept):
    frames, rows, width, feat_dev = q_pre.shape
    tokens = rows * width
    half = feat_dev // 2
    row_blocks = lax.axis_size("row")
    inputs = [array.reshape(tokens, feat_dev) for array in (q_pre, k_pre, values, target)]
    inputs += [gain_q, gain_k]
    inputs = [pltpu.with_memory_space_constraint(array, pltpu.HBM) for array in inputs]
    near_pairs = [(r, r + 1) for r in range(0, row_blocks - 1, 2)]
    far_pairs = [(r, r + 1) for r in range(1, row_blocks - 1, 2)]
    near, far = (pairs + [(b, a) for a, b in pairs] for pairs in (near_pairs, far_pairs))
    swap_near = [
        (f * row_blocks + a, (1 - f) * row_blocks + b) for f in range(2) for a, b in near
    ]

    def shape(first, last, dtype=BF16):
        return jax.ShapeDtypeStruct((first, last), dtype)

    block = shape(tokens, feat_dev)
    sum_pair = shape(2 * tokens, 1, F32)
    tokens_half = shape(tokens, half)
    gain = shape(1, feat_dev, F32)
    edge = shape(2 * width, half)
    padded_edge = shape(2 * width + 16, half)
    bias = shape(6 * width, 2 * width, F32)

    q_all, k_all, v_all, t_all, gain_q, gain_k, sums, v_out = call(
        load_kernel,
        (block,) * 4 + (gain,) * 2 + (sum_pair, tokens_half),
        in_specs=[pl.BlockSpec(memory_space=pltpu.HBM)] * 6,
        scratch_shapes=[pltpu.SemaphoreType.DMA((6,))],
    )(*inputs)
    swap_v = lax.ppermute(v_out, "frame", SWAP)
    peer = lax.ppermute(sums, "head", SWAP)
    scale, own_kq, k_out, qt_out, near_out, far_out = call(
        functools.partial(norm_kernel, width),
        (sum_pair, shape(2 * tokens, half), tokens_half, shape(2 * tokens, half), edge, edge),
    )(q_all, k_all, v_all, t_all, sums, peer, gain_q, gain_k)
    near_in = lax.ppermute(near_out, "row", near)
    swap_k = lax.ppermute(k_out, "frame", SWAP)
    swap_qt = lax.ppermute(qt_out, "frame", SWAP)
    far_in = lax.ppermute(far_out, "row", far)
    relay_near = call(functools.partial(relay_near_kernel, width), edge)(swap_k, swap_v, near_in)
    swap_near_in = lax.ppermute(relay_near, "row", near)
    relay_far, near_bias, far_bias = call(
        functools.partial(relay_far_kernel, width),
        (edge, bias, bias),
        in_specs=[pl.BlockSpec(memory_space=pltpu.SMEM)]
        + [pl.BlockSpec(memory_space=pltpu.VMEM)] * 3,
    )(kept.transpose(0, 2, 1), swap_k, swap_v, relay_near)
    swap_far_in = lax.ppermute(relay_far, "row", far)
    shared = (own_kq, v_all, t_all, swap_k, swap_v, swap_qt)
    near_out, swap_near_out, near_terms = call(
        functools.partial(attend_near_kernel, width),
        (padded_edge, padded_edge, shape(10 * width, half, F32)),
        flops=5 * 10**8,
        moved=2 * 10**6,
    )(near_in, swap_near_in, *shared, near_bias, far_in)
    near_total = lax.ppermute(near_out, "row", near)
    swap_near_total = lax.ppermute(swap_near_out, ("frame", "row"), swap_near)
    far_out, swap_far_out, own_total, first_out, last_terms = call(
        functools.partial(attend_far_kernel, width),
        (edge, edge, shape(3 * tokens, half, F32), shape(4 * width, half))
        + (shape(2 * width, half, F32),),
        flops=5 * 10**8,
        moved=2 * 10**6,
    )(far_in, swap_far_in, *shared, far_bias, near_terms)
    far_terms = lax.ppermute(swap_far_out, "row", far)
    swap_first = lax.ppermute(first_out, "frame", SWAP)
    far_total = lax.ppermute(far_out, "row", far)
    near_total, swap_near_total = call(
        functools.partial(near_kernel, width),
        (shape(2 * width, half, F32),) * 2,
        flops=3 * 10**9,
    )(own_total, near_total, swap_near_total)
    last_out = call(add_kernel, edge, flops=1, moved=1)(last_terms, far_terms)
    swap_last = lax.ppermute(last_out, "frame", SWAP)
    terms = (own_total, near_total, far_total, swap_first, swap_near_total, swap_last)
    gated = shape(tokens, feat_dev, F32)
    gated_q, sum_q = call(
        functools.partial(gather_q_kernel, width),
        (gated, shape(tokens, 1, F32)),
        flops=3 * 10**9,
    )(q_all, gain_q, own_total, swap_first, near_total)
    gated_k, sum_terms = call(functools.partial(gather_k_kernel, width), (gated, sum_pair))(
        k_all, gain_k, *terms, sum_q
    )
    sum_peer = lax.ppermute(sum_terms, "head", SWAP)
    grad_v = call(functools.partial(value_kernel, width), block)(*terms, sum_terms)
    grad_q, grad_k = call(
        finish_kernel,
        (block, block),
        out_specs=[pl.BlockSpec(memory_space=pltpu.HBM)] * 2,
        scratch_shapes=[pltpu.VMEM((tokens, feat_dev), BF16)] * 2 + [pltpu.SemaphoreType.DMA((4,))],
    )(
        q_all, k_all, gated_q, gated_k, scale, sum_terms, sum_peer
    )
    return tuple(
        array.reshape(frames, rows, width, feat_dev) for array in (grad_q, grad_k, grad_v)
    )


def on_device(q_pre, *rest):
    frames, rows, _, feat_dev = q_pre.shape
    paired = lax.axis_size("frame") == 2 and frames == 1 and rows == 2
    if paired and feat_dev % (2 * HD) == 0:
        return swapped_device(q_pre, *rest)
    return per_device(q_pre, *rest)


def solution(mesh):
    return jax.shard_map(
        on_device,
        mesh=mesh,
        in_specs=(
            P("frame", "row", None, "head"),
            P("frame", "row", None, "head"),
            P("frame", "row", None, "head"),
            P("frame", "row", None, "head"),
            P("head"),
            P("head"),
            P(),
        ),
        out_specs=(
            P("frame", "row", None, "head"),
            P("frame", "row", None, "head"),
            P("frame", "row", None, "head"),
        ),
        check_vma=False,
    )
```

```python
import functools

import jax
import jax.numpy as jnp
from jax import lax
from jax.experimental import pallas as pl
from jax.experimental.pallas import tpu as pltpu
from jax.sharding import PartitionSpec as P

TC = 16
HEADS = 20
HD = 128


norm_eps = 1e-06


def padded(x, sides, width):
    for axis, dim in sides:
        size, length = (lax.axis_size(axis), x.shape[dim])
        up = [(i, (i + 1) % size) for i in range(size - 1)]
        down = [(j, i) for i, j in up]
        last = lax.slice_in_dim(x, length - width, length, axis=dim)
        first = lax.slice_in_dim(x, 0, width, axis=dim)
        before = lax.ppermute(last, axis, up)
        after = lax.ppermute(first, axis, down)
        x = jnp.concatenate([before, x, after], axis=dim)
    return x


def from_behind(value, axis, steps):
    count = lax.axis_size(axis)
    first, last = (max(0, -steps), min(count, count - steps))
    return lax.ppermute(value, axis, [(source, source + steps) for source in range(first, last)])


def query_mask(kept_win, col_tile, tiles):
    near_cols = jnp.abs(col_tile[:, None] - col_tile[None, :]) <= 1
    same_tile = col_tile[:, None] == col_tile[None, :]
    one_hot = col_tile[:, None] == jnp.arange(tiles)[None, :]
    key_kept = jnp.any(one_hot[None, None] & (kept_win[:, :, None, :] > 0), axis=-1)
    centre = (jnp.arange(3)[:, None] == 1) & (jnp.arange(3)[None, :] == 1)
    allowed = near_cols[:, None, None, :] & (
        key_kept[None] | centre[None, :, :, None] & same_tile[:, None, None, :]
    )
    return allowed.reshape(col_tile.shape[0], -1)


def attend_line(query, kv_win, t_line, allowed):
    width, heads_dev, _ = query.shape
    score_scale = HD ** (-0.5)
    key_block = kv_win[0].reshape(9 * width, heads_dev, HD)
    value_block = kv_win[1].reshape(9 * width, heads_dev, HD)
    mask = allowed[None]
    scores = (
        jnp.einsum("qhd,khd->hqk", query, key_block, preferred_element_type=jnp.float32)
        * score_scale
    )
    scores = jnp.where(mask, scores, -jnp.inf)
    row_max = jnp.max(scores, -1, keepdims=True)
    expo = jnp.where(mask, jnp.exp(scores - row_max), 0.0)
    denominator = jnp.sum(expo, -1, keepdims=True)
    probability = expo / denominator
    prob_b = probability.astype(jnp.bfloat16)
    attended = jnp.einsum("hqk,khd->qhd", prob_b, value_block, preferred_element_type=jnp.float32)
    d_out = (attended - t_line.astype(jnp.float32)).astype(jnp.bfloat16)
    delta_sum = jnp.sum(d_out.astype(jnp.float32) * attended, -1).T
    prob_grad = jnp.einsum("qhd,khd->hqk", d_out, value_block, preferred_element_type=jnp.float32)
    score_grad = (probability * (prob_grad - delta_sum[:, :, None]) * score_scale).astype(
        jnp.bfloat16
    )
    dq_line = jnp.einsum("hqk,khd->qhd", score_grad, key_block, preferred_element_type=jnp.float32)
    log_total = row_max[..., 0] + jnp.log(denominator[..., 0])
    return (dq_line.reshape(width, heads_dev * HD), d_out, log_total, delta_sum, prob_b, score_grad)


def per_device(q_pre, k_pre, values, target, gain_q, gain_k, kept):
    frames, rows, width, feat_dev = q_pre.shape
    heads_dev = feat_dev // HD
    tiles = width // TC
    features = HEADS * HD
    line_count = frames * rows
    col_tile = jnp.arange(width) // TC
    q_float = q_pre.astype(jnp.float32)
    k_float = k_pre.astype(jnp.float32)
    square_q, square_k = lax.psum(
        (jnp.sum(q_float * q_float, -1), jnp.sum(k_float * k_float, -1)), "head"
    )
    scale_q = lax.rsqrt(square_q[..., None] / features + norm_eps)
    scale_k = lax.rsqrt(square_k[..., None] / features + norm_eps)
    q_norm = (q_float * scale_q * gain_q).astype(jnp.bfloat16)
    k_norm = (k_float * scale_k * gain_k).astype(jnp.bfloat16)
    kv_ext = padded(jnp.stack([k_norm, values]), (("frame", 1), ("row", 2)), 1)
    frame_at = lax.axis_index("frame")
    row_at = lax.axis_index("row")
    zero = jnp.int32(0)
    kept_pad = jnp.pad(kept, ((1, 1), (1, 1), (0, 0)))
    kept_ext = lax.dynamic_slice(
        kept_pad, (frame_at * frames, row_at * rows, zero), (frames + 2, rows + 2, tiles)
    )
    line_ids = jnp.arange(line_count, dtype=jnp.int32)
    q_lines = q_norm.reshape(line_count, width, heads_dev, HD)
    t_lines = target.reshape(line_count, width, heads_dev, HD)

    def query_window(line):
        f_at = line // rows
        r_at = line % rows
        kv_win = lax.dynamic_slice(
            kv_ext, (zero, f_at, r_at, zero, zero), (2, 3, 3, width, feat_dev)
        )
        kept_win = lax.dynamic_slice(kept_ext, (f_at, r_at, zero), (3, 3, tiles))
        return (f_at, r_at, kv_win, query_mask(kept_win, col_tile, tiles))

    def returned_step(totals, inputs):
        line, query, t_line = inputs
        f_at, r_at, kv_win, allowed = query_window(line)
        dq_line, d_out, log_total, delta_sum, prob_b, score_grad = attend_line(
            query, kv_win, t_line, allowed
        )
        key_grad = jnp.einsum("hqk,qhd->khd", score_grad, query, preferred_element_type=jnp.float32)
        value_grad = jnp.einsum("hqk,qhd->khd", prob_b, d_out, preferred_element_type=jnp.float32)
        both = jnp.stack(
            [key_grad.reshape(3, 3, width, feat_dev), value_grad.reshape(3, 3, width, feat_dev)]
        )
        start = (zero, f_at, r_at, zero, zero)
        current = lax.dynamic_slice(totals, start, (2, 3, 3, width, feat_dev))
        totals = lax.dynamic_update_slice(totals, current + both, start)
        return (totals, dq_line)

    empty = jnp.zeros((2, frames + 2, rows + 2, width, feat_dev), jnp.float32)
    totals, dq_lines = lax.scan(returned_step, empty, (line_ids, q_lines, t_lines))
    inner = totals[:, :, 1 : rows + 1]
    row_edges = (totals[:, :, 0:1], totals[:, :, rows + 1 : rows + 2])
    row_moved = [
        from_behind(row_edges[side], "row", by_value) for side, by_value in ((0, -1), (1, 1))
    ]
    inner = inner.at[:, :, rows - 1 : rows].add(row_moved[0])
    inner = inner.at[:, :, 0:1].add(row_moved[1])
    middle = inner[:, 1 : frames + 1]
    frame_edges = (inner[:, 0:1], inner[:, frames + 1 : frames + 2])
    frame_moved = [
        from_behind(frame_edges[side], "frame", by_value) for side, by_value in ((0, -1), (1, 1))
    ]
    middle = middle.at[:, frames - 1 : frames].add(frame_moved[0])
    middle = middle.at[:, 0:1].add(frame_moved[1])
    dk_norm = middle[0]
    value_total = middle[1]
    dq_norm = dq_lines.reshape(frames, rows, width, feat_dev)
    gated_q = gain_q * dq_norm
    gated_k = gain_k * dk_norm
    sum_q, sum_k = lax.psum(
        (jnp.sum(q_float * gated_q, -1), jnp.sum(k_float * gated_k, -1)), "head"
    )
    grad_q = (scale_q * gated_q - q_float * scale_q**3 * sum_q[..., None] / features).astype(
        jnp.bfloat16
    )
    grad_k = (scale_k * gated_k - k_float * scale_k**3 * sum_k[..., None] / features).astype(
        jnp.bfloat16
    )
    return (grad_q, grad_k, value_total.astype(jnp.bfloat16))


SWAP = [(0, 1), (1, 0)]
F32 = jnp.float32
BF16 = jnp.bfloat16
VMEM_LIMIT = 48 * 1024 * 1024


def call(body, out_shape, flops=10**6, moved=10**6, **kw):
    return pl.pallas_call(
        body,
        out_shape=out_shape,
        compiler_params=pltpu.CompilerParams(vmem_limit_bytes=VMEM_LIMIT),
        cost_estimate=pl.CostEstimate(flops=flops, bytes_accessed=moved, transcendentals=0),
        **kw,
    )


def halves(half):
    frame_at = lax.axis_index("frame")
    mine = pl.multiple_of(frame_at * half, HD)
    theirs = pl.multiple_of((1 - frame_at) * half, HD)
    return (pl.ds(mine, half), pl.ds(theirs, half))


def sides(width):
    odd = lax.rem(lax.axis_index("row"), 2)
    near = pl.multiple_of((1 - odd) * width, width)
    far = pl.multiple_of(odd * width, width)
    return (pl.ds(near, width), pl.ds(far, width))


def load_kernel(
    q_in,
    k_in,
    v_in,
    t_in,
    gain_q_in,
    gain_k_in,
    q_ref,
    k_ref,
    v_ref,
    t_ref,
    gain_q_ref,
    gain_k_ref,
    sums_ref,
    v_out_ref,
    sems,
):
    tokens, feat_dev = q_ref.shape
    _, theirs = halves(feat_dev // 2)
    pairs = (
        (q_in, q_ref),
        (k_in, k_ref),
        (v_in, v_ref),
        (t_in, t_ref),
        (gain_q_in, gain_q_ref.at[0]),
        (gain_k_in, gain_k_ref.at[0]),
    )
    copies = [pltpu.make_async_copy(a, b, sems.at[i]) for i, (a, b) in enumerate(pairs)]
    for copy in copies:
        copy.start()
    copies[0].wait()
    q_float = q_ref[...].astype(F32)
    sums_ref[:tokens] = jnp.sum(q_float * q_float, -1, keepdims=True)
    copies[1].wait()
    k_float = k_ref[...].astype(F32)
    sums_ref[tokens:] = jnp.sum(k_float * k_float, -1, keepdims=True)
    copies[2].wait()
    v_out_ref[...] = v_ref[:, theirs]
    for copy in copies[3:]:
        copy.wait()


def norm_kernel(
    width,
    q_ref,
    k_ref,
    v_ref,
    t_ref,
    sums_ref,
    peer_ref,
    gain_q_ref,
    gain_k_ref,
    scale_ref,
    own_ref,
    k_out_ref,
    qt_out_ref,
    near_ref,
    far_ref,
):
    tokens, feat_dev = q_ref.shape
    features = HEADS * HD
    mine, theirs = halves(feat_dev // 2)
    near, far = sides(width)
    scale = lax.rsqrt((sums_ref[...] + peer_ref[...]) / features + norm_eps)
    scale_ref[...] = scale
    scale_q, scale_k = (scale[:tokens], scale[tokens:])

    def normed(ref, part, scales, gain_ref):
        return (ref[:, part].astype(F32) * scales * gain_ref[:, part]).astype(BF16)

    k_out_ref[...] = normed(k_ref, theirs, scale_k, gain_k_ref)
    qt_out_ref[:tokens] = normed(q_ref, theirs, scale_q, gain_q_ref)
    qt_out_ref[tokens:] = t_ref[:, theirs]
    own_ref[:tokens] = normed(k_ref, mine, scale_k, gain_k_ref)
    own_ref[tokens:] = normed(q_ref, mine, scale_q, gain_q_ref)
    for out_ref, rows in ((near_ref, near), (far_ref, far)):
        out_ref[:width] = own_ref[rows]
        out_ref[width:] = v_ref[rows, mine]


def relay_near_kernel(width, k_ref, v_ref, earlier_ref, out_ref):
    near, _ = sides(width)
    out_ref[:width] = k_ref[near]
    out_ref[width:] = v_ref[near]


def relay_far_kernel(width, kept_ref, k_ref, v_ref, earlier_ref, out_ref, near_ref, far_ref):
    _, far = sides(width)
    out_ref[:width] = k_ref[far]
    out_ref[width:] = v_ref[far]
    rows = 2
    count = kept_ref.shape[2]
    tiles = width // TC
    frame_at = lax.axis_index("frame")
    first_row = lax.axis_index("row") * rows
    odd = lax.rem(lax.axis_index("row"), 2)
    query_at = lax.broadcasted_iota(jnp.int32, (TC, near_ref.shape[1]), 1)
    query_tile = lax.rem(query_at, width) // TC
    for out_ref, row in ((near_ref, 1 - odd), (far_ref, odd)):
        for part in range(2):
            frame = frame_at if part == 0 else 1 - frame_at
            for slot, place in enumerate((3 * row - 1, row, 1 - row)):
                at = first_row + place
                inside = (at >= 0) & (at < count)
                at = jnp.clip(at, 0, count - 1)
                for tile in range(tiles):
                    value = jnp.where(inside, kept_ref[frame, tile, at], 0)
                    allowed = (jnp.abs(query_tile - tile) <= 1) & (value > 0)
                    if slot == 1:
                        allowed |= (query_tile == tile) & (query_at // width == part)
                    here = ((part * 3 + slot) * tiles + tile) * TC
                    out_ref[here : here + TC] = jnp.where(allowed, 0.0, -1e30)


def attend(width, row, halo_ref, swap_halo_ref, own_ref, v_ref, t_ref, swap_k_ref, swap_v_ref,
           swap_qt_ref, bias_ref, store):
    tokens, half = swap_k_ref.shape
    score_scale = HD ** (-0.5)
    mine = lax.axis_index("frame") * half
    bias = bias_ref[...]
    own_at = pl.multiple_of(row * width, width)
    other_at = pl.multiple_of((1 - row) * width, width)
    rows = (pl.ds(own_at, width), pl.ds(other_at, width))
    query_at = pl.ds(pl.multiple_of(tokens + own_at, width), width)

    def product(a, b, a_dim, b_dim):
        return lax.dot_general(a, b, (((a_dim,), (b_dim,)), ((), ())), preferred_element_type=F32)

    def load(head):
        at = slice(head * HD, (head + 1) * HD)
        mine_at = pl.ds(pl.multiple_of(mine + head * HD, HD), HD)
        query = jnp.concatenate([own_ref[query_at, at], swap_qt_ref[rows[0], at]], 0)
        target = jnp.concatenate([t_ref[rows[0], mine_at], swap_qt_ref[query_at, at]], 0)
        key = jnp.concatenate(
            [halo_ref[:width, at]]
            + [own_ref[r, at] for r in rows]
            + [swap_halo_ref[:width, at]]
            + [swap_k_ref[r, at] for r in rows],
            0,
        )
        value = jnp.concatenate(
            [halo_ref[width:, at]]
            + [v_ref[r, mine_at] for r in rows]
            + [swap_halo_ref[width:, at]]
            + [swap_v_ref[r, at] for r in rows],
            0,
        )
        return (query, target, key, value)

    def weights(query, key):
        scores = product(key, query, 1, 1) * score_scale + bias
        expo = jnp.exp(scores - jnp.max(scores, 0, keepdims=True))
        return expo * (1.0 / jnp.sum(expo, 0, keepdims=True))

    def output_grad(prob_b, target, value):
        attended = product(value, prob_b, 0, 0)
        d_out = (attended - target.astype(F32).T).astype(BF16)
        return (d_out, jnp.sum(d_out.astype(F32) * attended, 0, keepdims=True))

    def score_grads(probability, d_out, delta_sum, value):
        prob_grad = product(value, d_out, 1, 0)
        return (probability * (prob_grad - delta_sum) * score_scale).astype(BF16)

    def grads(score_grad, prob_b, d_out, query, key):
        dq = product(key, score_grad, 0, 0).T
        dk = product(score_grad, query, 1, 0)
        return (dq, dk, product(prob_b, d_out, 1, 1))

    heads = range(half // HD)
    loaded = [load(head) for head in heads]
    probability = [weights(query, key) for query, _, key, _ in loaded]
    prob_b = [p.astype(BF16) for p in probability]
    outs = [output_grad(p, t, v) for p, (_, t, _, v) in zip(prob_b, loaded)]
    score_grad = [score_grads(p, *o, x[3]) for p, o, x in zip(probability, outs, loaded)]
    for head in heads:
        query, _, key, _ = loaded[head]
        at = slice(head * HD, (head + 1) * HD)
        store(at, *grads(score_grad[head], prob_b[head], outs[head][0], query, key))


def attend_near_kernel(
    width,
    halo_ref,
    swap_halo_ref,
    own_ref,
    v_ref,
    t_ref,
    swap_k_ref,
    swap_v_ref,
    swap_qt_ref,
    bias_ref,
    earlier_ref,
    halo_grad_ref,
    swap_halo_grad_ref,
    grad_ref,
):
    def store(at, dq, dk, dv):
        for place, grad in ((0, dk), (1, dv)):
            to = slice(place * width, (place + 1) * width)
            halo_grad_ref[to, at] = grad[:width].astype(BF16)
            swap_halo_grad_ref[to, at] = grad[3 * width : 4 * width].astype(BF16)
            for part in range(2):
                start = (5 * part + 1 + 2 * place) * width
                first = (3 * part + 1) * width
                grad_ref[start : start + 2 * width, at] = grad[first : first + 2 * width]
        for part in range(2):
            start = 5 * part * width
            grad_ref[start : start + width, at] = dq[part * width : (part + 1) * width]

    row = 1 - lax.rem(lax.axis_index("row"), 2)
    attend(width, row, halo_ref, swap_halo_ref, own_ref, v_ref, t_ref, swap_k_ref, swap_v_ref,
           swap_qt_ref, bias_ref, store)


def attend_far_kernel(
    width,
    halo_ref,
    swap_halo_ref,
    own_ref,
    v_ref,
    t_ref,
    swap_k_ref,
    swap_v_ref,
    swap_qt_ref,
    bias_ref,
    grad_ref,
    halo_grad_ref,
    swap_halo_grad_ref,
    total_ref,
    swap_first_ref,
    swap_last_ref,
):
    def block(ref, index, at):
        return ref[index * width : (index + 1) * width, at]

    def put(ref, index, at, value):
        ref[index * width : (index + 1) * width, at] = value.astype(ref.dtype)

    def store(at, dq, dk, dv):
        put(total_ref, 0, at, block(grad_ref, 0, at))
        put(total_ref, 1, at, dq[:width])
        put(swap_first_ref, 0, at, block(grad_ref, 5, at))
        put(swap_first_ref, 1, at, dq[width:])
        for place, grad in ((0, dk), (1, dv)):
            parts = [grad[i * width : (i + 1) * width] for i in range(6)]
            put(halo_grad_ref, place, at, parts[0])
            put(swap_halo_grad_ref, place, at, parts[3])
            put(total_ref, 2 + 2 * place, at, parts[2] + block(grad_ref, 1 + 2 * place, at))
            put(total_ref, 3 + 2 * place, at, parts[1] + block(grad_ref, 2 + 2 * place, at))
            put(swap_first_ref, 2 + place, at, parts[5] + block(grad_ref, 6 + 2 * place, at))
            put(swap_last_ref, place, at, parts[4] + block(grad_ref, 7 + 2 * place, at))

    row = lax.rem(lax.axis_index("row"), 2)
    attend(width, row, halo_ref, swap_halo_ref, own_ref, v_ref, t_ref, swap_k_ref, swap_v_ref,
           swap_qt_ref, bias_ref, store)


def near_kernel(width, own_ref, near_ref, swap_near_ref, out_ref, swap_out_ref):
    for place in range(2):
        rows = slice(place * width, (place + 1) * width)
        at = 2 + 2 * place
        own = own_ref[at * width : (at + 1) * width]
        out_ref[rows] = own + near_ref[rows].astype(F32)
    swap_out_ref[...] = swap_near_ref[: 2 * width].astype(F32)


def add_kernel(a_ref, b_ref, out_ref):
    out_ref[...] = (a_ref[...] + b_ref[...].astype(F32)).astype(BF16)


def gather_early_kernel(
    width,
    q_ref,
    k_ref,
    gain_ref,
    gain_k_ref,
    own_ref,
    swap_first_ref,
    near_ref,
    swap_near_ref,
    gated_ref,
    gated_near_ref,
    sums_ref,
    sum_near_ref,
):
    mine, theirs = halves(q_ref.shape[1] // 2)
    near, _ = sides(width)
    near_dk = swap_first_ref[2 * width : 3 * width].astype(F32) + swap_near_ref[:width]
    gated_near_ref[:, mine] = gain_k_ref[:, mine] * near_ref[:width]
    gated_near_ref[:, theirs] = gain_k_ref[:, theirs] * near_dk
    k_near = k_ref[near].astype(F32)
    sum_near_ref[...] = jnp.sum(k_near * gated_near_ref[...], -1, keepdims=True)
    for index, rows in enumerate(sides(width)):
        at = slice(index * width, (index + 1) * width)
        gated_ref[rows, mine] = gain_ref[:, mine] * own_ref[at]
        gated_ref[rows, theirs] = gain_ref[:, theirs] * swap_first_ref[at].astype(F32)
    sums_ref[...] = jnp.sum(q_ref[...].astype(F32) * gated_ref[...], -1, keepdims=True)


def gather_k_kernel(
    width,
    k_ref,
    gain_ref,
    own_ref,
    far_ref,
    swap_last_ref,
    gated_near_ref,
    sum_near_ref,
    sum_q_ref,
    gated_ref,
    sums_ref,
):
    tokens = k_ref.shape[0]
    mine, theirs = halves(k_ref.shape[1] // 2)
    near, far = sides(width)
    far_dk = own_ref[3 * width : 4 * width] + far_ref[:width].astype(F32)
    gated_ref[far, mine] = gain_ref[:, mine] * far_dk
    gated_ref[far, theirs] = gain_ref[:, theirs] * swap_last_ref[:width].astype(F32)
    sum_far = jnp.sum(k_ref[far].astype(F32) * gated_ref[far], -1, keepdims=True)
    gated_ref[near] = gated_near_ref[...]
    sums_ref[:tokens] = sum_q_ref[...]
    sums_ref[pl.ds(pl.multiple_of(tokens + near.start, width), width)] = sum_near_ref[...]
    sums_ref[pl.ds(pl.multiple_of(tokens + far.start, width), width)] = sum_far


def value_kernel(
    width,
    own_ref,
    near_ref,
    far_ref,
    swap_first_ref,
    swap_near_ref,
    swap_last_ref,
    earlier_ref,
    out_ref,
):
    mine, theirs = halves(out_ref.shape[1] // 2)
    near, far = sides(width)

    def term(ref, index):
        return ref[index * width : (index + 1) * width].astype(F32)

    out_ref[near, mine] = term(near_ref, 1).astype(BF16)
    out_ref[far, mine] = (term(own_ref, 5) + term(far_ref, 1)).astype(BF16)
    near_dv = term(swap_first_ref, 3) + term(swap_near_ref, 1)
    out_ref[near, theirs] = near_dv.astype(BF16)
    out_ref[far, theirs] = swap_last_ref[width:]


def finish_kernel(
    q_ref,
    k_ref,
    gated_q_ref,
    gated_k_ref,
    scale_ref,
    sums_ref,
    peer_ref,
    grad_q_out,
    grad_k_out,
    grad_q_ref,
    grad_k_ref,
    sems,
):
    tokens = q_ref.shape[0]
    features = HEADS * HD
    half = tokens // 2
    copies = []
    for base, pre_ref, gated_ref, out_ref, out in (
        (0, q_ref, gated_q_ref, grad_q_ref, grad_q_out),
        (tokens, k_ref, gated_k_ref, grad_k_ref, grad_k_out),
    ):
        for start in (0, half):
            rows, at = (slice(start, start + half), slice(base + start, base + start + half))
            scale = scale_ref[at]
            slope = scale * scale * scale * (sums_ref[at] + peer_ref[at]) / features
            out_ref[rows] = (
                scale * gated_ref[rows] - pre_ref[rows].astype(F32) * slope
            ).astype(BF16)
            copy = pltpu.make_async_copy(out_ref.at[rows], out.at[rows], sems.at[len(copies)])
            copy.start()
            copies.append(copy)
    for copy in copies:
        copy.wait()


def swapped_device(q_pre, k_pre, values, target, gain_q, gain_k, kept):
    frames, rows, width, feat_dev = q_pre.shape
    tokens = rows * width
    half = feat_dev // 2
    row_blocks = lax.axis_size("row")
    inputs = [array.reshape(tokens, feat_dev) for array in (q_pre, k_pre, values, target)]
    inputs += [gain_q, gain_k]
    inputs = [pltpu.with_memory_space_constraint(array, pltpu.HBM) for array in inputs]
    near_pairs = [(r, r + 1) for r in range(0, row_blocks - 1, 2)]
    far_pairs = [(r, r + 1) for r in range(1, row_blocks - 1, 2)]
    near, far = (pairs + [(b, a) for a, b in pairs] for pairs in (near_pairs, far_pairs))
    swap_near = [
        (f * row_blocks + a, (1 - f) * row_blocks + b) for f in range(2) for a, b in near
    ]

    def shape(first, last, dtype=BF16):
        return jax.ShapeDtypeStruct((first, last), dtype)

    block = shape(tokens, feat_dev)
    sum_pair = shape(2 * tokens, 1, F32)
    tokens_half = shape(tokens, half)
    gain = shape(1, feat_dev, F32)
    edge = shape(2 * width, half)
    padded_edge = shape(2 * width + 16, half)
    bias = shape(6 * width, 2 * width, F32)

    q_all, k_all, v_all, t_all, gain_q, gain_k, sums, v_out = call(
        load_kernel,
        (block,) * 4 + (gain,) * 2 + (sum_pair, tokens_half),
        in_specs=[pl.BlockSpec(memory_space=pltpu.HBM)] * 6,
        scratch_shapes=[pltpu.SemaphoreType.DMA((6,))],
    )(*inputs)
    swap_v = lax.ppermute(v_out, "frame", SWAP)
    peer = lax.ppermute(sums, "head", SWAP)
    scale, own_kq, k_out, qt_out, near_out, far_out = call(
        functools.partial(norm_kernel, width),
        (sum_pair, shape(2 * tokens, half), tokens_half, shape(2 * tokens, half), edge, edge),
    )(q_all, k_all, v_all, t_all, sums, peer, gain_q, gain_k)
    near_in = lax.ppermute(near_out, "row", near)
    swap_k = lax.ppermute(k_out, "frame", SWAP)
    swap_qt = lax.ppermute(qt_out, "frame", SWAP)
    far_in = lax.ppermute(far_out, "row", far)
    relay_near = call(functools.partial(relay_near_kernel, width), edge)(swap_k, swap_v, near_in)
    swap_near_in = lax.ppermute(relay_near, "row", near)
    relay_far, near_bias, far_bias = call(
        functools.partial(relay_far_kernel, width),
        (edge, bias, bias),
        in_specs=[pl.BlockSpec(memory_space=pltpu.SMEM)]
        + [pl.BlockSpec(memory_space=pltpu.VMEM)] * 3,
    )(kept.transpose(0, 2, 1), swap_k, swap_v, relay_near)
    swap_far_in = lax.ppermute(relay_far, "row", far)
    shared = (own_kq, v_all, t_all, swap_k, swap_v, swap_qt)
    near_out, swap_near_out, near_terms = call(
        functools.partial(attend_near_kernel, width),
        (padded_edge, padded_edge, shape(10 * width, half, F32)),
        flops=5 * 10**8,
        moved=2 * 10**6,
    )(near_in, swap_near_in, *shared, near_bias, far_in)
    near_total = lax.ppermute(near_out, "row", near)
    swap_near_total = lax.ppermute(swap_near_out, ("frame", "row"), swap_near)
    far_out, swap_far_out, own_total, first_out, last_terms = call(
        functools.partial(attend_far_kernel, width),
        (edge, edge, shape(3 * tokens, half, F32), shape(4 * width, half))
        + (shape(2 * width, half, F32),),
        flops=5 * 10**8,
        moved=2 * 10**6,
    )(far_in, swap_far_in, *shared, far_bias, near_terms)
    far_terms = lax.ppermute(swap_far_out, "row", far)
    swap_first = lax.ppermute(first_out, "frame", SWAP)
    far_total = lax.ppermute(far_out, "row", far)
    near_total, swap_near_total = call(
        functools.partial(near_kernel, width),
        (shape(2 * width, half, F32),) * 2,
        flops=3 * 10**9,
    )(own_total, near_total, swap_near_total)
    last_out = call(add_kernel, edge, flops=1, moved=1)(last_terms, far_terms)
    swap_last = lax.ppermute(last_out, "frame", SWAP)
    terms = (own_total, near_total, far_total, swap_first, swap_near_total, swap_last)
    gated = shape(tokens, feat_dev, F32)
    gated_q, gated_near, sum_q, sum_near = call(
        functools.partial(gather_early_kernel, width),
        (gated, shape(width, feat_dev, F32), shape(tokens, 1, F32), shape(width, 1, F32)),
        flops=3 * 10**9,
    )(q_all, k_all, gain_q, gain_k, own_total, swap_first, near_total, swap_near_total)
    gated_k, sum_terms = call(functools.partial(gather_k_kernel, width), (gated, sum_pair))(
        k_all, gain_k, own_total, far_total, swap_last, gated_near, sum_near, sum_q
    )
    sum_peer = lax.ppermute(sum_terms, "head", SWAP)
    grad_v = call(functools.partial(value_kernel, width), block)(*terms, sum_terms)
    grad_q, grad_k = call(
        finish_kernel,
        (block, block),
        out_specs=[pl.BlockSpec(memory_space=pltpu.HBM)] * 2,
        scratch_shapes=[pltpu.VMEM((tokens, feat_dev), BF16)] * 2 + [pltpu.SemaphoreType.DMA((4,))],
    )(
        q_all, k_all, gated_q, gated_k, scale, sum_terms, sum_peer
    )
    return tuple(
        array.reshape(frames, rows, width, feat_dev) for array in (grad_q, grad_k, grad_v)
    )


def on_device(q_pre, *rest):
    frames, rows, _, feat_dev = q_pre.shape
    paired = lax.axis_size("frame") == 2 and frames == 1 and rows == 2
    if paired and feat_dev % (2 * HD) == 0:
        return swapped_device(q_pre, *rest)
    return per_device(q_pre, *rest)


def solution(mesh):
    return jax.shard_map(
        on_device,
        mesh=mesh,
        in_specs=(
            P("frame", "row", None, "head"),
            P("frame", "row", None, "head"),
            P("frame", "row", None, "head"),
            P("frame", "row", None, "head"),
            P("head"),
            P("head"),
            P(),
        ),
        out_specs=(
            P("frame", "row", None, "head"),
            P("frame", "row", None, "head"),
            P("frame", "row", None, "head"),
        ),
        check_vma=False,
    )
```

```python
import functools

import jax
import jax.numpy as jnp
from jax import lax
from jax.experimental import pallas as pl
from jax.experimental.pallas import tpu as pltpu
from jax.sharding import PartitionSpec as P

TC = 16
HEADS = 20
HD = 128


norm_eps = 1e-06


def padded(x, sides, width):
    for axis, dim in sides:
        size, length = (lax.axis_size(axis), x.shape[dim])
        up = [(i, (i + 1) % size) for i in range(size - 1)]
        down = [(j, i) for i, j in up]
        last = lax.slice_in_dim(x, length - width, length, axis=dim)
        first = lax.slice_in_dim(x, 0, width, axis=dim)
        before = lax.ppermute(last, axis, up)
        after = lax.ppermute(first, axis, down)
        x = jnp.concatenate([before, x, after], axis=dim)
    return x


def from_behind(value, axis, steps):
    count = lax.axis_size(axis)
    first, last = (max(0, -steps), min(count, count - steps))
    return lax.ppermute(value, axis, [(source, source + steps) for source in range(first, last)])


def query_mask(kept_win, col_tile, tiles):
    near_cols = jnp.abs(col_tile[:, None] - col_tile[None, :]) <= 1
    same_tile = col_tile[:, None] == col_tile[None, :]
    one_hot = col_tile[:, None] == jnp.arange(tiles)[None, :]
    key_kept = jnp.any(one_hot[None, None] & (kept_win[:, :, None, :] > 0), axis=-1)
    centre = (jnp.arange(3)[:, None] == 1) & (jnp.arange(3)[None, :] == 1)
    allowed = near_cols[:, None, None, :] & (
        key_kept[None] | centre[None, :, :, None] & same_tile[:, None, None, :]
    )
    return allowed.reshape(col_tile.shape[0], -1)


def attend_line(query, kv_win, t_line, allowed):
    width, heads_dev, _ = query.shape
    score_scale = HD ** (-0.5)
    key_block = kv_win[0].reshape(9 * width, heads_dev, HD)
    value_block = kv_win[1].reshape(9 * width, heads_dev, HD)
    mask = allowed[None]
    scores = (
        jnp.einsum("qhd,khd->hqk", query, key_block, preferred_element_type=jnp.float32)
        * score_scale
    )
    scores = jnp.where(mask, scores, -jnp.inf)
    row_max = jnp.max(scores, -1, keepdims=True)
    expo = jnp.where(mask, jnp.exp(scores - row_max), 0.0)
    denominator = jnp.sum(expo, -1, keepdims=True)
    probability = expo / denominator
    prob_b = probability.astype(jnp.bfloat16)
    attended = jnp.einsum("hqk,khd->qhd", prob_b, value_block, preferred_element_type=jnp.float32)
    d_out = (attended - t_line.astype(jnp.float32)).astype(jnp.bfloat16)
    delta_sum = jnp.sum(d_out.astype(jnp.float32) * attended, -1).T
    prob_grad = jnp.einsum("qhd,khd->hqk", d_out, value_block, preferred_element_type=jnp.float32)
    score_grad = (probability * (prob_grad - delta_sum[:, :, None]) * score_scale).astype(
        jnp.bfloat16
    )
    dq_line = jnp.einsum("hqk,khd->qhd", score_grad, key_block, preferred_element_type=jnp.float32)
    log_total = row_max[..., 0] + jnp.log(denominator[..., 0])
    return (dq_line.reshape(width, heads_dev * HD), d_out, log_total, delta_sum, prob_b, score_grad)


def per_device(q_pre, k_pre, values, target, gain_q, gain_k, kept):
    frames, rows, width, feat_dev = q_pre.shape
    heads_dev = feat_dev // HD
    tiles = width // TC
    features = HEADS * HD
    line_count = frames * rows
    col_tile = jnp.arange(width) // TC
    q_float = q_pre.astype(jnp.float32)
    k_float = k_pre.astype(jnp.float32)
    square_q, square_k = lax.psum(
        (jnp.sum(q_float * q_float, -1), jnp.sum(k_float * k_float, -1)), "head"
    )
    scale_q = lax.rsqrt(square_q[..., None] / features + norm_eps)
    scale_k = lax.rsqrt(square_k[..., None] / features + norm_eps)
    q_norm = (q_float * scale_q * gain_q).astype(jnp.bfloat16)
    k_norm = (k_float * scale_k * gain_k).astype(jnp.bfloat16)
    kv_ext = padded(jnp.stack([k_norm, values]), (("frame", 1), ("row", 2)), 1)
    frame_at = lax.axis_index("frame")
    row_at = lax.axis_index("row")
    zero = jnp.int32(0)
    kept_pad = jnp.pad(kept, ((1, 1), (1, 1), (0, 0)))
    kept_ext = lax.dynamic_slice(
        kept_pad, (frame_at * frames, row_at * rows, zero), (frames + 2, rows + 2, tiles)
    )
    line_ids = jnp.arange(line_count, dtype=jnp.int32)
    q_lines = q_norm.reshape(line_count, width, heads_dev, HD)
    t_lines = target.reshape(line_count, width, heads_dev, HD)

    def query_window(line):
        f_at = line // rows
        r_at = line % rows
        kv_win = lax.dynamic_slice(
            kv_ext, (zero, f_at, r_at, zero, zero), (2, 3, 3, width, feat_dev)
        )
        kept_win = lax.dynamic_slice(kept_ext, (f_at, r_at, zero), (3, 3, tiles))
        return (f_at, r_at, kv_win, query_mask(kept_win, col_tile, tiles))

    def returned_step(totals, inputs):
        line, query, t_line = inputs
        f_at, r_at, kv_win, allowed = query_window(line)
        dq_line, d_out, log_total, delta_sum, prob_b, score_grad = attend_line(
            query, kv_win, t_line, allowed
        )
        key_grad = jnp.einsum("hqk,qhd->khd", score_grad, query, preferred_element_type=jnp.float32)
        value_grad = jnp.einsum("hqk,qhd->khd", prob_b, d_out, preferred_element_type=jnp.float32)
        both = jnp.stack(
            [key_grad.reshape(3, 3, width, feat_dev), value_grad.reshape(3, 3, width, feat_dev)]
        )
        start = (zero, f_at, r_at, zero, zero)
        current = lax.dynamic_slice(totals, start, (2, 3, 3, width, feat_dev))
        totals = lax.dynamic_update_slice(totals, current + both, start)
        return (totals, dq_line)

    empty = jnp.zeros((2, frames + 2, rows + 2, width, feat_dev), jnp.float32)
    totals, dq_lines = lax.scan(returned_step, empty, (line_ids, q_lines, t_lines))
    inner = totals[:, :, 1 : rows + 1]
    row_edges = (totals[:, :, 0:1], totals[:, :, rows + 1 : rows + 2])
    row_moved = [
        from_behind(row_edges[side], "row", by_value) for side, by_value in ((0, -1), (1, 1))
    ]
    inner = inner.at[:, :, rows - 1 : rows].add(row_moved[0])
    inner = inner.at[:, :, 0:1].add(row_moved[1])
    middle = inner[:, 1 : frames + 1]
    frame_edges = (inner[:, 0:1], inner[:, frames + 1 : frames + 2])
    frame_moved = [
        from_behind(frame_edges[side], "frame", by_value) for side, by_value in ((0, -1), (1, 1))
    ]
    middle = middle.at[:, frames - 1 : frames].add(frame_moved[0])
    middle = middle.at[:, 0:1].add(frame_moved[1])
    dk_norm = middle[0]
    value_total = middle[1]
    dq_norm = dq_lines.reshape(frames, rows, width, feat_dev)
    gated_q = gain_q * dq_norm
    gated_k = gain_k * dk_norm
    sum_q, sum_k = lax.psum(
        (jnp.sum(q_float * gated_q, -1), jnp.sum(k_float * gated_k, -1)), "head"
    )
    grad_q = (scale_q * gated_q - q_float * scale_q**3 * sum_q[..., None] / features).astype(
        jnp.bfloat16
    )
    grad_k = (scale_k * gated_k - k_float * scale_k**3 * sum_k[..., None] / features).astype(
        jnp.bfloat16
    )
    return (grad_q, grad_k, value_total.astype(jnp.bfloat16))


SWAP = [(0, 1), (1, 0)]
F32 = jnp.float32
BF16 = jnp.bfloat16
VMEM_LIMIT = 48 * 1024 * 1024
LOG2_E = 1.4426950408889634


def call(body, out_shape, flops=10**6, moved=10**6, **kw):
    return pl.pallas_call(
        body,
        out_shape=out_shape,
        compiler_params=pltpu.CompilerParams(vmem_limit_bytes=VMEM_LIMIT),
        cost_estimate=pl.CostEstimate(flops=flops, bytes_accessed=moved, transcendentals=0),
        **kw,
    )


def halves(half):
    frame_at = lax.axis_index("frame")
    mine = pl.multiple_of(frame_at * half, HD)
    theirs = pl.multiple_of((1 - frame_at) * half, HD)
    return (pl.ds(mine, half), pl.ds(theirs, half))


def sides(width):
    odd = lax.rem(lax.axis_index("row"), 2)
    near = pl.multiple_of((1 - odd) * width, width)
    far = pl.multiple_of(odd * width, width)
    return (pl.ds(near, width), pl.ds(far, width))


def load_kernel(
    q_in,
    k_in,
    v_in,
    t_in,
    gain_q_in,
    gain_k_in,
    q_ref,
    k_ref,
    v_ref,
    t_ref,
    gain_q_ref,
    gain_k_ref,
    sums_ref,
    v_out_ref,
    sems,
):
    tokens, feat_dev = q_ref.shape
    _, theirs = halves(feat_dev // 2)
    pairs = (
        (q_in, q_ref),
        (k_in, k_ref),
        (v_in, v_ref),
        (t_in, t_ref),
        (gain_q_in, gain_q_ref.at[0]),
        (gain_k_in, gain_k_ref.at[0]),
    )
    copies = [pltpu.make_async_copy(a, b, sems.at[i]) for i, (a, b) in enumerate(pairs)]
    for copy in copies:
        copy.start()
    copies[0].wait()
    q_float = q_ref[...].astype(F32)
    sums_ref[:tokens] = jnp.sum(q_float * q_float, -1, keepdims=True)
    copies[1].wait()
    k_float = k_ref[...].astype(F32)
    sums_ref[tokens:] = jnp.sum(k_float * k_float, -1, keepdims=True)
    copies[2].wait()
    v_out_ref[...] = v_ref[:, theirs]
    for copy in copies[3:]:
        copy.wait()


def norm_kernel(
    width,
    q_ref,
    k_ref,
    v_ref,
    t_ref,
    sums_ref,
    peer_ref,
    gain_q_ref,
    gain_k_ref,
    scale_ref,
    own_ref,
    k_out_ref,
    qt_out_ref,
    near_ref,
    far_ref,
):
    tokens, feat_dev = q_ref.shape
    features = HEADS * HD
    mine, theirs = halves(feat_dev // 2)
    near, far = sides(width)
    scale = lax.rsqrt((sums_ref[...] + peer_ref[...]) / features + norm_eps)
    scale_ref[...] = scale
    scale_q, scale_k = (scale[:tokens], scale[tokens:])

    def normed(ref, part, scales, gain_ref):
        return (ref[:, part].astype(F32) * scales * gain_ref[:, part]).astype(BF16)

    k_out_ref[...] = normed(k_ref, theirs, scale_k, gain_k_ref)
    qt_out_ref[:tokens] = normed(q_ref, theirs, scale_q, gain_q_ref)
    qt_out_ref[tokens:] = t_ref[:, theirs]
    own_ref[:tokens] = normed(k_ref, mine, scale_k, gain_k_ref)
    own_ref[tokens:] = normed(q_ref, mine, scale_q, gain_q_ref)
    for out_ref, rows in ((near_ref, near), (far_ref, far)):
        out_ref[:width] = own_ref[rows]
        out_ref[width:] = v_ref[rows, mine]


def relay_near_kernel(width, k_ref, v_ref, earlier_ref, out_ref):
    near, _ = sides(width)
    out_ref[:width] = k_ref[near]
    out_ref[width:] = v_ref[near]


def relay_far_kernel(width, kept_ref, k_ref, v_ref, earlier_ref, out_ref, near_ref, far_ref):
    _, far = sides(width)
    out_ref[:width] = k_ref[far]
    out_ref[width:] = v_ref[far]
    rows = 2
    count = kept_ref.shape[2]
    tiles = width // TC
    frame_at = lax.axis_index("frame")
    first_row = lax.axis_index("row") * rows
    odd = lax.rem(lax.axis_index("row"), 2)
    query_at = lax.broadcasted_iota(jnp.int32, (TC, near_ref.shape[1]), 1)
    query_tile = lax.rem(query_at, width) // TC
    for out_ref, row in ((near_ref, 1 - odd), (far_ref, odd)):
        for part in range(2):
            frame = frame_at if part == 0 else 1 - frame_at
            for slot, place in enumerate((3 * row - 1, row, 1 - row)):
                at = first_row + place
                inside = (at >= 0) & (at < count)
                at = jnp.clip(at, 0, count - 1)
                for tile in range(tiles):
                    value = jnp.where(inside, kept_ref[frame, tile, at], 0)
                    allowed = (jnp.abs(query_tile - tile) <= 1) & (value > 0)
                    if slot == 1:
                        allowed |= (query_tile == tile) & (query_at // width == part)
                    here = ((part * 3 + slot) * tiles + tile) * TC
                    out_ref[here : here + TC] = jnp.where(allowed, 0.0, -1e30)


def attend(width, row, halo_ref, swap_halo_ref, own_ref, v_ref, t_ref, swap_k_ref, swap_v_ref,
           swap_qt_ref, bias_ref, store):
    tokens, half = swap_k_ref.shape
    score_scale = HD ** (-0.5)
    mine = lax.axis_index("frame") * half
    bias = bias_ref[...]
    own_at = pl.multiple_of(row * width, width)
    other_at = pl.multiple_of((1 - row) * width, width)
    rows = (pl.ds(own_at, width), pl.ds(other_at, width))
    query_at = pl.ds(pl.multiple_of(tokens + own_at, width), width)

    def product(a, b, a_dim, b_dim):
        return lax.dot_general(a, b, (((a_dim,), (b_dim,)), ((), ())), preferred_element_type=F32)

    def load(head):
        at = slice(head * HD, (head + 1) * HD)
        mine_at = pl.ds(pl.multiple_of(mine + head * HD, HD), HD)
        query = jnp.concatenate([own_ref[query_at, at], swap_qt_ref[rows[0], at]], 0)
        target = jnp.concatenate([t_ref[rows[0], mine_at], swap_qt_ref[query_at, at]], 0)
        key = jnp.concatenate(
            [halo_ref[:width, at]]
            + [own_ref[r, at] for r in rows]
            + [swap_halo_ref[:width, at]]
            + [swap_k_ref[r, at] for r in rows],
            0,
        )
        value = jnp.concatenate(
            [halo_ref[width:, at]]
            + [v_ref[r, mine_at] for r in rows]
            + [swap_halo_ref[width:, at]]
            + [swap_v_ref[r, at] for r in rows],
            0,
        )
        return (query, target, key, value)

    def weights(query, key):
        scores = product(key, query, 1, 1) * (score_scale * LOG2_E) + bias
        expo = jnp.exp2(scores - jnp.max(scores, 0, keepdims=True))
        return expo * (1.0 / jnp.sum(expo, 0, keepdims=True))

    def output_grad(prob_b, target, value):
        attended = product(value, prob_b, 0, 0)
        d_out = (attended - target.astype(F32).T).astype(BF16)
        return (d_out, jnp.sum(d_out.astype(F32) * attended, 0, keepdims=True))

    def score_grads(probability, d_out, delta_sum, value):
        prob_grad = product(value, d_out, 1, 0)
        return (probability * (prob_grad - delta_sum) * score_scale).astype(BF16)

    def grads(score_grad, prob_b, d_out, query, key):
        dq = product(key, score_grad, 0, 0).T
        dk = product(score_grad, query, 1, 0)
        return (dq, dk, product(prob_b, d_out, 1, 1))

    heads = range(half // HD)
    loaded = [load(head) for head in heads]
    probability = [weights(query, key) for query, _, key, _ in loaded]
    prob_b = [p.astype(BF16) for p in probability]
    outs = [output_grad(p, t, v) for p, (_, t, _, v) in zip(prob_b, loaded)]
    score_grad = [score_grads(p, *o, x[3]) for p, o, x in zip(probability, outs, loaded)]
    for head in heads:
        query, _, key, _ = loaded[head]
        at = slice(head * HD, (head + 1) * HD)
        store(at, *grads(score_grad[head], prob_b[head], outs[head][0], query, key))


def attend_near_kernel(
    width,
    halo_ref,
    swap_halo_ref,
    own_ref,
    v_ref,
    t_ref,
    swap_k_ref,
    swap_v_ref,
    swap_qt_ref,
    bias_ref,
    earlier_ref,
    halo_grad_ref,
    swap_halo_grad_ref,
    grad_ref,
):
    def store(at, dq, dk, dv):
        for place, grad in ((0, dk), (1, dv)):
            to = slice(place * width, (place + 1) * width)
            halo_grad_ref[to, at] = grad[:width].astype(BF16)
            swap_halo_grad_ref[to, at] = grad[3 * width : 4 * width].astype(BF16)
            for part in range(2):
                start = (5 * part + 1 + 2 * place) * width
                first = (3 * part + 1) * width
                grad_ref[start : start + 2 * width, at] = grad[first : first + 2 * width]
        for part in range(2):
            start = 5 * part * width
            grad_ref[start : start + width, at] = dq[part * width : (part + 1) * width]

    row = 1 - lax.rem(lax.axis_index("row"), 2)
    attend(width, row, halo_ref, swap_halo_ref, own_ref, v_ref, t_ref, swap_k_ref, swap_v_ref,
           swap_qt_ref, bias_ref, store)


def attend_far_kernel(
    width,
    halo_ref,
    swap_halo_ref,
    own_ref,
    v_ref,
    t_ref,
    swap_k_ref,
    swap_v_ref,
    swap_qt_ref,
    bias_ref,
    grad_ref,
    halo_grad_ref,
    swap_halo_grad_ref,
    total_ref,
    swap_first_ref,
    swap_last_ref,
):
    def block(ref, index, at):
        return ref[index * width : (index + 1) * width, at]

    def put(ref, index, at, value):
        ref[index * width : (index + 1) * width, at] = value.astype(ref.dtype)

    def store(at, dq, dk, dv):
        put(total_ref, 0, at, block(grad_ref, 0, at))
        put(total_ref, 1, at, dq[:width])
        put(swap_first_ref, 0, at, block(grad_ref, 5, at))
        put(swap_first_ref, 1, at, dq[width:])
        for place, grad in ((0, dk), (1, dv)):
            parts = [grad[i * width : (i + 1) * width] for i in range(6)]
            put(halo_grad_ref, place, at, parts[0])
            put(swap_halo_grad_ref, place, at, parts[3])
            put(total_ref, 2 + 2 * place, at, parts[2] + block(grad_ref, 1 + 2 * place, at))
            put(total_ref, 3 + 2 * place, at, parts[1] + block(grad_ref, 2 + 2 * place, at))
            put(swap_first_ref, 2 + place, at, parts[5] + block(grad_ref, 6 + 2 * place, at))
            put(swap_last_ref, place, at, parts[4] + block(grad_ref, 7 + 2 * place, at))

    row = lax.rem(lax.axis_index("row"), 2)
    attend(width, row, halo_ref, swap_halo_ref, own_ref, v_ref, t_ref, swap_k_ref, swap_v_ref,
           swap_qt_ref, bias_ref, store)


def near_kernel(width, own_ref, near_ref, swap_near_ref, out_ref, swap_out_ref):
    for place in range(2):
        rows = slice(place * width, (place + 1) * width)
        at = 2 + 2 * place
        own = own_ref[at * width : (at + 1) * width]
        out_ref[rows] = own + near_ref[rows].astype(F32)
    swap_out_ref[...] = swap_near_ref[: 2 * width].astype(F32)


def add_kernel(a_ref, b_ref, out_ref):
    out_ref[...] = (a_ref[...] + b_ref[...].astype(F32)).astype(BF16)


def gather_early_kernel(
    width,
    q_ref,
    k_ref,
    gain_ref,
    gain_k_ref,
    own_ref,
    swap_first_ref,
    near_ref,
    swap_near_ref,
    gated_ref,
    gated_near_ref,
    sums_ref,
    sum_near_ref,
):
    mine, theirs = halves(q_ref.shape[1] // 2)
    near, _ = sides(width)
    near_dk = swap_first_ref[2 * width : 3 * width].astype(F32) + swap_near_ref[:width]
    gated_near_ref[:, mine] = gain_k_ref[:, mine] * near_ref[:width]
    gated_near_ref[:, theirs] = gain_k_ref[:, theirs] * near_dk
    k_near = k_ref[near].astype(F32)
    sum_near_ref[...] = jnp.sum(k_near * gated_near_ref[...], -1, keepdims=True)
    for index, rows in enumerate(sides(width)):
        at = slice(index * width, (index + 1) * width)
        gated_ref[rows, mine] = gain_ref[:, mine] * own_ref[at]
        gated_ref[rows, theirs] = gain_ref[:, theirs] * swap_first_ref[at].astype(F32)
    sums_ref[...] = jnp.sum(q_ref[...].astype(F32) * gated_ref[...], -1, keepdims=True)


def gather_k_kernel(
    width,
    k_ref,
    gain_ref,
    own_ref,
    far_ref,
    swap_last_ref,
    gated_near_ref,
    sum_near_ref,
    sum_q_ref,
    gated_ref,
    sums_ref,
):
    tokens = k_ref.shape[0]
    mine, theirs = halves(k_ref.shape[1] // 2)
    near, far = sides(width)
    far_dk = own_ref[3 * width : 4 * width] + far_ref[:width].astype(F32)
    gated_ref[far, mine] = gain_ref[:, mine] * far_dk
    gated_ref[far, theirs] = gain_ref[:, theirs] * swap_last_ref[:width].astype(F32)
    sum_far = jnp.sum(k_ref[far].astype(F32) * gated_ref[far], -1, keepdims=True)
    gated_ref[near] = gated_near_ref[...]
    sums_ref[:tokens] = sum_q_ref[...]
    sums_ref[pl.ds(pl.multiple_of(tokens + near.start, width), width)] = sum_near_ref[...]
    sums_ref[pl.ds(pl.multiple_of(tokens + far.start, width), width)] = sum_far


def value_kernel(
    width,
    own_ref,
    near_ref,
    far_ref,
    swap_first_ref,
    swap_near_ref,
    swap_last_ref,
    earlier_ref,
    out_ref,
):
    mine, theirs = halves(out_ref.shape[1] // 2)
    near, far = sides(width)

    def term(ref, index):
        return ref[index * width : (index + 1) * width].astype(F32)

    out_ref[near, mine] = term(near_ref, 1).astype(BF16)
    out_ref[far, mine] = (term(own_ref, 5) + term(far_ref, 1)).astype(BF16)
    near_dv = term(swap_first_ref, 3) + term(swap_near_ref, 1)
    out_ref[near, theirs] = near_dv.astype(BF16)
    out_ref[far, theirs] = swap_last_ref[width:]


def finish_kernel(
    q_ref,
    k_ref,
    gated_q_ref,
    gated_k_ref,
    scale_ref,
    sums_ref,
    peer_ref,
    grad_q_out,
    grad_k_out,
    grad_q_ref,
    grad_k_ref,
    sems,
):
    tokens = q_ref.shape[0]
    features = HEADS * HD
    half = tokens // 2
    copies = []
    for base, pre_ref, gated_ref, out_ref, out in (
        (0, q_ref, gated_q_ref, grad_q_ref, grad_q_out),
        (tokens, k_ref, gated_k_ref, grad_k_ref, grad_k_out),
    ):
        for start in (0, half):
            rows, at = (slice(start, start + half), slice(base + start, base + start + half))
            scale = scale_ref[at]
            slope = scale * scale * scale * (sums_ref[at] + peer_ref[at]) / features
            out_ref[rows] = (
                scale * gated_ref[rows] - pre_ref[rows].astype(F32) * slope
            ).astype(BF16)
            copy = pltpu.make_async_copy(out_ref.at[rows], out.at[rows], sems.at[len(copies)])
            copy.start()
            copies.append(copy)
    for copy in copies:
        copy.wait()


def swapped_device(q_pre, k_pre, values, target, gain_q, gain_k, kept):
    frames, rows, width, feat_dev = q_pre.shape
    tokens = rows * width
    half = feat_dev // 2
    row_blocks = lax.axis_size("row")
    inputs = [array.reshape(tokens, feat_dev) for array in (q_pre, k_pre, values, target)]
    inputs += [gain_q, gain_k]
    inputs = [pltpu.with_memory_space_constraint(array, pltpu.HBM) for array in inputs]
    near_pairs = [(r, r + 1) for r in range(0, row_blocks - 1, 2)]
    far_pairs = [(r, r + 1) for r in range(1, row_blocks - 1, 2)]
    near, far = (pairs + [(b, a) for a, b in pairs] for pairs in (near_pairs, far_pairs))
    swap_near = [
        (f * row_blocks + a, (1 - f) * row_blocks + b) for f in range(2) for a, b in near
    ]

    def shape(first, last, dtype=BF16):
        return jax.ShapeDtypeStruct((first, last), dtype)

    block = shape(tokens, feat_dev)
    sum_pair = shape(2 * tokens, 1, F32)
    tokens_half = shape(tokens, half)
    gain = shape(1, feat_dev, F32)
    edge = shape(2 * width, half)
    padded_edge = shape(2 * width + 16, half)
    bias = shape(6 * width, 2 * width, F32)

    q_all, k_all, v_all, t_all, gain_q, gain_k, sums, v_out = call(
        load_kernel,
        (block,) * 4 + (gain,) * 2 + (sum_pair, tokens_half),
        in_specs=[pl.BlockSpec(memory_space=pltpu.HBM)] * 6,
        scratch_shapes=[pltpu.SemaphoreType.DMA((6,))],
    )(*inputs)
    swap_v = lax.ppermute(v_out, "frame", SWAP)
    peer = lax.ppermute(sums, "head", SWAP)
    scale, own_kq, k_out, qt_out, near_out, far_out = call(
        functools.partial(norm_kernel, width),
        (sum_pair, shape(2 * tokens, half), tokens_half, shape(2 * tokens, half), edge, edge),
    )(q_all, k_all, v_all, t_all, sums, peer, gain_q, gain_k)
    near_in = lax.ppermute(near_out, "row", near)
    swap_k = lax.ppermute(k_out, "frame", SWAP)
    swap_qt = lax.ppermute(qt_out, "frame", SWAP)
    far_in = lax.ppermute(far_out, "row", far)
    relay_near = call(functools.partial(relay_near_kernel, width), edge)(swap_k, swap_v, near_in)
    swap_near_in = lax.ppermute(relay_near, "row", near)
    relay_far, near_bias, far_bias = call(
        functools.partial(relay_far_kernel, width),
        (edge, bias, bias),
        in_specs=[pl.BlockSpec(memory_space=pltpu.SMEM)]
        + [pl.BlockSpec(memory_space=pltpu.VMEM)] * 3,
    )(kept.transpose(0, 2, 1), swap_k, swap_v, relay_near)
    swap_far_in = lax.ppermute(relay_far, "row", far)
    shared = (own_kq, v_all, t_all, swap_k, swap_v, swap_qt)
    near_out, swap_near_out, near_terms = call(
        functools.partial(attend_near_kernel, width),
        (padded_edge, padded_edge, shape(10 * width, half, F32)),
        flops=5 * 10**8,
        moved=2 * 10**6,
    )(near_in, swap_near_in, *shared, near_bias, far_in)
    near_total = lax.ppermute(near_out, "row", near)
    swap_near_total = lax.ppermute(swap_near_out, ("frame", "row"), swap_near)
    far_out, swap_far_out, own_total, first_out, last_terms = call(
        functools.partial(attend_far_kernel, width),
        (edge, edge, shape(3 * tokens, half, F32), shape(4 * width, half))
        + (shape(2 * width, half, F32),),
        flops=5 * 10**8,
        moved=2 * 10**6,
    )(far_in, swap_far_in, *shared, far_bias, near_terms)
    far_terms = lax.ppermute(swap_far_out, "row", far)
    swap_first = lax.ppermute(first_out, "frame", SWAP)
    far_total = lax.ppermute(far_out, "row", far)
    near_total, swap_near_total = call(
        functools.partial(near_kernel, width),
        (shape(2 * width, half, F32),) * 2,
        flops=3 * 10**9,
    )(own_total, near_total, swap_near_total)
    last_out = call(add_kernel, edge, flops=1, moved=1)(last_terms, far_terms)
    swap_last = lax.ppermute(last_out, "frame", SWAP)
    terms = (own_total, near_total, far_total, swap_first, swap_near_total, swap_last)
    gated = shape(tokens, feat_dev, F32)
    gated_q, gated_near, sum_q, sum_near = call(
        functools.partial(gather_early_kernel, width),
        (gated, shape(width, feat_dev, F32), shape(tokens, 1, F32), shape(width, 1, F32)),
        flops=3 * 10**9,
    )(q_all, k_all, gain_q, gain_k, own_total, swap_first, near_total, swap_near_total)
    gated_k, sum_terms = call(functools.partial(gather_k_kernel, width), (gated, sum_pair))(
        k_all, gain_k, own_total, far_total, swap_last, gated_near, sum_near, sum_q
    )
    sum_peer = lax.ppermute(sum_terms, "head", SWAP)
    grad_v = call(functools.partial(value_kernel, width), block)(*terms, sum_terms)
    grad_q, grad_k = call(
        finish_kernel,
        (block, block),
        out_specs=[pl.BlockSpec(memory_space=pltpu.HBM)] * 2,
        scratch_shapes=[pltpu.VMEM((tokens, feat_dev), BF16)] * 2 + [pltpu.SemaphoreType.DMA((4,))],
    )(
        q_all, k_all, gated_q, gated_k, scale, sum_terms, sum_peer
    )
    return tuple(
        array.reshape(frames, rows, width, feat_dev) for array in (grad_q, grad_k, grad_v)
    )


def on_device(q_pre, *rest):
    frames, rows, _, feat_dev = q_pre.shape
    paired = lax.axis_size("frame") == 2 and frames == 1 and rows == 2
    if paired and feat_dev % (2 * HD) == 0:
        return swapped_device(q_pre, *rest)
    return per_device(q_pre, *rest)


def solution(mesh):
    return jax.shard_map(
        on_device,
        mesh=mesh,
        in_specs=(
            P("frame", "row", None, "head"),
            P("frame", "row", None, "head"),
            P("frame", "row", None, "head"),
            P("frame", "row", None, "head"),
            P("head"),
            P("head"),
            P(),
        ),
        out_specs=(
            P("frame", "row", None, "head"),
            P("frame", "row", None, "head"),
            P("frame", "row", None, "head"),
        ),
        check_vma=False,
    )
```
